32 devices in a mesh: seq: 16 (over z, x, core), dp: 2 (over y).
Axes of the slice: x: 2, y: 2, z: 4, core: 2. Of those that a mesh axis runs over, the one named last changes fastest.
Arguments:
- activations: bfloat16 [2, 2048, 768], P('dp', 'seq'), may hold values from -6 to 6
- cotangent: bfloat16 [2, 2048, 768], P('dp', 'seq'), may hold values from -6 to 6
- weights: bfloat16 [3840, 768], P(('seq', 'dp')), may hold values from -0.09375 to 0.09375
- norm_gain: float32 [768], replicated, may hold values from 0.25 to 1.75
- pairing: int32 [768], replicated, may hold values from 0 to 767, as said below
Outputs:
- combined: bfloat16 [2, 2048, 768], P('dp', 'seq')
- grad_input: bfloat16 [2, 2048, 768], P('dp', 'seq')
- grad_kernel: float32 [3840, 768], P(('seq', 'dp'))
- grad_gain: float32 [768], P(('seq', 'dp'))
The draws below stay inside these ranges and needn't reach their ends.
Inputs may be any that keep to these rules, and one draw needn't show every extreme that they name: pairing is an involution without fixed points: pairing[pairing[c]] = c != pairing[c].
All inputs are finite; a program needn't handle non-finite values.
Results may differ from the reference program's by a relative error of at most 0.0055.
Values may be sent and summed in bfloat16 or wider, within the bound.
No kernel may reach another device: no remote copies, remote signals or barrier semaphores. Data moves between devices by JAX's collectives and lax.ppermute only.
A program may use at most 192 MiB of HBM per device.

```python
import jax
import jax.numpy as jnp
from jax import lax

CHANNELS = 768
TAPS = 5
LENGTH = 2048
SEQS = 2


def draw_pairing(key, part):
    shuffled = jax.random.permutation(jax.random.fold_in(key, 7), CHANNELS).astype(jnp.int32)
    lead_half = shuffled[0::2]
    tail_half = shuffled[1::2]
    result = jnp.zeros((CHANNELS,), jnp.int32)
    result = result.at[lead_half].set(tail_half).at[tail_half].set(lead_half)
    return result.astype(jnp.int32)


def strengthened(entries, own_key, source, target, shards_of, factor):
    owner, partner = [(jnp.arange(entries.shape[position]) // (entries.shape[position] // shards_of)).reshape([-1 if axis == position else 1 for axis in range(entries.ndim)]) for position in (source, target)]
    chosen = jax.random.permutation(own_key, shards_of)[partner]
    strong = (owner == chosen) | (owner == (partner + shards_of // 2) % shards_of)
    return jnp.where(strong, factor * entries, entries)


def block_levels(own_key, shape, shards, least, top_value):
    level = 1.0
    for dim, shards_of in shards:
        steps = jax.random.uniform(jax.random.fold_in(jax.random.fold_in(own_key, 6), dim), (shards_of,), jnp.float32, least / len(shards), top_value / len(shards))
        level = level * jnp.repeat(jnp.exp(steps), shape[dim] // shards_of).reshape((-1,) + (1,) * (len(shape) - 1 - dim))
    return level


def scatter_about(rng, dims, scale, bound, shards=(), kind=jnp.bfloat16):
    values = scale * jax.random.normal(rng, dims, jnp.float32)
    if shards:
        values = values * block_levels(rng, dims, shards, -0.22, 0.18)
    return jnp.clip(values, -bound, bound).astype(kind)


def heavy_noise(own_key, dims, scale, reach, shards, heavy, kind=jnp.bfloat16):
    values = scale * jax.random.normal(own_key, dims, jnp.float32)
    if shards:
        values = values * block_levels(own_key, dims, shards, -0.22, 0.18)
    return jnp.clip(strengthened(values, jax.random.fold_in(own_key, 3), *heavy), -reach, reach).astype(kind)


def setup_inputs(seed: int = 0) -> dict:
    key_of = jax.random.split(jax.random.key(seed), 6)
    activations = heavy_noise(key_of[0], (SEQS, LENGTH, CHANNELS), 1.0, 6.0, ((0, 2), (1, 16)), (1, 2, 16, 2.0))
    cotangent = scatter_about(key_of[1], (SEQS, LENGTH, CHANNELS), 1.0, 6.0, ((0, 2), (1, 16)))
    weights = scatter_about(key_of[2], (TAPS * CHANNELS, CHANNELS), (TAPS * CHANNELS) ** -0.5, 0.09375, ((0, 32),))
    norm_gain = jnp.clip(1.0 + 0.15 * jax.random.normal(key_of[3], (CHANNELS,), jnp.float32), 0.25, 1.75)
    pairing = draw_pairing(jax.random.fold_in(key_of[5], 71), 0)
    return {"activations": activations, "cotangent": cotangent, "weights": weights, "norm_gain": norm_gain, "pairing": pairing}


epsilon = 1e-06

def strand(values_in, cot_half, kernel, norm_gain):
    values = values_in.astype(jnp.float32)
    inverse_rms = lax.rsqrt(lax.optimization_barrier(jnp.mean(values * values, -1, keepdims=True)) + epsilon)
    normed = (values * inverse_rms * norm_gain).astype(jnp.bfloat16)
    padded = jnp.pad(normed, ((2, 2), (0, 0)))
    windows = jnp.concatenate([padded[offset:offset + LENGTH] for offset in range(TAPS)], -1)
    preact = jnp.dot(windows, kernel, preferred_element_type=jnp.float32)
    result = values + jax.nn.gelu(preact)
    _, pullback = jax.vjp(jax.nn.gelu, preact)
    grad_pre = pullback(cot_half)[0].astype(jnp.bfloat16)
    kernel_term = jnp.dot(windows.T, grad_pre, preferred_element_type=jnp.float32)
    grad_pad = jnp.pad(grad_pre, ((2, 2), (0, 0)))
    back_windows = jnp.concatenate([grad_pad[TAPS - 1 - offset:TAPS - 1 - offset + LENGTH] for offset in range(TAPS)], -1)
    kernel_t = kernel.reshape(TAPS, CHANNELS, CHANNELS).transpose(0, 2, 1).reshape(TAPS * CHANNELS, CHANNELS)
    grad_normed = jnp.dot(back_windows, kernel_t, preferred_element_type=jnp.float32)
    gain_term = lax.optimization_barrier(jnp.sum(grad_normed * values * inverse_rms, 0))
    scaled = grad_normed * norm_gain
    grad_values = cot_half + inverse_rms * scaled - values * inverse_rms ** 3 * lax.optimization_barrier(jnp.mean(scaled * values, -1, keepdims=True))
    return (result, grad_values, kernel_term, gain_term)

def reference(activations, cotangent, weights, norm_gain, pairing):

    def one_sequence(pieces):
        seq_in, seq_cot = pieces
        half_cot = 0.5 * seq_cot.astype(jnp.float32)
        fwd_out, fwd_grad, fwd_kernel, fwd_gain = strand(seq_in, half_cot, weights, norm_gain)
        rev_in = seq_in[::-1][:, pairing]
        rev_cot = half_cot[::-1][:, pairing]
        rev_out, rev_grad, rev_kernel, rev_gain = strand(rev_in, rev_cot, weights, norm_gain)
        out_round = lax.optimization_barrier(rev_out.astype(jnp.bfloat16))[::-1][:, pairing]
        grad_round = lax.optimization_barrier(rev_grad.astype(jnp.bfloat16))[::-1][:, pairing]
        combined = (0.5 * (fwd_out + out_round.astype(jnp.float32))).astype(jnp.bfloat16)
        grad_input = (fwd_grad + grad_round.astype(jnp.float32)).astype(jnp.bfloat16)
        return (combined, grad_input, fwd_kernel + rev_kernel, fwd_gain + rev_gain)
    combined, grad_input, kernels, gains = lax.map(one_sequence, (activations, cotangent))
    return (combined, grad_input, lax.optimization_barrier(jnp.sum(kernels, 0)), lax.optimization_barrier(jnp.sum(gains, 0)))
```

```python
import jax
import jax.numpy as jnp
from jax import lax
from jax.sharding import Mesh, PartitionSpec as P

epsilon = 1e-06


def neighbours(block, axis, width):
    count = lax.axis_size(axis)
    forward = [(i, i + 1) for i in range(count - 1)]
    backward = [(target, source) for source, target in forward]
    low = lax.ppermute(block[-width:], axis, forward)
    high = lax.ppermute(block[:width], axis, backward)
    return low, high


def gelu_and_slope(preact):
    result, pullback = jax.vjp(jax.nn.gelu, preact)
    return result, pullback(jnp.ones_like(preact))[0]


def per_device(activations, cotangent, weights, norm_gain, pairing):
    ranks = lax.axis_size("rank")
    blocks = lax.axis_size("block")
    copies = lax.axis_size("dp")
    positions, channels = activations.shape[1:]
    rows = weights.shape[0]
    taps = rows * ranks * blocks * copies // channels
    part = channels // ranks
    half = taps // 2
    reach = 2 * half
    span = positions * ranks
    mine = lax.all_to_all(weights, "rank", split_axis=1, concat_axis=0, tiled=True)
    packed = mine.reshape(2, ranks * rows // 2, part).transpose(1, 0, 2).reshape(-1, 2 * part)
    gathered = lax.all_gather(packed, ("block", "dp"), axis=0, tiled=True)
    kernel = gathered.reshape(blocks, copies, ranks // 2, rows, 2, part)
    kernel = kernel.transpose(0, 4, 2, 1, 3, 5).reshape(taps, channels, part)
    kernel = kernel.transpose(1, 0, 2).reshape(channels, taps * part)
    swap = (pairing[None, :] == jnp.arange(channels, dtype=pairing.dtype)[:, None]).astype(jnp.bfloat16)
    values = activations[0]
    cot = cotangent[0]
    cot_swapped = jnp.dot(cot, swap)
    whole = jnp.broadcast_to(values, (ranks, positions, channels))
    slices = [t.reshape(positions, ranks, part).transpose(1, 0, 2) for t in (cot, cot_swapped)]
    message = jnp.concatenate([whole] + slices, -1).reshape(span, -1)
    message = lax.all_to_all(message, "rank", split_axis=0, concat_axis=0, tiled=True)
    low, high = neighbours(message, "block", reach)
    extended = jnp.concatenate([low, message, high], 0)
    group = extended[:, :channels]
    group_swapped = jnp.dot(group, swap)
    group = group.astype(jnp.float32)
    inverse_rms = lax.rsqrt(jnp.mean(group * group, -1, keepdims=True) + epsilon)
    normed = jnp.stack(
        [
            (group * inverse_rms * norm_gain).astype(jnp.bfloat16),
            (group_swapped.astype(jnp.float32) * inverse_rms * norm_gain).astype(jnp.bfloat16),
        ]
    )
    halves = 0.5 * extended[half:-half, channels:].astype(jnp.float32)
    terms = jnp.einsum("src,ce->sre", normed, kernel, preferred_element_type=jnp.float32)
    wide = span + reach
    tap_list = range(taps)
    gelus, shifted = [], []
    for strand in range(2):
        starts = [k if strand == 0 else reach - k for k in tap_list]
        preact = sum(
            terms[strand, starts[k] : starts[k] + wide, k * part : (k + 1) * part] for k in tap_list
        )
        result, slope = gelu_and_slope(preact)
        gelus.append(result[half : half + span].astype(jnp.bfloat16))
        grad_pre = (halves[:, strand * part : (strand + 1) * part] * slope).astype(jnp.bfloat16)
        shifted.append(
            jnp.concatenate([grad_pre[reach - s : reach - s + span] for s in starts], -1)
        )
    shifted = jnp.stack(shifted)
    inner = normed[:, reach : reach + span]
    kernel_term = jnp.einsum("src,sre->ce", inner, shifted, preferred_element_type=jnp.float32)
    gain_term = jnp.sum(kernel_term * kernel.astype(jnp.float32), -1) / norm_gain
    kernel_rows = kernel_term.astype(jnp.bfloat16).reshape(channels, taps, part).transpose(1, 0, 2)
    kernel_rows = kernel_rows.reshape(blocks, 2, ranks // 2, copies, rows, part)
    kernel_rows = kernel_rows.transpose(0, 3, 2, 4, 1, 5).reshape(blocks * copies, -1, 2 * part)
    gain_rows = gain_term.reshape(blocks, ranks, copies, -1).transpose(0, 2, 1, 3)
    gain_rows = gain_rows.reshape(blocks * copies, -1)
    gain_high = gain_rows.astype(jnp.bfloat16)
    gain_low = (gain_rows - gain_high.astype(jnp.float32)).astype(jnp.bfloat16)
    extra = jnp.concatenate([gain_high, gain_low], -1)
    gain_count = extra.shape[-1]
    extra_rows = -(-gain_count // (2 * part * 16)) * 16
    extra = jnp.pad(extra, ((0, 0), (0, extra_rows * 2 * part - gain_count)))
    outgoing = jnp.concatenate([kernel_rows, extra.reshape(blocks * copies, extra_rows, 2 * part)], 1)
    summed = lax.psum_scatter(outgoing, ("block", "dp"), scatter_dimension=0, tiled=True)[0]
    summed = summed.astype(jnp.float32)
    kernel_sum = summed[:-extra_rows].reshape(ranks // 2, rows, 2, part).transpose(2, 0, 1, 3)
    kernel_sum = kernel_sum.reshape(ranks, rows, part)
    gain_sum = summed[-extra_rows:].reshape(-1)[:gain_count].reshape(2, ranks, -1).sum(0)
    gain_sum = jnp.pad(gain_sum, ((0, 0), (0, part - gain_sum.shape[1])))
    last = jnp.concatenate([kernel_sum, gain_sum[:, None]], 1)
    last = lax.all_to_all(last, "rank", split_axis=0, concat_axis=0, tiled=True)
    grad_kernel = last[:, :rows].transpose(1, 0, 2).reshape(rows, channels)
    grad_gain = last[:, rows, : channels // (ranks * blocks * copies)].sum(0)
    kernel_swapped = jnp.dot(swap, kernel)
    grad_scaled = (
        jnp.einsum("re,ce->rc", shifted[0], kernel, preferred_element_type=jnp.float32) * norm_gain
        + jnp.einsum("re,ce->rc", shifted[1], kernel_swapped, preferred_element_type=jnp.float32)
        * norm_gain[pairing]
    )
    back = jnp.concatenate([grad_scaled.astype(jnp.bfloat16)] + gelus, -1)
    back = lax.all_to_all(back, "rank", split_axis=0, concat_axis=0, tiled=True)
    back = back.reshape(ranks, positions, -1)
    scaled = back[:, :, :channels].astype(jnp.float32).sum(0)
    gelu_plain = back[:, :, channels : channels + part].transpose(1, 0, 2).reshape(positions, channels)
    gelu_other = back[:, :, channels + part :].transpose(1, 0, 2).reshape(positions, channels)
    gelu_other = jnp.dot(gelu_other, swap).astype(jnp.float32)
    values = values.astype(jnp.float32)
    cot = cot.astype(jnp.float32)
    own_rms = lax.rsqrt(jnp.mean(values * values, -1, keepdims=True) + epsilon)
    reverse_out = (values + gelu_other).astype(jnp.bfloat16).astype(jnp.float32)
    combined = (0.5 * (values + gelu_plain.astype(jnp.float32) + reverse_out)).astype(jnp.bfloat16)
    grad_input = (
        cot + own_rms * scaled - values * own_rms**3 * jnp.mean(scaled * values, -1, keepdims=True)
    ).astype(jnp.bfloat16)
    return combined[None], grad_input[None], grad_kernel, grad_gain


def solution(mesh):
    seq, dp = mesh.shape["seq"], mesh.shape["dp"]
    ranks = 4
    grouped = Mesh(mesh.devices.reshape(seq // ranks, ranks, dp), ("block", "rank", "dp"))
    along = P("dp", ("block", "rank"), None)
    every = ("block", "rank", "dp")
    return jax.shard_map(
        per_device,
        mesh=grouped,
        in_specs=(along, along, P(every, None), P(), P()),
        out_specs=(along, along, P(every, None), P(every)),
        check_vma=False,
    )
```

```python
import jax
import jax.numpy as jnp
from jax import lax
from jax.sharding import Mesh, PartitionSpec as P

epsilon = 1e-06
RANK = ("seq_rank", "dp_rank")
BLOCK = ("seq_block", "dp_block")


def neighbours(block, axis, width, dim):
    count = lax.axis_size(axis)
    forward = [(i, i + 1) for i in range(count - 1)]
    backward = [(target, source) for source, target in forward]
    size = block.shape[dim]
    low = lax.ppermute(lax.slice_in_dim(block, size - width, size, axis=dim), axis, forward)
    high = lax.ppermute(lax.slice_in_dim(block, 0, width, axis=dim), axis, backward)
    return low, high


def gathered_direct(block, axes):
    count = lax.axis_size(axes)
    me = lax.axis_index(axes)
    result = lax.dynamic_update_index_in_dim(
        jnp.zeros((count,) + block.shape, block.dtype), block, me, 0
    )
    for shift in range(1, count):
        other = lax.ppermute(block, axes, [(i, (i + shift) % count) for i in range(count)])
        result = lax.dynamic_update_index_in_dim(result, other, (me + count - shift) % count, 0)
    return result


def gelu_and_slope(preact):
    result, pullback = jax.vjp(jax.nn.gelu, preact)
    return result, pullback(jnp.ones_like(preact))[0]


def per_device(activations, cotangent, weights, norm_gain, pairing):
    seq_ranks = lax.axis_size("seq_rank")
    dp_ranks = lax.axis_size("dp_rank")
    seq_blocks = lax.axis_size("seq_block")
    dp_blocks = lax.axis_size("dp_block")
    ranks = seq_ranks * dp_ranks
    blocks = seq_blocks * dp_blocks
    positions, channels = activations.shape[1:]
    rows = weights.shape[0]
    taps = rows * ranks * blocks // channels
    part = channels // ranks
    half = taps // 2
    reach = 2 * half
    span = positions * seq_ranks
    mine = lax.all_to_all(weights.T.reshape(ranks, part, rows), RANK, 0, 0, tiled=True)
    mine = mine.transpose(1, 0, 2).reshape(part, ranks * rows)
    kernel = gathered_direct(mine, BLOCK)
    kernel = kernel.reshape(seq_blocks, dp_blocks, part, seq_ranks, dp_ranks, rows)
    kernel = kernel.transpose(2, 0, 3, 1, 4, 5).reshape(part, taps, channels)
    kernel = kernel.transpose(1, 0, 2).reshape(taps * part, channels)
    swap = (pairing[None, :] == jnp.arange(channels, dtype=pairing.dtype)[:, None]).astype(jnp.bfloat16)
    values = activations[0]
    cot = cotangent[0]
    cot_swapped = jnp.dot(cot, swap)
    whole = jnp.broadcast_to(values, (ranks, positions, channels))
    slices = [t.reshape(positions, ranks, part).transpose(1, 0, 2) for t in (cot, cot_swapped)]
    message = jnp.concatenate([whole] + slices, -1)
    message = lax.all_to_all(message, RANK, 0, 0, tiled=True)
    message = message.reshape(seq_ranks, dp_ranks, positions, -1).transpose(1, 0, 2, 3)
    message = message.reshape(dp_ranks, span, -1)
    low, high = neighbours(message, "seq_block", reach, 1)
    extended = jnp.concatenate([low, message, high], 1)
    group = extended[:, :, :channels]
    group_swapped = jnp.dot(group, swap)
    group = group.astype(jnp.float32)
    inverse_rms = lax.rsqrt(jnp.mean(group * group, -1, keepdims=True) + epsilon)
    normed = [
        (t.astype(jnp.float32) * inverse_rms * norm_gain).astype(jnp.bfloat16)
        for t in (group, group_swapped)
    ]
    halves = 0.5 * extended[:, half:-half, channels:].astype(jnp.float32)
    wide = span + reach
    gelus, shifted = [], []
    for strand in range(2):
        terms = jnp.einsum("brc,ec->bre", normed[strand], kernel, preferred_element_type=jnp.float32)
        starts = [k if strand == 0 else reach - k for k in range(taps)]
        preact = sum(
            terms[:, starts[k] : starts[k] + wide, k * part : (k + 1) * part] for k in range(taps)
        )
        result, slope = gelu_and_slope(preact)
        gelus.append(result[:, half : half + span].astype(jnp.bfloat16))
        grad_pre = (halves[:, :, strand * part : (strand + 1) * part] * slope).astype(jnp.bfloat16)
        shifted.append(
            jnp.concatenate([grad_pre[:, reach - s : reach - s + span] for s in starts], -1)
        )
    kernel_term = jnp.einsum(
        "sbre,sbrc->ec",
        jnp.stack(shifted),
        jnp.stack([n[:, reach : reach + span] for n in normed]),
        preferred_element_type=jnp.float32,
    )
    gain_term = jnp.sum(kernel_term * kernel.astype(jnp.float32), 0) / norm_gain
    outgoing = kernel_term.astype(jnp.bfloat16).reshape(taps, part, channels).transpose(1, 0, 2)
    outgoing = outgoing.reshape(part, seq_blocks, seq_ranks, dp_blocks, dp_ranks, rows)
    outgoing = outgoing.transpose(1, 3, 0, 2, 4, 5).reshape(blocks, part, ranks * rows)
    own_gain = channels // (ranks * blocks)
    gain_rows = gain_term.reshape(seq_blocks, seq_ranks, dp_blocks, dp_ranks, own_gain)
    gain_rows = gain_rows.transpose(0, 2, 1, 3, 4).reshape(blocks, 1, ranks, own_gain)
    gain_rows = jnp.pad(gain_rows, ((0, 0), (0, 0), (0, 0), (0, rows - own_gain)))
    gain_rows = gain_rows.reshape(blocks, 1, ranks * rows)
    gain_high = gain_rows.astype(jnp.bfloat16)
    gain_low = (gain_rows - gain_high.astype(jnp.float32)).astype(jnp.bfloat16)
    extra = jnp.pad(jnp.concatenate([gain_high, gain_low], 1), ((0, 0), (0, 14), (0, 0)))
    outgoing = jnp.concatenate([outgoing, extra], 1)
    terms = lax.all_to_all(outgoing, BLOCK, 0, 0, tiled=True)
    summed = terms.astype(jnp.float32).sum(0)
    gain_sum = summed[part : part + 1] + summed[part + 1 : part + 2]
    last = jnp.concatenate([summed[:part], jnp.pad(gain_sum, ((0, 7), (0, 0)))], 0)
    last = last.reshape(-1, ranks, rows).transpose(1, 0, 2)
    last = lax.all_to_all(last, RANK, 0, 0, tiled=True)
    grad_kernel = last[:, :part].reshape(channels, rows).T
    grad_gain = last[:, part, :own_gain].sum(0)
    kernel_swapped = jnp.dot(kernel, swap)
    grad_scaled = (
        jnp.einsum("bre,ec->brc", shifted[0], kernel, preferred_element_type=jnp.float32) * norm_gain
        + jnp.einsum("bre,ec->brc", shifted[1], kernel_swapped, preferred_element_type=jnp.float32)
        * norm_gain[pairing]
    )
    back = jnp.concatenate([grad_scaled.astype(jnp.bfloat16)] + gelus, -1)
    back = back.reshape(dp_ranks, seq_ranks, positions, -1).transpose(1, 0, 2, 3)
    back = back.reshape(ranks, positions, -1)
    back = lax.all_to_all(back, RANK, 0, 0, tiled=True)
    scaled = back[:, :, :channels].astype(jnp.float32).sum(0)
    gelu_plain = back[:, :, channels : channels + part].transpose(1, 0, 2).reshape(positions, channels)
    gelu_other = back[:, :, channels + part :].transpose(1, 0, 2).reshape(positions, channels)
    gelu_other = jnp.dot(gelu_other, swap).astype(jnp.float32)
    values = values.astype(jnp.float32)
    cot = cot.astype(jnp.float32)
    own_rms = lax.rsqrt(jnp.mean(values * values, -1, keepdims=True) + epsilon)
    reverse_out = (values + gelu_other).astype(jnp.bfloat16).astype(jnp.float32)
    combined = (0.5 * (values + gelu_plain.astype(jnp.float32) + reverse_out)).astype(jnp.bfloat16)
    grad_input = (
        cot + own_rms * scaled - values * own_rms**3 * jnp.mean(scaled * values, -1, keepdims=True)
    ).astype(jnp.bfloat16)
    return combined[None], grad_input[None], grad_kernel, grad_gain


def solution(mesh):
    seq, dp = mesh.shape["seq"], mesh.shape["dp"]
    seq_ranks, dp_ranks = 4, 2
    grouped = Mesh(
        mesh.devices.reshape(seq // seq_ranks, seq_ranks, dp // dp_ranks, dp_ranks),
        ("seq_block", "seq_rank", "dp_block", "dp_rank"),
    )
    along = P(("dp_block", "dp_rank"), ("seq_block", "seq_rank"), None)
    every = ("seq_block", "seq_rank", "dp_block", "dp_rank")
    return jax.shard_map(
        per_device,
        mesh=grouped,
        in_specs=(along, along, P(every, None), P(), P()),
        out_specs=(along, along, P(every, None), P(every)),
        check_vma=False,
    )
```

```python
import jax
import jax.numpy as jnp
from jax import lax
from jax.experimental import pallas as pl
from jax.experimental.pallas import tpu as pltpu
from jax.sharding import Mesh, PartitionSpec as P

epsilon = 1e-06
RANK = ("seq_rank", "dp_rank")
BLOCK = ("seq_block", "dp_block")
EVERY = ("seq_block", "seq_rank", "dp_block", "dp_rank")
LANES = 128
HALO = 16
EXTRA = 16
VMEM = pl.BlockSpec(memory_space=pltpu.VMEM)
SMEM = pl.BlockSpec(memory_space=pltpu.SMEM)
bf16 = jnp.bfloat16
f32 = jnp.float32


def called(body, outs, args, scratch=(), specs=None, flops=0, moved=0):
    return pl.pallas_call(
        body,
        out_shape=outs,
        in_specs=specs or [VMEM] * len(args),
        out_specs=jax.tree.map(lambda _: VMEM, outs),
        scratch_shapes=list(scratch),
        compiler_params=pltpu.CompilerParams(vmem_limit_bytes=50 * 2**20),
        cost_estimate=pl.CostEstimate(flops=flops, bytes_accessed=moved, transcendentals=0),
    )(*args)


def shape_of(shape, dtype):
    return jax.ShapeDtypeStruct(shape, dtype)


def dot(a, b, contract):
    return lax.dot_general(a, b, (contract, ((), ())), preferred_element_type=f32)


def gelu_and_slope(x):
    inner = 0.7978845608028654 * (x + 0.044715 * (x * x * x))
    bend = jnp.tanh(inner)
    half_sum = 0.5 * (1.0 + bend)
    slope = half_sum + (0.5 * x) * (1.0 - bend * bend) * (
        0.7978845608028654 * (1.0 + 0.134145 * (x * x))
    )
    return x * half_sum, slope


def pack_message(values_ref, cot_ref, plain_ref, other_ref, message_ref):
    ranks = message_ref.shape[0]
    channels = values_ref.shape[1]
    cot = cot_ref[...]
    pieces = [dot(cot, ref[...], ((1,), (0,))).astype(bf16) for ref in (plain_ref, other_ref)]
    for j in range(ranks):
        message_ref[j, :, :channels] = values_ref[...]
        for n, piece in enumerate(pieces):
            start = channels + n * LANES
            message_ref[j, :, start : start + LANES] = piece[:, j * LANES : (j + 1) * LANES]


def prepare(message_ref, low_ref, high_ref, gain_ref, swap_ref, normed_ref, grads_ref):
    dp_ranks = low_ref.shape[0]
    ranks, positions = message_ref.shape[:2]
    channels = gain_ref.shape[1]

    def put(block, b, start):
        count = block.shape[0]
        x = block[:, :channels]
        other = dot(x, swap_ref[...], ((1,), (0,)))
        x = x.astype(f32)
        rms = lax.rsqrt(jnp.mean(x * x, -1, keepdims=True) + epsilon)
        normed_ref[b, pl.ds(start, count), :] = (x * rms * gain_ref[...]).astype(bf16)
        normed_ref[dp_ranks + b, pl.ds(start, count), :] = (other * rms * gain_ref[...]).astype(bf16)
        for n in range(2):
            lane = channels + n * LANES
            grads_ref[n * dp_ranks + b, pl.ds(start, count), :] = 0.5 * block[:, lane : lane + LANES].astype(f32)

    for b in range(dp_ranks):
        put(low_ref[b], b, 0)
        for i in range(ranks // dp_ranks):
            put(message_ref[i * dp_ranks + b], b, HALO + i * positions)
        put(high_ref[b], b, HALO + (ranks // dp_ranks) * positions)


def main_body(sizes, me_ref, own_ref, *refs):
    seq_blocks, dp_blocks, seq_ranks, dp_ranks = sizes
    blocks = seq_blocks * dp_blocks
    others = refs[: blocks - 1]
    normed_ref, grads_ref, gain_ref = refs[blocks - 1 : blocks + 2]
    shifted_ref, kernel_ref, gelu_ref, out_ref = refs[blocks + 2 : blocks + 6]
    pieces, terms, bent, slopes, total = refs[blocks + 6 :]
    part, rows = own_ref.shape[1:]
    strands, long, channels = normed_ref.shape
    taps = kernel_ref.shape[0] // LANES
    half = taps // 2
    reach = 2 * half
    span = long - 2 * HALO
    wide = bent.shape[0]
    me = me_ref[0]
    pieces[me] = own_ref[...]
    for shift in range(1, blocks):
        pieces[lax.rem(me + blocks - shift, blocks)] = others[shift - 1][...]
    kernel_ref[...] = jnp.zeros_like(kernel_ref)
    owners = [
        (sb * dp_blocks + db, sr * dp_ranks + dr)
        for sb in range(seq_blocks)
        for sr in range(seq_ranks)
        for db in range(dp_blocks)
        for dr in range(dp_ranks)
    ]

    def runs(owner):
        first, last = owner * rows, (owner + 1) * rows
        while first < last:
            tap, channel = divmod(first, channels)
            count = min(last - first, channels - channel)
            yield tap, channel, count, first - owner * rows
            first += count

    for owner, (block, rank) in enumerate(owners):
        for tap, channel, count, offset in runs(owner):
            kernel_ref[tap * LANES : tap * LANES + part, channel : channel + count] = pieces[
                block, rank, :, offset : offset + count
            ]
    for strand in range(strands):
        terms[...] = dot(normed_ref[strand], kernel_ref[...], ((1,), (1,)))
        forward = strand < dp_ranks
        preact = jnp.zeros((wide, LANES), f32)
        for k in range(taps):
            start = HALO - reach + k if forward else HALO - k
            preact += terms[start : start + wide, k * LANES : (k + 1) * LANES]
        result, slope = gelu_and_slope(preact)
        bent[...] = result
        gelu_ref[strand] = bent[half : half + span, :].astype(bf16)
        slopes[...] = grads_ref[strand, HALO - half : HALO - half + wide, :] * slope
        edge = jnp.zeros((HALO, taps * LANES), bf16)
        shifted_ref[strand, :HALO, :] = edge
        shifted_ref[strand, HALO + span :, :] = edge
        for k in range(taps):
            start = reach - k if forward else k
            shifted_ref[strand, HALO : HALO + span, k * LANES : (k + 1) * LANES] = slopes[
                start : start + span, :
            ].astype(bf16)
    total[...] = dot(
        shifted_ref[...].reshape(strands * long, taps * LANES),
        normed_ref[...].reshape(strands * long, channels),
        ((0,), (0,)),
    )
    gain = jnp.sum(total[...] * kernel_ref[...].astype(f32), 0, keepdims=True) / gain_ref[...]
    gain_high = gain.astype(bf16).astype(f32)
    row = lax.broadcasted_iota(jnp.int32, (EXTRA, channels), 0)
    extra = jnp.where(row == 0, gain_high, jnp.where(row == 1, gain - gain_high, 0.0))
    own_gain = channels // len(owners)
    for owner in range(len(owners)):
        for tap, channel, count, offset in runs(owner):
            out_ref[owner, :part, offset : offset + count] = total[
                tap * LANES : tap * LANES + part, channel : channel + count
            ].astype(bf16)
        out_ref[owner, part:, :] = jnp.zeros((EXTRA, rows), bf16)
        out_ref[owner, part:, :own_gain] = extra[
            :, owner * own_gain : (owner + 1) * own_gain
        ].astype(bf16)


def input_gradient(rank_ref, shifted_ref, kernel_ref, swap_ref, gain_ref, swapped_gain_ref, gelu_ref, *refs):
    outs, scaled = refs[:-1], refs[-1]
    ranks = len(outs)
    strands, long, _ = shifted_ref.shape
    dp_ranks = strands // 2
    span = long - 2 * HALO
    positions = outs[0].shape[0]
    channels = gain_ref.shape[1]
    kernel = kernel_ref[...]
    swapped = dot(kernel, swap_ref[...], ((1,), (0,))).astype(bf16)
    for b in range(dp_ranks):
        scaled[b] = (
            dot(shifted_ref[b, HALO : HALO + span, :], kernel, ((1,), (0,))) * gain_ref[...]
            + dot(shifted_ref[dp_ranks + b, HALO : HALO + span, :], swapped, ((1,), (0,)))
            * swapped_gain_ref[...]
        ).astype(bf16)
    for shift in range(ranks):
        target = lax.bitwise_xor(rank_ref[0], shift)
        b = lax.rem(target, dp_ranks)
        start = pl.multiple_of(lax.div(target, dp_ranks) * positions, positions)
        outs[shift][:, :channels] = scaled[b, pl.ds(start, positions), :]
        for n in range(2):
            lane = channels + n * LANES
            outs[shift][:, lane : lane + LANES] = gelu_ref[n * dp_ranks + b, pl.ds(start, positions), :]


def finish(rank_ref, values_ref, cot_ref, plain_ref, other_ref, *refs):
    blocks, (combined_ref, grad_ref, gelus) = refs[:-3], refs[-3:]
    channels = values_ref.shape[1]
    scaled = jnp.zeros(values_ref.shape, f32)
    for shift, block in enumerate(blocks):
        source = lax.bitwise_xor(rank_ref[0], shift)
        scaled += block[:, :channels].astype(f32)
        for n in range(2):
            lane = channels + n * LANES
            gelus[n, source] = block[:, lane : lane + LANES]
    plain = jnp.zeros(values_ref.shape, f32)
    other = jnp.zeros(values_ref.shape, f32)
    joined = [jnp.concatenate([gelus[n, j] for j in range(len(blocks))], -1) for n in range(2)]
    plain = dot(joined[0], plain_ref[...], ((1,), (1,)))
    other = dot(joined[1], other_ref[...], ((1,), (1,)))
    values = values_ref[...].astype(f32)
    rms = lax.rsqrt(jnp.mean(values * values, -1, keepdims=True) + epsilon)
    reverse_out = (values + other).astype(bf16).astype(f32)
    combined_ref[...] = (0.5 * (values + plain + reverse_out)).astype(bf16)
    along = jnp.mean(scaled * values, -1, keepdims=True)
    grad_ref[...] = (cot_ref[...].astype(f32) + rms * scaled - values * (rms * rms * rms * along)).astype(bf16)


def shifted_pairs(count, shift):
    return [(i, (i + shift) % count) for i in range(count)]


def flipped_pairs(count, mask):
    return [(i, i ^ mask) for i in range(count)]


def per_device(activations, cotangent, weights, norm_gain, pairing):
    seq_ranks = lax.axis_size("seq_rank")
    dp_ranks = lax.axis_size("dp_rank")
    seq_blocks = lax.axis_size("seq_block")
    dp_blocks = lax.axis_size("dp_block")
    ranks = seq_ranks * dp_ranks
    blocks = seq_blocks * dp_blocks
    owners = ranks * blocks
    positions, channels = activations.shape[1:]
    rows = weights.shape[0]
    taps = rows * owners // channels
    part = channels // ranks
    span = positions * seq_ranks
    long = span + 2 * HALO
    reach = taps - taps % 2
    wide = -(-(span + reach) // 8) * 8
    strands = 2 * dp_ranks
    width = channels + 2 * LANES
    me = lax.axis_index(BLOCK).reshape(1)
    rank = lax.axis_index(RANK).reshape(1)
    values, cot = activations[0], cotangent[0]
    mine = lax.all_to_all(weights.T.reshape(ranks, part, rows), RANK, 0, 0, tiled=True)
    other_kernels = [
        lax.ppermute(mine, BLOCK, shifted_pairs(blocks, shift)) for shift in range(1, blocks)
    ]
    slot = jnp.arange(ranks * LANES)
    inside = slot % LANES < part
    channel_of = jnp.where(inside, slot // LANES * part + slot % LANES, 0).astype(jnp.int32)
    channel_list = jnp.arange(channels, dtype=jnp.int32)[:, None]
    plain_map = ((channel_list == channel_of) & inside).astype(bf16)
    other_map = ((channel_list == pairing[channel_of]) & inside).astype(bf16)
    swap = (channel_list == pairing).astype(bf16)
    gain = norm_gain.reshape(1, channels)
    swapped_gain = norm_gain[pairing].reshape(1, channels)
    message = called(
        pack_message,
        shape_of((ranks, positions, width), bf16),
        (values, cot, plain_map, other_map),
    )
    message = lax.all_to_all(message, RANK, 0, 0, tiled=True)
    by_seq = message.reshape(seq_ranks, dp_ranks, positions, width)
    forward = [(i, i + 1) for i in range(seq_blocks - 1)]
    backward = [(target, source) for source, target in forward]
    low = lax.ppermute(by_seq[-1, :, -HALO:], "seq_block", forward)
    high = lax.ppermute(by_seq[0, :, :HALO], "seq_block", backward)
    normed, grads = called(
        prepare,
        (shape_of((strands, long, channels), bf16), shape_of((strands, long, LANES), f32)),
        (message, low, high, gain, swap),
    )
    main_args = (me, mine, *other_kernels, normed, grads, gain)
    sizes = (seq_blocks, dp_blocks, seq_ranks, dp_ranks)
    shifted, kernel, gelus, outgoing = called(
        lambda *refs: main_body(sizes, *refs),
        (
            shape_of((strands, long, taps * LANES), bf16),
            shape_of((taps * LANES, channels), bf16),
            shape_of((strands, span, LANES), bf16),
            shape_of((owners, part + EXTRA, rows), bf16),
        ),
        main_args,
        scratch=[
            pltpu.VMEM((blocks, ranks, part, rows), bf16),
            pltpu.VMEM((long, taps * LANES), f32),
            pltpu.VMEM((wide, LANES), f32),
            pltpu.VMEM((wide, LANES), f32),
            pltpu.VMEM((taps * LANES, channels), f32),
        ],
        specs=[SMEM] + [VMEM] * (len(main_args) - 1),
        flops=4 * strands * long * taps * LANES * channels,
    )
    terms = lax.all_to_all(outgoing, EVERY, 0, 0, tiled=True)
    back = called(
        input_gradient,
        tuple(shape_of((positions, width), bf16) for _ in range(ranks)),
        (rank, shifted, kernel, swap, gain, swapped_gain, gelus),
        scratch=[pltpu.VMEM((dp_ranks, span, channels), bf16)],
        specs=[SMEM] + [VMEM] * 6,
        flops=2 * strands * span * taps * LANES * channels,
    )
    returned = [back[0]] + [
        lax.ppermute(back[mask], RANK, flipped_pairs(ranks, mask)) for mask in range(1, ranks)
    ]
    combined, grad_input = called(
        finish,
        (shape_of((positions, channels), bf16), shape_of((positions, channels), bf16)),
        (rank, values, cot, plain_map, other_map, *returned),
        scratch=[pltpu.VMEM((2, ranks, positions, LANES), bf16)],
        specs=[SMEM] + [VMEM] * (4 + ranks),
    )
    summed = terms.reshape(seq_blocks, seq_ranks, dp_blocks, dp_ranks, -1, rows).astype(f32).sum((0, 2))
    summed = summed.reshape(ranks, -1, rows)
    grad_kernel = summed[:, :part].reshape(channels, rows).T
    grad_gain = summed[:, part : part + 2, : channels // owners].sum((0, 1))
    return combined[None], grad_input[None], grad_kernel, grad_gain


def solution(mesh):
    seq, dp = mesh.shape["seq"], mesh.shape["dp"]
    seq_ranks, dp_ranks = 4, 2
    grouped = Mesh(mesh.devices.reshape(seq // seq_ranks, seq_ranks, dp // dp_ranks, dp_ranks), EVERY)
    along = P(("dp_block", "dp_rank"), ("seq_block", "seq_rank"), None)
    return jax.shard_map(
        per_device,
        mesh=grouped,
        in_specs=(along, along, P(EVERY, None), P(), P()),
        out_specs=(along, along, P(EVERY, None), P(EVERY)),
        check_vma=False,
    )
```

```python
import jax
import jax.numpy as jnp
from jax import lax
from jax.experimental import pallas as pl
from jax.experimental.pallas import tpu as pltpu
from jax.sharding import Mesh, PartitionSpec as P

epsilon = 1e-06
RANK = ("seq_rank", "dp_rank")
BLOCK = ("seq_block", "dp_block")
EVERY = ("seq_block", "seq_rank", "dp_block", "dp_rank")
LANES = 128
HALO = 16
EXTRA = 16
VMEM = pl.BlockSpec(memory_space=pltpu.VMEM)
SMEM = pl.BlockSpec(memory_space=pltpu.SMEM)
bf16 = jnp.bfloat16
f32 = jnp.float32


def called(body, outs, args, vmem, scratch=(), specs=None, flops=0, moved=0):
    return pl.pallas_call(
        body,
        out_shape=outs,
        in_specs=specs or [VMEM] * len(args),
        out_specs=jax.tree.map(lambda _: VMEM, outs),
        scratch_shapes=list(scratch),
        compiler_params=pltpu.CompilerParams(vmem_limit_bytes=vmem * 2**20),
        cost_estimate=pl.CostEstimate(flops=flops, bytes_accessed=moved, transcendentals=0),
    )(*args)


def shape_of(shape, dtype):
    return jax.ShapeDtypeStruct(shape, dtype)


def dot(a, b, contract):
    return lax.dot_general(a, b, (contract, ((), ())), preferred_element_type=f32)


def gelu_and_slope(x):
    inner = 0.7978845608028654 * (x + 0.044715 * (x * x * x))
    bend = jnp.tanh(inner)
    half_sum = 0.5 * (1.0 + bend)
    slope = half_sum + (0.5 * x) * (1.0 - bend * bend) * (
        0.7978845608028654 * (1.0 + 0.134145 * (x * x))
    )
    return x * half_sum, slope


def pack_message(values_ref, cot_ref, plain_ref, other_ref, message_ref):
    ranks = message_ref.shape[0]
    channels = values_ref.shape[1]
    cot = cot_ref[...]
    pieces = [dot(cot, ref[...], ((1,), (0,))).astype(bf16) for ref in (plain_ref, other_ref)]
    for j in range(ranks):
        message_ref[j, :, :channels] = values_ref[...]
        for n, piece in enumerate(pieces):
            start = channels + n * LANES
            message_ref[j, :, start : start + LANES] = piece[:, j * LANES : (j + 1) * LANES]


def normalize(x, gain, swap):
    other = dot(x, swap, ((1,), (0,)))
    x = x.astype(f32)
    rms = lax.rsqrt(jnp.mean(x * x, -1, keepdims=True) + epsilon)
    return [(t * rms * gain).astype(bf16) for t in (x, other)]


def prepare(message_ref, gain_ref, swap_ref, normed_ref, grads_ref, swapped_gain_ref):
    ranks, positions = message_ref.shape[:2]
    dp_ranks = normed_ref.shape[0] // 2
    channels = gain_ref.shape[1]
    for rank in range(ranks):
        b, start = rank % dp_ranks, rank // dp_ranks * positions
        for n, normed in enumerate(normalize(message_ref[rank, :, :channels], gain_ref[...], swap_ref[...])):
            normed_ref[n * dp_ranks + b, start : start + positions, :] = normed
            lane = channels + n * LANES
            grads_ref[n * dp_ranks + b, start : start + positions, :] = (
                0.5 * message_ref[rank, :, lane : lane + LANES].astype(f32)
            ).astype(bf16)
    gain = gain_ref[...]
    first = gain.astype(bf16).astype(f32)
    second = (gain - first).astype(bf16).astype(f32)
    third = gain - first - second
    row = lax.broadcasted_iota(jnp.int32, (HALO, channels), 0)
    parts = jnp.where(row == 0, first, jnp.where(row == 1, second, jnp.where(row == 2, third, 0.0)))
    swapped = dot(parts.astype(bf16), swap_ref[...], ((1,), (0,)))
    swapped_gain_ref[...] = swapped[0:1] + swapped[1:2] + swapped[2:3]


def main_body(sizes, me_ref, own_ref, *refs):
    seq_blocks, dp_blocks, seq_ranks, dp_ranks = sizes
    blocks = seq_blocks * dp_blocks
    others = refs[: blocks - 1]
    normed_ref, grads_ref, low_ref, high_ref, gain_ref, swap_ref = refs[blocks - 1 : blocks + 5]
    shifted_ref, kernel_ref, gelu_ref, out_ref = refs[blocks + 5 : blocks + 9]
    pieces, terms, halves, bent, slopes, total = refs[blocks + 9 :]
    part, rows = own_ref.shape[1:]
    strands, span, channels = normed_ref.shape
    taps = kernel_ref.shape[0] // LANES
    half = taps // 2
    reach = 2 * half
    wide = bent.shape[0]
    me = me_ref[0]
    pieces[me] = own_ref[...]
    for shift in range(1, blocks):
        pieces[lax.rem(me + blocks - shift, blocks)] = others[shift - 1][...]
    kernel_ref[...] = jnp.zeros_like(kernel_ref)
    owners = [
        (sb * dp_blocks + db, sr * dp_ranks + dr)
        for sb in range(seq_blocks)
        for sr in range(seq_ranks)
        for db in range(dp_blocks)
        for dr in range(dp_ranks)
    ]

    def runs(owner):
        first, last = owner * rows, (owner + 1) * rows
        while first < last:
            tap, channel = divmod(first, channels)
            count = min(last - first, channels - channel)
            yield tap, channel, count, first - owner * rows
            first += count

    for owner, (block, rank) in enumerate(owners):
        for tap, channel, count, offset in runs(owner):
            kernel_ref[tap * LANES : tap * LANES + part, channel : channel + count] = pieces[
                block, rank, :, offset : offset + count
            ]
    edges = [ref[b] for ref in (low_ref, high_ref) for b in range(dp_ranks)]
    edges = jnp.concatenate(edges, 0)
    edge_normed = jnp.concatenate(normalize(edges[:, :channels], gain_ref[...], swap_ref[...]), 0)
    edge_terms = dot(edge_normed, kernel_ref[...], ((1,), (1,)))
    for strand in range(strands):
        forward = strand < dp_ranks
        n, b = divmod(strand, dp_ranks)
        terms[HALO : HALO + span, :] = dot(normed_ref[strand], kernel_ref[...], ((1,), (1,)))
        halves[HALO : HALO + span, :] = grads_ref[strand].astype(f32)
        for side, start in enumerate((0, HALO + span)):
            edge = (side * dp_ranks + b) * HALO
            first = n * 2 * dp_ranks * HALO + edge
            terms[start : start + HALO, :] = edge_terms[first : first + HALO]
            lane = channels + n * LANES
            halves[start : start + HALO, :] = 0.5 * edges[
                edge : edge + HALO, lane : lane + LANES
            ].astype(f32)
        preact = jnp.zeros((wide, LANES), f32)
        for k in range(taps):
            start = HALO - reach + k if forward else HALO - k
            preact += terms[start : start + wide, k * LANES : (k + 1) * LANES]
        result, slope = gelu_and_slope(preact)
        bent[...] = result
        gelu_ref[strand] = bent[half : half + span, :].astype(bf16)
        slopes[...] = halves[HALO - half : HALO - half + wide, :] * slope
        for k in range(taps):
            start = reach - k if forward else k
            shifted_ref[strand, :, k * LANES : (k + 1) * LANES] = slopes[
                start : start + span, :
            ].astype(bf16)
    total[...] = dot(
        shifted_ref[...].reshape(strands * span, taps * LANES),
        normed_ref[...].reshape(strands * span, channels),
        ((0,), (0,)),
    )
    gain = jnp.sum(total[...] * kernel_ref[...].astype(f32), 0, keepdims=True) / gain_ref[...]
    gain_high = gain.astype(bf16).astype(f32)
    row = lax.broadcasted_iota(jnp.int32, (EXTRA, channels), 0)
    extra = jnp.where(row == 0, gain_high, jnp.where(row == 1, gain - gain_high, 0.0))
    own_gain = channels // len(owners)
    for owner in range(len(owners)):
        for tap, channel, count, offset in runs(owner):
            out_ref[owner, :part, offset : offset + count] = total[
                tap * LANES : tap * LANES + part, channel : channel + count
            ].astype(bf16)
        out_ref[owner, part:, :] = jnp.zeros((EXTRA, rows), bf16)
        out_ref[owner, part:, :own_gain] = extra[
            :, owner * own_gain : (owner + 1) * own_gain
        ].astype(bf16)


def chip_masks(ranks, core):
    return [mask for mask in range(ranks) if not mask & core]


def input_gradient(
    rank_ref, shifted_ref, kernel_ref, swap_ref, gain_ref, swapped_gain_ref, gelu_ref, own_ref, cross_ref, scaled
):
    strands = shifted_ref.shape[0]
    dp_ranks = strands // 2
    chips, positions, _ = own_ref.shape
    channels = gain_ref.shape[1]
    kernel = kernel_ref[...]
    swapped = dot(kernel, swap_ref[...], ((1,), (0,))).astype(bf16)
    for b in range(dp_ranks):
        scaled[b] = (
            dot(shifted_ref[b], kernel, ((1,), (0,))) * gain_ref[...]
            + dot(shifted_ref[dp_ranks + b], swapped, ((1,), (0,))) * swapped_gain_ref[...]
        ).astype(bf16)
    for m, mask in enumerate(chip_masks(2 * chips, dp_ranks)):
        for out, flip in ((own_ref, mask), (cross_ref, mask | dp_ranks)):
            target = lax.bitwise_xor(rank_ref[0], flip)
            b = lax.rem(target, dp_ranks)
            start = pl.multiple_of(lax.div(target, dp_ranks) * positions, positions)
            out[m, :, :channels] = scaled[b, pl.ds(start, positions), :]
            for n in range(2):
                lane = channels + n * LANES
                out[m, :, lane : lane + LANES] = gelu_ref[n * dp_ranks + b, pl.ds(start, positions), :]


def chip_sum(part, own_ref, crossed_ref, *outs):
    channels = own_ref.shape[2] - 2 * LANES
    for m, out in enumerate(outs):
        out[:, :channels] = (
            own_ref[m, :, :channels].astype(f32) + crossed_ref[m, :, :channels].astype(f32)
        ).astype(bf16)
        for c, ref in enumerate((own_ref, crossed_ref)):
            for n in range(2):
                lane = channels + n * LANES
                start = channels + (2 * c + n) * part
                out[:, start : start + part] = ref[m, :, lane : lane + part]


def finish(part, core, rank_ref, values_ref, cot_ref, plain_ref, other_ref, *refs):
    arrived, (combined_ref, grad_ref, gelus) = refs[:-3], refs[-3:]
    channels = values_ref.shape[1]
    ranks = gelus.shape[1]
    gelus[...] = jnp.zeros_like(gelus)
    scaled = jnp.zeros(values_ref.shape, f32)
    for mask, block in zip(chip_masks(ranks, core), arrived):
        scaled += block[:, :channels].astype(f32)
        for c in range(2):
            source = lax.bitwise_xor(rank_ref[0], mask | c * core)
            for n in range(2):
                start = channels + (2 * c + n) * part
                gelus[n, source, :, :part] = block[:, start : start + part]
    joined = [jnp.concatenate([gelus[n, j] for j in range(ranks)], -1) for n in range(2)]
    plain = dot(joined[0], plain_ref[...], ((1,), (1,)))
    other = dot(joined[1], other_ref[...], ((1,), (1,)))
    values = values_ref[...].astype(f32)
    rms = lax.rsqrt(jnp.mean(values * values, -1, keepdims=True) + epsilon)
    reverse_out = (values + other).astype(bf16).astype(f32)
    combined_ref[...] = (0.5 * (values + plain + reverse_out)).astype(bf16)
    along = jnp.mean(scaled * values, -1, keepdims=True)
    grad_ref[...] = (cot_ref[...].astype(f32) + rms * scaled - values * (rms * rms * rms * along)).astype(bf16)


def shifted_pairs(count, shift):
    return [(i, (i + shift) % count) for i in range(count)]


def flipped_pairs(count, mask):
    return [(i, i ^ mask) for i in range(count)]


def per_device(activations, cotangent, weights, norm_gain, pairing):
    seq_ranks = lax.axis_size("seq_rank")
    dp_ranks = lax.axis_size("dp_rank")
    seq_blocks = lax.axis_size("seq_block")
    dp_blocks = lax.axis_size("dp_block")
    ranks = seq_ranks * dp_ranks
    blocks = seq_blocks * dp_blocks
    owners = ranks * blocks
    positions, channels = activations.shape[1:]
    rows = weights.shape[0]
    taps = rows * owners // channels
    part = channels // ranks
    span = positions * seq_ranks
    long = span + 2 * HALO
    reach = taps - taps % 2
    wide = -(-(span + reach) // 8) * 8
    strands = 2 * dp_ranks
    width = channels + 2 * LANES
    me = lax.axis_index(BLOCK).reshape(1)
    rank = lax.axis_index(RANK).reshape(1)
    values, cot = activations[0], cotangent[0]
    mine = lax.all_to_all(weights.T.reshape(ranks, part, rows), RANK, 0, 0, tiled=True)
    other_kernels = [
        lax.ppermute(mine, BLOCK, shifted_pairs(blocks, shift)) for shift in range(1, blocks)
    ]
    slot = jnp.arange(ranks * LANES, dtype=jnp.int32)
    channel_of = jnp.where(slot % LANES < part, slot // LANES * part + slot % LANES, -1)
    channel_list = jnp.arange(channels, dtype=jnp.int32)
    plain_map = (channel_list[:, None] == channel_of).astype(bf16)
    other_map = (pairing[:, None] == channel_of).astype(bf16)
    swap = (pairing[:, None] == channel_list).astype(bf16)
    gain = norm_gain.reshape(1, channels)
    message = called(
        pack_message,
        shape_of((ranks, positions, width), bf16),
        (values, cot, plain_map, other_map),
        16,
    )
    message = lax.all_to_all(message, RANK, 0, 0, tiled=True)
    by_seq = message.reshape(seq_ranks, dp_ranks, positions, width)
    forward = [(i, i + 1) for i in range(seq_blocks - 1)]
    backward = [(target, source) for source, target in forward]
    low = lax.ppermute(by_seq[-1, :, -HALO:], "seq_block", forward)
    high = lax.ppermute(by_seq[0, :, :HALO], "seq_block", backward)
    normed, grads, swapped_gain = called(
        prepare,
        (
            shape_of((strands, span, channels), bf16),
            shape_of((strands, span, LANES), bf16),
            shape_of((1, channels), f32),
        ),
        (message, gain, swap),
        16,
        flops=2 * ranks * positions * channels * channels,
        moved=ranks * positions * (width + 2 * channels) * 2,
    )
    main_args = (me, mine, *other_kernels, normed, grads, low, high, gain, swap)
    sizes = (seq_blocks, dp_blocks, seq_ranks, dp_ranks)
    shifted, kernel, gelus, outgoing = called(
        lambda *refs: main_body(sizes, *refs),
        (
            shape_of((strands, span, taps * LANES), bf16),
            shape_of((taps * LANES, channels), bf16),
            shape_of((strands, span, LANES), bf16),
            shape_of((owners, part + EXTRA, rows), bf16),
        ),
        main_args,
        32,
        scratch=[
            pltpu.VMEM((blocks, ranks, part, rows), bf16),
            pltpu.VMEM((long, taps * LANES), f32),
            pltpu.VMEM((long, LANES), f32),
            pltpu.VMEM((wide, LANES), f32),
            pltpu.VMEM((wide, LANES), f32),
            pltpu.VMEM((taps * LANES, channels), f32),
        ],
        specs=[SMEM] + [VMEM] * (len(main_args) - 1),
        flops=4 * strands * span * taps * LANES * channels,
    )
    terms = lax.all_to_all(outgoing, EVERY, 0, 0, tiled=True)
    core = dp_ranks
    masks = chip_masks(ranks, core)
    halves = shape_of((len(masks), positions, width), bf16)
    own, cross = called(
        input_gradient,
        (halves, halves),
        (rank, shifted, kernel, swap, gain, swapped_gain, gelus),
        16,
        scratch=[pltpu.VMEM((dp_ranks, span, channels), bf16)],
        specs=[SMEM] + [VMEM] * 6,
        flops=2 * strands * span * taps * LANES * channels,
    )
    crossed = lax.ppermute(cross, RANK, flipped_pairs(ranks, core))
    leaving = called(
        lambda *refs: chip_sum(part, *refs),
        tuple(shape_of((positions, channels + 4 * part), bf16) for _ in masks),
        (own, crossed),
        8,
    )
    arrived = leaving[:1] + tuple(
        lax.ppermute(block, RANK, flipped_pairs(ranks, mask))
        for block, mask in zip(leaving[1:], masks[1:])
    )
    combined, grad_input = called(
        lambda *refs: finish(part, core, *refs),
        (shape_of((positions, channels), bf16), shape_of((positions, channels), bf16)),
        (rank, values, cot, plain_map, other_map, *arrived),
        16,
        scratch=[pltpu.VMEM((2, ranks, positions, LANES), bf16)],
        specs=[SMEM] + [VMEM] * (4 + len(arrived)),
    )
    summed = terms.reshape(seq_blocks, seq_ranks, dp_blocks, dp_ranks, -1, rows).astype(f32).sum((0, 2))
    summed = summed.reshape(ranks, -1, rows)
    grad_kernel = summed[:, :part].reshape(channels, rows).T
    grad_gain = summed[:, part : part + 2, : channels // owners].sum((0, 1))
    return combined[None], grad_input[None], grad_kernel, grad_gain


def solution(mesh):
    seq, dp = mesh.shape["seq"], mesh.shape["dp"]
    seq_ranks, dp_ranks = 4, 2
    grouped = Mesh(mesh.devices.reshape(seq // seq_ranks, seq_ranks, dp // dp_ranks, dp_ranks), EVERY)
    along = P(("dp_block", "dp_rank"), ("seq_block", "seq_rank"), None)
    return jax.shard_map(
        per_device,
        mesh=grouped,
        in_specs=(along, along, P(EVERY, None), P(), P()),
        out_specs=(along, along, P(EVERY, None), P(EVERY)),
        check_vma=False,
    )
```

```python
import jax
import jax.numpy as jnp
from jax import lax
from jax.experimental import pallas as pl
from jax.experimental.pallas import tpu as pltpu
from jax.sharding import Mesh, PartitionSpec as P

epsilon = 1e-06
RANK = ("seq_rank", "dp_rank")
BLOCK = ("seq_block", "dp_block")
EVERY = ("seq_block", "seq_rank", "dp_block", "dp_rank")
LANES = 128
HALO = 16
EXTRA = 16
VMEM = pl.BlockSpec(memory_space=pltpu.VMEM)
SMEM = pl.BlockSpec(memory_space=pltpu.SMEM)
bf16 = jnp.bfloat16
f32 = jnp.float32


def called(body, outs, args, vmem, scratch=(), specs=None, flops=0, moved=0):
    return pl.pallas_call(
        body,
        out_shape=outs,
        in_specs=specs or [VMEM] * len(args),
        out_specs=jax.tree.map(lambda _: VMEM, outs),
        scratch_shapes=list(scratch),
        compiler_params=pltpu.CompilerParams(vmem_limit_bytes=vmem * 2**20),
        cost_estimate=pl.CostEstimate(flops=flops, bytes_accessed=moved, transcendentals=0),
    )(*args)


def shape_of(shape, dtype):
    return jax.ShapeDtypeStruct(shape, dtype)


def dot(a, b, contract):
    return lax.dot_general(a, b, (contract, ((), ())), preferred_element_type=f32)


def gelu_and_slope(x):
    inner = 0.7978845608028654 * (x + 0.044715 * (x * x * x))
    bend = jnp.tanh(inner)
    half_sum = 0.5 * (1.0 + bend)
    slope = half_sum + (0.5 * x) * (1.0 - bend * bend) * (
        0.7978845608028654 * (1.0 + 0.134145 * (x * x))
    )
    return x * half_sum, slope


def chip_masks(ranks, core):
    return [mask for mask in range(ranks) if not mask & core]


def pack_messages(core, rank_ref, values_ref, cot_ref, edge_ref, plain_ref, other_ref, *refs):
    home_ref, cross_ref, leaving, slices = refs[0], refs[1], refs[2:-1], refs[-1]
    positions, channels = values_ref.shape
    ranks = slices.shape[0]
    here, edge = slice(0, positions), slice(positions, None)
    for rows, source in ((here, cot_ref[...]), (edge, edge_ref[:, channels:])):
        for n, ref in enumerate((plain_ref, other_ref)):
            piece = dot(source, ref[...], ((1,), (0,))).astype(bf16)
            for j in range(ranks):
                slices[j, rows, n * LANES : (n + 1) * LANES] = piece[:, j * LANES : (j + 1) * LANES]
    rank = rank_ref[0]
    two = 2 * LANES
    starts = [(home_ref, 0), (cross_ref, two)] + [(out, two) for out in leaving]
    for out, start in starts:
        out[here, start : start + channels] = values_ref[...]
        out[edge, start : start + channels] = edge_ref[:, :channels]
    home_ref[:, channels:] = slices[rank]
    cross_ref[:, :two] = slices[lax.bitwise_xor(rank, core)]
    for mask, out in zip(chip_masks(ranks, core)[1:], leaving):
        out[:, :two] = slices[lax.bitwise_xor(rank, mask | core)]
        out[:, two + channels :] = slices[lax.bitwise_xor(rank, mask)]


def normalize(x, gain, swap):
    other = dot(x, swap, ((1,), (0,)))
    x = x.astype(f32)
    rms = lax.rsqrt(jnp.mean(x * x, -1, keepdims=True) + epsilon)
    return [(t * rms * gain).astype(bf16) for t in (x, other)]


def prepare(core, rank_ref, home_ref, home_crossed_ref, crossed_ref, *refs):
    arrived = refs[:-7]
    gain_ref, swap_ref, normed_ref, grads_ref, edge_normed_ref, edge_grads_ref, swapped_gain_ref = refs[-7:]
    dp_ranks = normed_ref.shape[0] // 2
    channels = gain_ref.shape[1]
    masks = chip_masks(2 * (len(arrived) + 1), core)
    seq_ranks = 2 * len(masks) // dp_ranks
    positions = home_ref.shape[0] - HALO
    two = 2 * LANES
    blocks = [(0, home_ref, 0, channels), (core, home_crossed_ref, two, 0)]
    for m, mask in enumerate(masks[1:]):
        blocks.append((mask, arrived[m], two, two + channels))
        blocks.append((mask | core, crossed_ref.at[m], two, 0))
    for flip, ref, lane, grad_lane in blocks:
        source = lax.bitwise_xor(rank_ref[0], flip)
        b, i = lax.rem(source, dp_ranks), lax.div(source, dp_ranks)
        start = pl.multiple_of(i * positions, positions)
        side = jnp.where(i == 0, 0, jnp.where(i == seq_ranks - 1, 1, 2))
        both = normalize(ref[:, lane : lane + channels], gain_ref[...], swap_ref[...])
        for n, normed in enumerate(both):
            first = grad_lane + n * LANES
            grads = (0.5 * ref[:, first : first + LANES].astype(f32)).astype(bf16)
            index = n * dp_ranks + b
            normed_ref[index, pl.ds(start, positions), :] = normed[:positions]
            grads_ref[index, pl.ds(start, positions), :] = grads[:positions]
            edge_normed_ref[side, index] = normed[positions:]
            edge_grads_ref[side, index] = grads[positions:]
    gain = gain_ref[...]
    first = gain.astype(bf16).astype(f32)
    second = (gain - first).astype(bf16).astype(f32)
    third = gain - first - second
    row = lax.broadcasted_iota(jnp.int32, (HALO, channels), 0)
    parts = jnp.where(row == 0, first, jnp.where(row == 1, second, jnp.where(row == 2, third, 0.0)))
    swapped = dot(parts.astype(bf16), swap_ref[...], ((1,), (0,)))
    swapped_gain_ref[...] = swapped[0:1] + swapped[1:2] + swapped[2:3]


def main_body(rank_ref, pieces_ref, normed_ref, grads_ref, edge_normed_ref, edge_grads_ref, *refs):
    gain_ref, swapped_gain_ref, swap_ref, out_ref, own_ref, cross_ref = refs[:6]
    kernel_ref, shifted, gelus, terms, halves, bent, slopes, total, scaled = refs[6:]
    owners, part, rows = pieces_ref.shape
    strands, span, channels = normed_ref.shape
    dp_ranks = strands // 2
    taps = kernel_ref.shape[0] // LANES
    half = taps // 2
    reach = 2 * half
    wide = bent.shape[0]

    def runs(owner):
        first, last = owner * rows, (owner + 1) * rows
        while first < last:
            tap, channel = divmod(first, channels)
            count = min(last - first, channels - channel)
            yield tap, channel, count, first - owner * rows
            first += count

    kernel_ref[...] = jnp.zeros_like(kernel_ref)
    for owner in range(owners):
        for tap, channel, count, offset in runs(owner):
            kernel_ref[tap * LANES : tap * LANES + part, channel : channel + count] = pieces_ref[
                owner, :, offset : offset + count
            ]
    kernel = kernel_ref[...]
    edge_normed = jnp.concatenate([edge_normed_ref[side, s] for side in range(2) for s in range(strands)], 0)
    edge_terms = dot(edge_normed, kernel, ((1,), (1,)))
    for strand in range(strands):
        forward = strand < dp_ranks
        terms[HALO : HALO + span, :] = dot(normed_ref[strand], kernel, ((1,), (1,)))
        halves[HALO : HALO + span, :] = grads_ref[strand].astype(f32)
        for side, start in enumerate((0, HALO + span)):
            first = (side * strands + strand) * HALO
            terms[start : start + HALO, :] = edge_terms[first : first + HALO]
            halves[start : start + HALO, :] = edge_grads_ref[side, strand].astype(f32)
        preact = jnp.zeros((wide, LANES), f32)
        for k in range(taps):
            start = HALO - reach + k if forward else HALO - k
            preact += terms[start : start + wide, k * LANES : (k + 1) * LANES]
        result, slope = gelu_and_slope(preact)
        bent[...] = result
        gelus[strand] = bent[half : half + span, :].astype(bf16)
        slopes[...] = halves[HALO - half : HALO - half + wide, :] * slope
        for k in range(taps):
            start = reach - k if forward else k
            shifted[strand, :, k * LANES : (k + 1) * LANES] = slopes[start : start + span, :].astype(bf16)
    total[...] = dot(
        shifted[...].reshape(strands * span, taps * LANES),
        normed_ref[...].reshape(strands * span, channels),
        ((0,), (0,)),
    )
    gain = jnp.sum(total[...] * kernel.astype(f32), 0, keepdims=True) / gain_ref[...]
    gain_high = gain.astype(bf16).astype(f32)
    row = lax.broadcasted_iota(jnp.int32, (EXTRA, channels), 0)
    extra = jnp.where(row == 0, gain_high, jnp.where(row == 1, gain - gain_high, 0.0))
    own_gain = channels // owners
    for owner in range(owners):
        for tap, channel, count, offset in runs(owner):
            out_ref[owner, :part, offset : offset + count] = total[
                tap * LANES : tap * LANES + part, channel : channel + count
            ].astype(bf16)
        out_ref[owner, part:, :] = jnp.zeros((EXTRA, rows), bf16)
        out_ref[owner, part:, :own_gain] = extra[
            :, owner * own_gain : (owner + 1) * own_gain
        ].astype(bf16)
    swapped = dot(kernel, swap_ref[...], ((1,), (0,))).astype(bf16)
    for b in range(dp_ranks):
        scaled[b] = (
            dot(shifted[b], kernel, ((1,), (0,))) * gain_ref[...]
            + dot(shifted[dp_ranks + b], swapped, ((1,), (0,))) * swapped_gain_ref[...]
        ).astype(bf16)
    chips, positions, _ = own_ref.shape
    for m, mask in enumerate(chip_masks(2 * chips, dp_ranks)):
        for out, flip in ((own_ref, mask), (cross_ref, mask | dp_ranks)):
            target = lax.bitwise_xor(rank_ref[0], flip)
            b = lax.rem(target, dp_ranks)
            start = pl.multiple_of(lax.div(target, dp_ranks) * positions, positions)
            out[m, :, :channels] = scaled[b, pl.ds(start, positions), :]
            for n in range(2):
                lane = channels + n * LANES
                out[m, :, lane : lane + LANES] = gelus[n * dp_ranks + b, pl.ds(start, positions), :]


def chip_sum(part, own_ref, crossed_ref, *outs):
    channels = own_ref.shape[2] - 2 * LANES
    for m, out in enumerate(outs):
        out[:, :channels] = (
            own_ref[m, :, :channels].astype(f32) + crossed_ref[m, :, :channels].astype(f32)
        ).astype(bf16)
        for c, ref in enumerate((own_ref, crossed_ref)):
            for n in range(2):
                lane = channels + n * LANES
                start = channels + (2 * c + n) * part
                out[:, start : start + part] = ref[m, :, lane : lane + part]


def finish(part, core, rank_ref, values_ref, cot_ref, plain_ref, other_ref, *refs):
    arrived, (combined_ref, grad_ref, gelus) = refs[:-3], refs[-3:]
    channels = values_ref.shape[1]
    ranks = gelus.shape[1]
    gelus[...] = jnp.zeros_like(gelus)
    scaled = jnp.zeros(values_ref.shape, f32)
    for mask, block in zip(chip_masks(ranks, core), arrived):
        scaled += block[:, :channels].astype(f32)
        for c in range(2):
            source = lax.bitwise_xor(rank_ref[0], mask | c * core)
            for n in range(2):
                start = channels + (2 * c + n) * part
                gelus[n, source, :, :part] = block[:, start : start + part]
    joined = [jnp.concatenate([gelus[n, j] for j in range(ranks)], -1) for n in range(2)]
    plain = dot(joined[0], plain_ref[...], ((1,), (1,)))
    other = dot(joined[1], other_ref[...], ((1,), (1,)))
    values = values_ref[...].astype(f32)
    rms = lax.rsqrt(jnp.mean(values * values, -1, keepdims=True) + epsilon)
    reverse_out = (values + other).astype(bf16).astype(f32)
    combined_ref[...] = (0.5 * (values + plain + reverse_out)).astype(bf16)
    along = jnp.mean(scaled * values, -1, keepdims=True)
    grad_ref[...] = (cot_ref[...].astype(f32) + rms * scaled - values * (rms * rms * rms * along)).astype(bf16)


def collect(owner_of, terms_ref, kernel_ref, gain_ref, joined):
    _, height, rows = terms_ref.shape
    part = height - EXTRA
    joined[...] = jnp.zeros_like(joined)
    gain = jnp.zeros((1, rows), f32)
    for rank, owners in enumerate(owner_of):
        total = terms_ref[owners[0]].astype(f32)
        for owner in owners[1:]:
            total += terms_ref[owner].astype(f32)
        joined[rank * part : (rank + 1) * part, :rows] = total[:part]
        gain += total[part : part + 1] + total[part + 1 : part + 2]
    kernel_ref[...] = joined[...].T[:rows]
    gain_ref[...] = gain[:, : gain_ref.shape[1]]


def flipped_pairs(count, mask):
    return [(i, i ^ mask) for i in range(count)]


def per_device(activations, cotangent, weights, norm_gain, pairing):
    seq_ranks = lax.axis_size("seq_rank")
    dp_ranks = lax.axis_size("dp_rank")
    seq_blocks = lax.axis_size("seq_block")
    dp_blocks = lax.axis_size("dp_block")
    ranks = seq_ranks * dp_ranks
    owners = ranks * seq_blocks * dp_blocks
    positions, channels = activations.shape[1:]
    rows = weights.shape[0]
    taps = rows * owners // channels
    part = channels // ranks
    span = positions * seq_ranks
    long = span + 2 * HALO
    reach = taps - taps % 2
    wide = -(-(span + reach) // 8) * 8
    strands = 2 * dp_ranks
    width = channels + 2 * LANES
    rank = lax.axis_index(RANK).reshape(1)
    values, cot = activations[0], cotangent[0]
    along = ("seq_block", "seq_rank")
    ends = [(b * seq_ranks - 1, b * seq_ranks) for b in range(1, seq_blocks)]
    both = jnp.concatenate([values, cot], -1)
    low = lax.ppermute(both[-HALO:], along, ends)
    high = lax.ppermute(both[:HALO], along, [(target, source) for source, target in ends])
    slices = weights.T.reshape(1, seq_ranks, 1, dp_ranks, part, rows)
    slices = jnp.broadcast_to(slices, (seq_blocks, seq_ranks, dp_blocks, dp_ranks, part, rows))
    pieces = lax.all_to_all(slices.reshape(owners, part, rows), EVERY, 0, 0, tiled=True)
    slot = jnp.arange(ranks * LANES, dtype=jnp.int32)
    channel_of = jnp.where(slot % LANES < part, slot // LANES * part + slot % LANES, -1)
    channel_list = jnp.arange(channels, dtype=jnp.int32)
    plain_map = (channel_list[:, None] == channel_of).astype(bf16)
    other_map = (pairing[:, None] == channel_of).astype(bf16)
    swap = (pairing[:, None] == channel_list).astype(bf16)
    gain = norm_gain.reshape(1, channels)
    core = dp_ranks
    masks = chip_masks(ranks, core)
    block = positions + HALO
    home, cross, *leaving = called(
        lambda *refs: pack_messages(core, *refs),
        (shape_of((block, width), bf16),) * 2
        + tuple(shape_of((block, width + 2 * LANES), bf16) for _ in masks[1:]),
        (rank, values, cot, low + high, plain_map, other_map),
        16,
        scratch=[pltpu.VMEM((ranks, block, 2 * LANES), bf16)],
        specs=[SMEM] + [VMEM] * 5,
    )
    arrived = [
        lax.ppermute(message, RANK, flipped_pairs(ranks, mask))
        for message, mask in zip(leaving, masks[1:])
    ]
    home_crossed = lax.ppermute(cross, RANK, flipped_pairs(ranks, core))
    crossed = lax.ppermute(
        jnp.stack([message[:, :width] for message in arrived]), RANK, flipped_pairs(ranks, core)
    )
    normed, grads, edge_normed, edge_grads, swapped_gain = called(
        lambda *refs: prepare(core, *refs),
        (
            shape_of((strands, span, channels), bf16),
            shape_of((strands, span, LANES), bf16),
            shape_of((3, strands, HALO, channels), bf16),
            shape_of((3, strands, HALO, LANES), bf16),
            shape_of((1, channels), f32),
        ),
        (rank, home, home_crossed, crossed, *arrived, gain, swap),
        16,
        specs=[SMEM] + [VMEM] * (5 + len(arrived)),
        flops=2 * ranks * positions * channels * channels,
        moved=ranks * positions * (width + 2 * channels) * 2,
    )
    sent = shape_of((len(masks), positions, width), bf16)
    outgoing, own, cross = called(
        main_body,
        (shape_of((owners, part + EXTRA, rows), bf16), sent, sent),
        (rank, pieces, normed, grads, edge_normed, edge_grads, gain, swapped_gain, swap),
        32,
        scratch=[
            pltpu.VMEM((taps * LANES, channels), bf16),
            pltpu.VMEM((strands, span, taps * LANES), bf16),
            pltpu.VMEM((strands, span, LANES), bf16),
            pltpu.VMEM((long, taps * LANES), f32),
            pltpu.VMEM((long, LANES), f32),
            pltpu.VMEM((wide, LANES), f32),
            pltpu.VMEM((wide, LANES), f32),
            pltpu.VMEM((taps * LANES, channels), f32),
            pltpu.VMEM((dp_ranks, span, channels), bf16),
        ],
        specs=[SMEM] + [VMEM] * 8,
        flops=6 * strands * span * taps * LANES * channels,
    )
    terms = lax.all_to_all(outgoing, EVERY, 0, 0, tiled=True)
    crossed = lax.ppermute(cross, RANK, flipped_pairs(ranks, core))
    leaving = called(
        lambda *refs: chip_sum(part, *refs),
        tuple(shape_of((positions, channels + 4 * part), bf16) for _ in masks),
        (own, crossed),
        8,
    )
    arrived = leaving[:1] + tuple(
        lax.ppermute(message, RANK, flipped_pairs(ranks, mask))
        for message, mask in zip(leaving[1:], masks[1:])
    )
    combined, grad_input = called(
        lambda *refs: finish(part, core, *refs),
        (shape_of((positions, channels), bf16), shape_of((positions, channels), bf16)),
        (rank, values, cot, plain_map, other_map, *arrived),
        16,
        scratch=[pltpu.VMEM((2, ranks, positions, LANES), bf16)],
        specs=[SMEM] + [VMEM] * (4 + len(arrived)),
    )
    order = [
        [
            ((sb * seq_ranks + sr) * dp_blocks + db) * dp_ranks + dr
            for sb in range(seq_blocks)
            for db in range(dp_blocks)
        ]
        for sr in range(seq_ranks)
        for dr in range(dp_ranks)
    ]
    grad_kernel, grad_gain = called(
        lambda *refs: collect(order, *refs),
        (shape_of((rows, channels), f32), shape_of((1, channels // owners), f32)),
        (terms,),
        16,
        scratch=[pltpu.VMEM((channels, -(-rows // LANES) * LANES), f32)],
    )
    return combined[None], grad_input[None], grad_kernel, grad_gain[0]


def solution(mesh):
    seq, dp = mesh.shape["seq"], mesh.shape["dp"]
    seq_ranks, dp_ranks = 4, 2
    grouped = Mesh(mesh.devices.reshape(seq // seq_ranks, seq_ranks, dp // dp_ranks, dp_ranks), EVERY)
    along = P(("dp_block", "dp_rank"), ("seq_block", "seq_rank"), None)
    return jax.shard_map(
        per_device,
        mesh=grouped,
        in_specs=(along, along, P(EVERY, None), P(), P()),
        out_specs=(along, along, P(EVERY, None), P(EVERY)),
        check_vma=False,
    )
```

```python
import jax
import jax.numpy as jnp
from jax import lax
from jax.experimental import pallas as pl
from jax.experimental.pallas import tpu as pltpu
from jax.sharding import Mesh, PartitionSpec as P

epsilon = 1e-06
RANK = ("seq_rank", "dp_rank")
BLOCK = ("seq_block", "dp_block")
EVERY = ("seq_block", "seq_rank", "dp_block", "dp_rank")
LANES = 128
HALO = 16
EXTRA = 16
VMEM = pl.BlockSpec(memory_space=pltpu.VMEM)
SMEM = pl.BlockSpec(memory_space=pltpu.SMEM)
HBM = pl.BlockSpec(memory_space=pltpu.HBM)
bf16 = jnp.bfloat16
f32 = jnp.float32


def called(body, outs, args, vmem, scratch=(), specs=None, out_specs=None, flops=0, moved=0):
    return pl.pallas_call(
        body,
        out_shape=outs,
        in_specs=specs or [VMEM] * len(args),
        out_specs=out_specs or jax.tree.map(lambda _: VMEM, outs),
        scratch_shapes=list(scratch),
        compiler_params=pltpu.CompilerParams(vmem_limit_bytes=vmem * 2**20),
        cost_estimate=pl.CostEstimate(flops=flops, bytes_accessed=moved, transcendentals=0),
    )(*args)


def shape_of(shape, dtype):
    return jax.ShapeDtypeStruct(shape, dtype)


def dot(a, b, contract):
    return lax.dot_general(a, b, (contract, ((), ())), preferred_element_type=f32)


def gelu_and_slope(x):
    inner = 0.7978845608028654 * (x + 0.044715 * (x * x * x))
    bend = jnp.tanh(inner)
    half_sum = 0.5 * (1.0 + bend)
    slope = half_sum + (0.5 * x) * (1.0 - bend * bend) * (
        0.7978845608028654 * (1.0 + 0.134145 * (x * x))
    )
    return x * half_sum, slope


def slot_maps(part, slots, pairing):
    shape = (slots, pairing.shape[1])
    slot = lax.broadcasted_iota(jnp.int32, shape, 0)
    lane = lax.bitwise_and(slot, LANES - 1)
    channel_of = jnp.where(lane < part, lax.div(slot, LANES) * part + lane, -1)
    channel = lax.broadcasted_iota(jnp.int32, shape, 1)
    return [jnp.where(channel_of == c, 1.0, 0.0).astype(bf16) for c in (channel, pairing)]


def swap_map(pairing):
    channels = pairing.shape[1]
    row = lax.broadcasted_iota(jnp.int32, (channels, channels), 0)
    return jnp.where(row == pairing, 1.0, 0.0).astype(bf16)


def chip_masks(ranks, core):
    return [mask for mask in range(ranks) if not mask & core]


def pack_messages(part, core, rank_ref, values_ref, cot_ref, edge_ref, pairing_ref, *refs):
    home_ref, cross_ref, leaving, slices = refs[0], refs[1], refs[2:-1], refs[-1]
    positions, channels = values_ref.shape
    ranks = slices.shape[0]
    here, edge = slice(0, positions), slice(positions, None)
    for n, map_of in enumerate(slot_maps(part, ranks * LANES, pairing_ref[...])):
        for rows, source in ((here, cot_ref[...]), (edge, edge_ref[:, channels:])):
            piece = dot(source, map_of, ((1,), (1,))).astype(bf16)
            for j in range(ranks):
                slices[j, rows, n * LANES : (n + 1) * LANES] = piece[:, j * LANES : (j + 1) * LANES]
    rank = rank_ref[0]
    two = 2 * LANES
    starts = [(home_ref, 0), (cross_ref, two)] + [(out, two) for out in leaving]
    for out, start in starts:
        out[here, start : start + channels] = values_ref[...]
        out[edge, start : start + channels] = edge_ref[:, :channels]
    home_ref[:, channels:] = slices[rank]
    cross_ref[:, :two] = slices[lax.bitwise_xor(rank, core)]
    for mask, out in zip(chip_masks(ranks, core)[1:], leaving):
        out[:, :two] = slices[lax.bitwise_xor(rank, mask | core)]
        out[:, two + channels :] = slices[lax.bitwise_xor(rank, mask)]


def stack_crossing(cross_ref, *refs):
    out_ref = refs[-1]
    width = out_ref.shape[2]
    for m, ref in enumerate((cross_ref,) + refs[:-1]):
        out_ref[m] = ref[:, :width]


def normalize(x, gain, swap):
    other = dot(x, swap, ((1,), (0,)))
    x = x.astype(f32)
    rms = lax.rsqrt(jnp.mean(x * x, -1, keepdims=True) + epsilon)
    return [(t * rms * gain).astype(bf16) for t in (x, other)]


def prepare(core, rank_ref, home_ref, crossed_ref, *refs):
    arrived = refs[:-7]
    gain_ref, pairing_ref, normed_ref, grads_ref, edge_normed_ref, edge_grads_ref, swapped_gain_ref = refs[-7:]
    dp_ranks = normed_ref.shape[0] // 2
    channels = gain_ref.shape[1]
    masks = chip_masks(2 * (len(arrived) + 1), core)
    seq_ranks = 2 * len(masks) // dp_ranks
    positions = home_ref.shape[0] - HALO
    two = 2 * LANES
    swap = swap_map(pairing_ref[...])
    blocks = [(0, home_ref, 0, channels)]
    blocks += [(mask, ref, two, two + channels) for mask, ref in zip(masks[1:], arrived)]
    blocks += [(mask | core, crossed_ref.at[m], two, 0) for m, mask in enumerate(masks)]
    for flip, ref, lane, grad_lane in blocks:
        source = lax.bitwise_xor(rank_ref[0], flip)
        b, i = lax.rem(source, dp_ranks), lax.div(source, dp_ranks)
        start = pl.multiple_of(i * positions, positions)
        side = jnp.where(i == 0, 0, jnp.where(i == seq_ranks - 1, 1, 2))
        both = normalize(ref[:, lane : lane + channels], gain_ref[...], swap)
        for n, normed in enumerate(both):
            first = grad_lane + n * LANES
            grads = (0.5 * ref[:, first : first + LANES].astype(f32)).astype(bf16)
            index = n * dp_ranks + b
            normed_ref[index, pl.ds(start, positions), :] = normed[:positions]
            grads_ref[index, pl.ds(start, positions), :] = grads[:positions]
            edge_normed_ref[side, index] = normed[positions:]
            edge_grads_ref[side, index] = grads[positions:]
    gain = gain_ref[...]
    first = gain.astype(bf16).astype(f32)
    second = (gain - first).astype(bf16).astype(f32)
    third = gain - first - second
    row = lax.broadcasted_iota(jnp.int32, (HALO, channels), 0)
    parts = jnp.where(row == 0, first, jnp.where(row == 1, second, jnp.where(row == 2, third, 0.0)))
    swapped = dot(parts.astype(bf16), swap, ((1,), (0,)))
    swapped_gain_ref[...] = swapped[0:1] + swapped[1:2] + swapped[2:3]


def main_body(sizes, place_ref, near_ref, far_ref, normed_ref, grads_ref, edge_normed_ref, edge_grads_ref, *refs):
    gain_ref, swapped_gain_ref, pairing_ref, sent_ref, own_ref, cross_ref = refs[:6]
    pieces, kernel_ref, shifted, gelus, terms, halves, bent, slopes, total, scaled = refs[6:16]
    out_ref, own, cross, sems = refs[16:]
    seq_blocks, dp_blocks, seq_ranks, dp_ranks = sizes
    rank, me = place_ref[0], place_ref[1]
    owners = seq_blocks * dp_blocks * seq_ranks * dp_ranks
    part, rows = near_ref.shape[2:]
    strands, span, channels = normed_ref.shape
    taps = kernel_ref.shape[0] // LANES
    half = taps // 2
    reach = 2 * half
    wide = bent.shape[0]

    def runs(owner):
        first, last = owner * rows, (owner + 1) * rows
        while first < last:
            tap, channel = divmod(first, channels)
            count = min(last - first, channels - channel)
            yield tap, channel, count, first - owner * rows
            first += count

    for ref, first in ((near_ref, 0), (far_ref, near_ref.shape[0])):
        for j in range(ref.shape[0]):
            pieces[lax.bitwise_xor(me, first + j)] = ref[j]
    kernel_ref[...] = jnp.zeros_like(kernel_ref)
    places = [
        (sb * dp_blocks + db, sr * dp_ranks + dr)
        for sb in range(seq_blocks)
        for sr in range(seq_ranks)
        for db in range(dp_blocks)
        for dr in range(dp_ranks)
    ]
    for owner, (source, piece) in enumerate(places):
        for tap, channel, count, offset in runs(owner):
            kernel_ref[tap * LANES : tap * LANES + part, channel : channel + count] = pieces[
                source, piece, :, offset : offset + count
            ]
    kernel = kernel_ref[...]
    edge_normed = jnp.concatenate([edge_normed_ref[side, s] for side in range(2) for s in range(strands)], 0)
    edge_terms = dot(edge_normed, kernel, ((1,), (1,)))
    for strand in range(strands):
        forward = strand < dp_ranks
        terms[HALO : HALO + span, :] = dot(normed_ref[strand], kernel, ((1,), (1,)))
        halves[HALO : HALO + span, :] = grads_ref[strand].astype(f32)
        for side, start in enumerate((0, HALO + span)):
            first = (side * strands + strand) * HALO
            terms[start : start + HALO, :] = edge_terms[first : first + HALO]
            halves[start : start + HALO, :] = edge_grads_ref[side, strand].astype(f32)
        preact = jnp.zeros((wide, LANES), f32)
        for k in range(taps):
            start = HALO - reach + k if forward else HALO - k
            preact += terms[start : start + wide, k * LANES : (k + 1) * LANES]
        result, slope = gelu_and_slope(preact)
        bent[...] = result
        gelus[strand] = bent[half : half + span, :].astype(bf16)
        slopes[...] = halves[HALO - half : HALO - half + wide, :] * slope
        for k in range(taps):
            start = reach - k if forward else k
            shifted[strand, :, k * LANES : (k + 1) * LANES] = slopes[start : start + span, :].astype(bf16)
    total[...] = dot(
        shifted[...].reshape(strands * span, taps * LANES),
        normed_ref[...].reshape(strands * span, channels),
        ((0,), (0,)),
    )
    gain = jnp.sum(total[...] * kernel.astype(f32), 0, keepdims=True) / gain_ref[...]
    gain_high = gain.astype(bf16).astype(f32)
    row = lax.broadcasted_iota(jnp.int32, (EXTRA, channels), 0)
    extra = jnp.where(row == 0, gain_high, jnp.where(row == 1, gain - gain_high, 0.0))
    own_gain = channels // owners
    for owner in range(owners):
        for tap, channel, count, offset in runs(owner):
            out_ref[owner, :part, offset : offset + count] = total[
                tap * LANES : tap * LANES + part, channel : channel + count
            ].astype(bf16)
        out_ref[owner, part:, :] = jnp.zeros((EXTRA, rows), bf16)
        out_ref[owner, part:, :own_gain] = extra[
            :, owner * own_gain : (owner + 1) * own_gain
        ].astype(bf16)
    copies = [pltpu.make_async_copy(out_ref, sent_ref, sems.at[0])]
    copies[0].start()
    swapped = dot(kernel, swap_map(pairing_ref[...]), ((1,), (0,))).astype(bf16)
    for b in range(dp_ranks):
        scaled[b] = (
            dot(shifted[b], kernel, ((1,), (0,))) * gain_ref[...]
            + dot(shifted[dp_ranks + b], swapped, ((1,), (0,))) * swapped_gain_ref[...]
        ).astype(bf16)
    chips, positions, _ = own.shape
    for c, (out, ref) in enumerate(((cross, cross_ref), (own, own_ref))):
        for m, mask in enumerate(chip_masks(2 * chips, dp_ranks)):
            target = lax.bitwise_xor(rank, mask if c else mask | dp_ranks)
            b = lax.rem(target, dp_ranks)
            start = pl.multiple_of(lax.div(target, dp_ranks) * positions, positions)
            out[m, :, :channels] = scaled[b, pl.ds(start, positions), :]
            for n in range(2):
                lane = channels + n * LANES
                out[m, :, lane : lane + LANES] = gelus[n * dp_ranks + b, pl.ds(start, positions), :]
        copies.append(pltpu.make_async_copy(out, ref, sems.at[1 + c]))
        copies[-1].start()
    for copy in copies:
        copy.wait()


def chip_sum(part, own_ref, crossed_ref, *outs):
    channels = own_ref.shape[2] - 2 * LANES
    for m, out in enumerate(outs):
        out[:, :channels] = (
            own_ref[m, :, :channels].astype(f32) + crossed_ref[m, :, :channels].astype(f32)
        ).astype(bf16)
        for c, ref in enumerate((own_ref, crossed_ref)):
            for n in range(2):
                lane = channels + n * LANES
                start = channels + (2 * c + n) * part
                out[:, start : start + part] = ref[m, :, lane : lane + part]


def finish(part, core, rank_ref, values_ref, cot_ref, pairing_ref, *refs):
    arrived, (combined_ref, grad_ref, gelus) = refs[:-3], refs[-3:]
    channels = values_ref.shape[1]
    ranks = gelus.shape[1]
    gelus[...] = jnp.zeros_like(gelus)
    scaled = jnp.zeros(values_ref.shape, f32)
    for mask, block in zip(chip_masks(ranks, core), arrived):
        scaled += block[:, :channels].astype(f32)
        for c in range(2):
            source = lax.bitwise_xor(rank_ref[0], mask | c * core)
            for n in range(2):
                start = channels + (2 * c + n) * part
                gelus[n, source, :, :part] = block[:, start : start + part]
    joined = [jnp.concatenate([gelus[n, j] for j in range(ranks)], -1) for n in range(2)]
    maps = slot_maps(part, ranks * LANES, pairing_ref[...])
    plain, other = [dot(j, m, ((1,), (0,))) for j, m in zip(joined, maps)]
    values = values_ref[...].astype(f32)
    rms = lax.rsqrt(jnp.mean(values * values, -1, keepdims=True) + epsilon)
    reverse_out = (values + other).astype(bf16).astype(f32)
    combined_ref[...] = (0.5 * (values + plain + reverse_out)).astype(bf16)
    along = jnp.mean(scaled * values, -1, keepdims=True)
    grad_ref[...] = (cot_ref[...].astype(f32) + rms * scaled - values * (rms * rms * rms * along)).astype(bf16)


def collect(owner_of, terms_ref, kernel_ref, gain_ref, joined):
    _, height, rows = terms_ref.shape
    part = height - EXTRA
    joined[...] = jnp.zeros_like(joined)
    gain = jnp.zeros((1, rows), f32)
    for rank, owners in enumerate(owner_of):
        total = terms_ref[owners[0]].astype(f32)
        for owner in owners[1:]:
            total += terms_ref[owner].astype(f32)
        joined[rank * part : (rank + 1) * part, :rows] = total[:part]
        gain += total[part : part + 1] + total[part + 1 : part + 2]
    kernel_ref[...] = joined[...].T[:rows]
    gain_ref[...] = gain[:, : gain_ref.shape[1]]


def flipped_pairs(count, mask):
    return [(i, i ^ mask) for i in range(count)]


def per_device(activations, cotangent, weights, norm_gain, pairing):
    seq_ranks = lax.axis_size("seq_rank")
    dp_ranks = lax.axis_size("dp_rank")
    seq_blocks = lax.axis_size("seq_block")
    dp_blocks = lax.axis_size("dp_block")
    ranks = seq_ranks * dp_ranks
    owners = ranks * seq_blocks * dp_blocks
    positions, channels = activations.shape[1:]
    rows = weights.shape[0]
    taps = rows * owners // channels
    part = channels // ranks
    span = positions * seq_ranks
    long = span + 2 * HALO
    reach = taps - taps % 2
    wide = -(-(span + reach) // 8) * 8
    strands = 2 * dp_ranks
    width = channels + 2 * LANES
    rank = lax.axis_index(RANK).reshape(1)
    place = jnp.concatenate([rank, lax.axis_index(BLOCK).reshape(1)])
    values, cot = activations[0], cotangent[0]
    slices = lax.all_to_all(weights.T.reshape(ranks, part, rows), RANK, 0, 0, tiled=True)
    far = slices[None]
    stages = [1 << bit for bit in range((seq_blocks * dp_blocks).bit_length() - 1)]
    for mask in stages:
        near = far if mask == 1 else jnp.concatenate([near, far])
        far = lax.ppermute(near, BLOCK, flipped_pairs(seq_blocks * dp_blocks, mask))
    slices, values, cot = lax.optimization_barrier((slices, values, cot))
    along = ("seq_block", "seq_rank")
    ends = [(b * seq_ranks - 1, b * seq_ranks) for b in range(1, seq_blocks)]
    both = jnp.concatenate([values, cot], -1)
    low = lax.ppermute(both[-HALO:], along, ends)
    high = lax.ppermute(both[:HALO], along, [(target, source) for source, target in ends])
    pairing = pairing.reshape(1, channels)
    gain = norm_gain.reshape(1, channels)
    core = dp_ranks
    masks = chip_masks(ranks, core)
    block = positions + HALO
    home, cross, *leaving = called(
        lambda *refs: pack_messages(part, core, *refs),
        (shape_of((block, width), bf16),) * 2
        + tuple(shape_of((block, width + 2 * LANES), bf16) for _ in masks[1:]),
        (rank, values, cot, low + high, pairing),
        16,
        scratch=[pltpu.VMEM((ranks, block, 2 * LANES), bf16)],
        specs=[SMEM] + [VMEM] * 4,
    )
    arrived = [
        lax.ppermute(message, RANK, flipped_pairs(ranks, mask))
        for message, mask in zip(leaving, masks[1:])
    ]
    crossing = called(
        stack_crossing, shape_of((len(masks), block, width), bf16), (cross, *arrived), 8
    )
    crossed = lax.ppermute(crossing, RANK, flipped_pairs(ranks, core))
    normed, grads, edge_normed, edge_grads, swapped_gain = called(
        lambda *refs: prepare(core, *refs),
        (
            shape_of((strands, span, channels), bf16),
            shape_of((strands, span, LANES), bf16),
            shape_of((3, strands, HALO, channels), bf16),
            shape_of((3, strands, HALO, LANES), bf16),
            shape_of((1, channels), f32),
        ),
        (rank, home, crossed, *arrived, gain, pairing),
        16,
        specs=[SMEM] + [VMEM] * (4 + len(arrived)),
        flops=2 * ranks * positions * channels * channels,
        moved=ranks * positions * (width + 2 * channels) * 2,
    )
    sent = (owners, part + EXTRA, rows)
    halves = (len(masks), positions, width)
    sizes = (seq_blocks, dp_blocks, seq_ranks, dp_ranks)
    outgoing, own, cross = called(
        lambda *refs: main_body(sizes, *refs),
        tuple(pltpu.HBM(shape, bf16) for shape in (sent, halves, halves)),
        (place, near, far, normed, grads, edge_normed, edge_grads, gain, swapped_gain, pairing),
        40,
        scratch=[
            pltpu.VMEM((seq_blocks * dp_blocks, ranks, part, rows), bf16),
            pltpu.VMEM((taps * LANES, channels), bf16),
            pltpu.VMEM((strands, span, taps * LANES), bf16),
            pltpu.VMEM((strands, span, LANES), bf16),
            pltpu.VMEM((long, taps * LANES), f32),
            pltpu.VMEM((long, LANES), f32),
            pltpu.VMEM((wide, LANES), f32),
            pltpu.VMEM((wide, LANES), f32),
            pltpu.VMEM((taps * LANES, channels), f32),
            pltpu.VMEM((dp_ranks, span, channels), bf16),
            pltpu.VMEM(sent, bf16),
            pltpu.VMEM(halves, bf16),
            pltpu.VMEM(halves, bf16),
            pltpu.SemaphoreType.DMA((3,)),
        ],
        specs=[SMEM] + [VMEM] * 9,
        out_specs=(HBM,) * 3,
        flops=6 * strands * span * taps * LANES * channels,
    )
    terms = lax.all_to_all(outgoing, EVERY, 0, 0, tiled=True)
    crossed = lax.ppermute(cross, RANK, flipped_pairs(ranks, core))
    leaving = called(
        lambda *refs: chip_sum(part, *refs),
        tuple(shape_of((positions, channels + 4 * part), bf16) for _ in masks),
        (own, crossed),
        8,
    )
    arrived = leaving[:1] + tuple(
        lax.ppermute(message, RANK, flipped_pairs(ranks, mask))
        for message, mask in zip(leaving[1:], masks[1:])
    )
    combined, grad_input = called(
        lambda *refs: finish(part, core, *refs),
        (shape_of((positions, channels), bf16), shape_of((positions, channels), bf16)),
        (rank, values, cot, pairing, *arrived),
        16,
        scratch=[pltpu.VMEM((2, ranks, positions, LANES), bf16)],
        specs=[SMEM] + [VMEM] * (3 + len(arrived)),
    )
    order = [
        [
            ((sb * seq_ranks + sr) * dp_blocks + db) * dp_ranks + dr
            for sb in range(seq_blocks)
            for db in range(dp_blocks)
        ]
        for sr in range(seq_ranks)
        for dr in range(dp_ranks)
    ]
    grad_kernel, grad_gain = called(
        lambda *refs: collect(order, *refs),
        (shape_of((rows, channels), f32), shape_of((1, channels // owners), f32)),
        (terms,),
        16,
        scratch=[pltpu.VMEM((channels, -(-rows // LANES) * LANES), f32)],
    )
    return combined[None], grad_input[None], grad_kernel, grad_gain[0]


def solution(mesh):
    seq, dp = mesh.shape["seq"], mesh.shape["dp"]
    seq_ranks, dp_ranks = 4, 2
    grouped = Mesh(mesh.devices.reshape(seq // seq_ranks, seq_ranks, dp // dp_ranks, dp_ranks), EVERY)
    along = P(("dp_block", "dp_rank"), ("seq_block", "seq_rank"), None)
    return jax.shard_map(
        per_device,
        mesh=grouped,
        in_specs=(along, along, P(EVERY, None), P(), P()),
        out_specs=(along, along, P(EVERY, None), P(EVERY)),
        check_vma=False,
    )
```

```python
import jax
import jax.numpy as jnp
from jax import lax
from jax.experimental import pallas as pl
from jax.experimental.pallas import tpu as pltpu
from jax.sharding import Mesh, PartitionSpec as P

epsilon = 1e-06
RANK = ("seq_rank", "dp_rank")
BLOCK = ("seq_block", "dp_block")
EVERY = ("seq_block", "seq_rank", "dp_block", "dp_rank")
LANES = 128
HALO = 16
EXTRA = 16
VMEM = pl.BlockSpec(memory_space=pltpu.VMEM)
SMEM = pl.BlockSpec(memory_space=pltpu.SMEM)
HBM = pl.BlockSpec(memory_space=pltpu.HBM)
bf16 = jnp.bfloat16
f32 = jnp.float32


def called(body, outs, args, vmem, scratch=(), specs=None, out_specs=None, flops=0, moved=0):
    return pl.pallas_call(
        body,
        out_shape=outs,
        in_specs=specs or [VMEM] * len(args),
        out_specs=out_specs or jax.tree.map(lambda _: VMEM, outs),
        scratch_shapes=list(scratch),
        compiler_params=pltpu.CompilerParams(vmem_limit_bytes=vmem * 2**20),
        cost_estimate=pl.CostEstimate(flops=0, bytes_accessed=0, transcendentals=0),
    )(*args)


def shape_of(shape, dtype):
    return jax.ShapeDtypeStruct(shape, dtype)


def dot(a, b, contract):
    return lax.dot_general(a, b, (contract, ((), ())), preferred_element_type=f32)


def gelu_and_slope(x):
    inner = 0.7978845608028654 * (x + 0.044715 * (x * x * x))
    bend = jnp.tanh(inner)
    half_sum = 0.5 * (1.0 + bend)
    slope = half_sum + (0.5 * x) * (1.0 - bend * bend) * (
        0.7978845608028654 * (1.0 + 0.134145 * (x * x))
    )
    return x * half_sum, slope


def slot_maps(part, slots, pairing):
    shape = (slots, pairing.shape[1])
    slot = lax.broadcasted_iota(jnp.int32, shape, 0)
    lane = lax.bitwise_and(slot, LANES - 1)
    channel_of = jnp.where(lane < part, lax.div(slot, LANES) * part + lane, -1)
    channel = lax.broadcasted_iota(jnp.int32, shape, 1)
    return [jnp.where(channel_of == c, 1.0, 0.0).astype(bf16) for c in (channel, pairing)]


def swap_map(pairing):
    channels = pairing.shape[1]
    row = lax.broadcasted_iota(jnp.int32, (channels, channels), 0)
    return jnp.where(row == pairing, 1.0, 0.0).astype(bf16)


def chip_masks(ranks, core):
    return [mask for mask in range(ranks) if not mask & core]


def pack_messages(part, core, rank_ref, values_ref, cot_ref, edge_ref, pairing_ref, *refs):
    home_ref, cross_ref, leaving, slices = refs[0], refs[1], refs[2:-1], refs[-1]
    positions, channels = values_ref.shape
    ranks = slices.shape[0]
    here, edge = slice(0, positions), slice(positions, None)
    for n, map_of in enumerate(slot_maps(part, ranks * LANES, pairing_ref[...])):
        for rows, source in ((here, cot_ref[...]), (edge, edge_ref[:, channels:])):
            piece = dot(source, map_of, ((1,), (1,))).astype(bf16)
            for j in range(ranks):
                slices[j, rows, n * LANES : (n + 1) * LANES] = piece[:, j * LANES : (j + 1) * LANES]
    rank = rank_ref[0]
    two = 2 * LANES
    starts = [(home_ref, 0), (cross_ref, two)] + [(out, two) for out in leaving]
    for out, start in starts:
        out[here, start : start + channels] = values_ref[...]
        out[edge, start : start + channels] = edge_ref[:, :channels]
    home_ref[:, channels:] = slices[rank]
    cross_ref[:, :two] = slices[lax.bitwise_xor(rank, core)]
    for mask, out in zip(chip_masks(ranks, core)[1:], leaving):
        out[:, :two] = slices[lax.bitwise_xor(rank, mask | core)]
        out[:, two + channels :] = slices[lax.bitwise_xor(rank, mask)]


def stack_crossing(cross_ref, *refs):
    out_ref = refs[-1]
    width = out_ref.shape[2]
    for m, ref in enumerate((cross_ref,) + refs[:-1]):
        out_ref[m] = ref[:, :width]


def normalize(x, gain, swap):
    other = dot(x, swap, ((1,), (0,)))
    x = x.astype(f32)
    rms = lax.rsqrt(jnp.mean(x * x, -1, keepdims=True) + epsilon)
    return [(t * rms * gain).astype(bf16) for t in (x, other)]


def prepare(core, rank_ref, home_ref, crossed_ref, *refs):
    arrived = refs[:-7]
    gain_ref, pairing_ref, normed_ref, grads_ref, edge_normed_ref, edge_grads_ref, swapped_gain_ref = refs[-7:]
    dp_ranks = normed_ref.shape[0] // 2
    channels = gain_ref.shape[1]
    masks = chip_masks(2 * (len(arrived) + 1), core)
    seq_ranks = 2 * len(masks) // dp_ranks
    positions = home_ref.shape[0] - HALO
    two = 2 * LANES
    swap = swap_map(pairing_ref[...])
    blocks = [(0, home_ref, 0, channels)]
    blocks += [(mask, ref, two, two + channels) for mask, ref in zip(masks[1:], arrived)]
    blocks += [(mask | core, crossed_ref.at[m], two, 0) for m, mask in enumerate(masks)]
    for flip, ref, lane, grad_lane in blocks:
        source = lax.bitwise_xor(rank_ref[0], flip)
        b, i = lax.rem(source, dp_ranks), lax.div(source, dp_ranks)
        start = pl.multiple_of(i * positions, positions)
        side = jnp.where(i == 0, 0, jnp.where(i == seq_ranks - 1, 1, 2))
        both = normalize(ref[:, lane : lane + channels], gain_ref[...], swap)
        for n, normed in enumerate(both):
            first = grad_lane + n * LANES
            grads = (0.5 * ref[:, first : first + LANES].astype(f32)).astype(bf16)
            index = n * dp_ranks + b
            normed_ref[index, pl.ds(start, positions), :] = normed[:positions]
            grads_ref[index, pl.ds(start, positions), :] = grads[:positions]
            edge_normed_ref[side, index] = normed[positions:]
            edge_grads_ref[side, index] = grads[positions:]
    gain = gain_ref[...]
    first = gain.astype(bf16).astype(f32)
    second = (gain - first).astype(bf16).astype(f32)
    third = gain - first - second
    row = lax.broadcasted_iota(jnp.int32, (HALO, channels), 0)
    parts = jnp.where(row == 0, first, jnp.where(row == 1, second, jnp.where(row == 2, third, 0.0)))
    swapped = dot(parts.astype(bf16), swap, ((1,), (0,)))
    swapped_gain_ref[...] = swapped[0:1] + swapped[1:2] + swapped[2:3]


def main_body(sizes, place_ref, near_ref, far_ref, normed_ref, grads_ref, edge_normed_ref, edge_grads_ref, *refs):
    gain_ref, swapped_gain_ref, pairing_ref, sent_ref, own_ref, cross_ref = refs[:6]
    pieces, kernel_ref, shifted, gelus, terms, halves, bent, slopes, total, scaled = refs[6:16]
    out_ref, own, cross, sems = refs[16:]
    seq_blocks, dp_blocks, seq_ranks, dp_ranks = sizes
    rank, me = place_ref[0], place_ref[1]
    owners = seq_blocks * dp_blocks * seq_ranks * dp_ranks
    part, rows = near_ref.shape[2:]
    strands, span, channels = normed_ref.shape
    taps = kernel_ref.shape[0] // LANES
    half = taps // 2
    reach = 2 * half
    wide = bent.shape[0]

    def runs(owner):
        first, last = owner * rows, (owner + 1) * rows
        while first < last:
            tap, channel = divmod(first, channels)
            count = min(last - first, channels - channel)
            yield tap, channel, count, first - owner * rows
            first += count

    for ref, first in ((near_ref, 0), (far_ref, near_ref.shape[0])):
        for j in range(ref.shape[0]):
            pieces[lax.bitwise_xor(me, first + j)] = ref[j]
    kernel_ref[...] = jnp.zeros_like(kernel_ref)
    places = [
        (sb * dp_blocks + db, sr * dp_ranks + dr)
        for sb in range(seq_blocks)
        for sr in range(seq_ranks)
        for db in range(dp_blocks)
        for dr in range(dp_ranks)
    ]
    for owner, (source, piece) in enumerate(places):
        for tap, channel, count, offset in runs(owner):
            kernel_ref[tap * LANES : tap * LANES + part, channel : channel + count] = pieces[
                source, piece, :, offset : offset + count
            ]
    kernel = kernel_ref[...]
    edge_normed = jnp.concatenate([edge_normed_ref[side, s] for side in range(2) for s in range(strands)], 0)
    edge_terms = dot(edge_normed, kernel, ((1,), (1,)))
    for strand in range(strands):
        forward = strand < dp_ranks
        terms[HALO : HALO + span, :] = dot(normed_ref[strand], kernel, ((1,), (1,)))
        halves[HALO : HALO + span, :] = grads_ref[strand].astype(f32)
        for side, start in enumerate((0, HALO + span)):
            first = (side * strands + strand) * HALO
            terms[start : start + HALO, :] = edge_terms[first : first + HALO]
            halves[start : start + HALO, :] = edge_grads_ref[side, strand].astype(f32)
        preact = jnp.zeros((wide, LANES), f32)
        for k in range(taps):
            start = HALO - reach + k if forward else HALO - k
            preact += terms[start : start + wide, k * LANES : (k + 1) * LANES]
        result, slope = gelu_and_slope(preact)
        bent[...] = result
        gelus[strand] = bent[half : half + span, :].astype(bf16)
        slopes[...] = halves[HALO - half : HALO - half + wide, :] * slope
        for k in range(taps):
            start = reach - k if forward else k
            shifted[strand, :, k * LANES : (k + 1) * LANES] = slopes[start : start + span, :].astype(bf16)
    total[...] = dot(
        shifted[...].reshape(strands * span, taps * LANES),
        normed_ref[...].reshape(strands * span, channels),
        ((0,), (0,)),
    )
    gain = jnp.sum(total[...] * kernel.astype(f32), 0, keepdims=True) / gain_ref[...]
    gain_high = gain.astype(bf16).astype(f32)
    row = lax.broadcasted_iota(jnp.int32, (EXTRA, channels), 0)
    extra = jnp.where(row == 0, gain_high, jnp.where(row == 1, gain - gain_high, 0.0))
    own_gain = channels // owners
    for owner in range(owners):
        for tap, channel, count, offset in runs(owner):
            out_ref[owner, :part, offset : offset + count] = total[
                tap * LANES : tap * LANES + part, channel : channel + count
            ].astype(bf16)
        out_ref[owner, part:, :] = jnp.zeros((EXTRA, rows), bf16)
        out_ref[owner, part:, :own_gain] = extra[
            :, owner * own_gain : (owner + 1) * own_gain
        ].astype(bf16)
    copies = [pltpu.make_async_copy(out_ref, sent_ref, sems.at[0])]
    copies[0].start()
    swapped = dot(kernel, swap_map(pairing_ref[...]), ((1,), (0,))).astype(bf16)
    for b in range(dp_ranks):
        scaled[b] = (
            dot(shifted[b], kernel, ((1,), (0,))) * gain_ref[...]
            + dot(shifted[dp_ranks + b], swapped, ((1,), (0,))) * swapped_gain_ref[...]
        ).astype(bf16)
    chips, positions, _ = own.shape
    for c, (out, ref) in enumerate(((cross, cross_ref), (own, own_ref))):
        for m, mask in enumerate(chip_masks(2 * chips, dp_ranks)):
            target = lax.bitwise_xor(rank, mask if c else mask | dp_ranks)
            b = lax.rem(target, dp_ranks)
            start = pl.multiple_of(lax.div(target, dp_ranks) * positions, positions)
            out[m, :, :channels] = scaled[b, pl.ds(start, positions), :]
            for n in range(2):
                lane = channels + n * LANES
                out[m, :, lane : lane + LANES] = gelus[n * dp_ranks + b, pl.ds(start, positions), :]
        copies.append(pltpu.make_async_copy(out, ref, sems.at[1 + c]))
        copies[-1].start()
    for copy in copies:
        copy.wait()


def chip_sum(part, own_ref, crossed_ref, *outs):
    channels = own_ref.shape[2] - 2 * LANES
    for m, out in enumerate(outs):
        out[:, :channels] = (
            own_ref[m, :, :channels].astype(f32) + crossed_ref[m, :, :channels].astype(f32)
        ).astype(bf16)
        for c, ref in enumerate((own_ref, crossed_ref)):
            for n in range(2):
                lane = channels + n * LANES
                start = channels + (2 * c + n) * part
                out[:, start : start + part] = ref[m, :, lane : lane + part]


def finish(part, core, rank_ref, values_ref, cot_ref, pairing_ref, *refs):
    arrived, (combined_ref, grad_ref, gelus) = refs[:-3], refs[-3:]
    channels = values_ref.shape[1]
    ranks = gelus.shape[1]
    gelus[...] = jnp.zeros_like(gelus)
    scaled = jnp.zeros(values_ref.shape, f32)
    for mask, block in zip(chip_masks(ranks, core), arrived):
        scaled += block[:, :channels].astype(f32)
        for c in range(2):
            source = lax.bitwise_xor(rank_ref[0], mask | c * core)
            for n in range(2):
                start = channels + (2 * c + n) * part
                gelus[n, source, :, :part] = block[:, start : start + part]
    joined = [jnp.concatenate([gelus[n, j] for j in range(ranks)], -1) for n in range(2)]
    maps = slot_maps(part, ranks * LANES, pairing_ref[...])
    plain, other = [dot(j, m, ((1,), (0,))) for j, m in zip(joined, maps)]
    values = values_ref[...].astype(f32)
    rms = lax.rsqrt(jnp.mean(values * values, -1, keepdims=True) + epsilon)
    reverse_out = (values + other).astype(bf16).astype(f32)
    combined_ref[...] = (0.5 * (values + plain + reverse_out)).astype(bf16)
    along = jnp.mean(scaled * values, -1, keepdims=True)
    grad_ref[...] = (cot_ref[...].astype(f32) + rms * scaled - values * (rms * rms * rms * along)).astype(bf16)


def collect(owner_of, terms_ref, kernel_ref, gain_ref, joined):
    _, height, rows = terms_ref.shape
    part = height - EXTRA
    joined[...] = jnp.zeros_like(joined)
    gain = jnp.zeros((1, rows), f32)
    for rank, owners in enumerate(owner_of):
        total = terms_ref[owners[0]].astype(f32)
        for owner in owners[1:]:
            total += terms_ref[owner].astype(f32)
        joined[rank * part : (rank + 1) * part, :rows] = total[:part]
        gain += total[part : part + 1] + total[part + 1 : part + 2]
    kernel_ref[...] = joined[...].T[:rows]
    gain_ref[...] = gain[:, : gain_ref.shape[1]]


def flipped_pairs(count, mask):
    return [(i, i ^ mask) for i in range(count)]


def per_device(activations, cotangent, weights, norm_gain, pairing):
    seq_ranks = lax.axis_size("seq_rank")
    dp_ranks = lax.axis_size("dp_rank")
    seq_blocks = lax.axis_size("seq_block")
    dp_blocks = lax.axis_size("dp_block")
    ranks = seq_ranks * dp_ranks
    owners = ranks * seq_blocks * dp_blocks
    positions, channels = activations.shape[1:]
    rows = weights.shape[0]
    taps = rows * owners // channels
    part = channels // ranks
    span = positions * seq_ranks
    long = span + 2 * HALO
    reach = taps - taps % 2
    wide = -(-(span + reach) // 8) * 8
    strands = 2 * dp_ranks
    width = channels + 2 * LANES
    rank = lax.axis_index(RANK).reshape(1)
    place = jnp.concatenate([rank, lax.axis_index(BLOCK).reshape(1)])
    values, cot = activations[0], cotangent[0]
    slices = lax.all_to_all(weights.T.reshape(ranks, part, rows), RANK, 0, 0, tiled=True)
    far = slices[None]
    stages = [1 << bit for bit in range((seq_blocks * dp_blocks).bit_length() - 1)]
    for mask in stages:
        near = far if mask == 1 else jnp.concatenate([near, far])
        far = lax.ppermute(near, BLOCK, flipped_pairs(seq_blocks * dp_blocks, mask))
    along = ("seq_block", "seq_rank")
    ends = [(b * seq_ranks - 1, b * seq_ranks) for b in range(1, seq_blocks)]
    both = jnp.concatenate([values, cot], -1)
    low = lax.ppermute(both[-HALO:], along, ends)
    high = lax.ppermute(both[:HALO], along, [(target, source) for source, target in ends])
    pairing = pairing.reshape(1, channels)
    gain = norm_gain.reshape(1, channels)
    core = dp_ranks
    masks = chip_masks(ranks, core)
    block = positions + HALO
    home, cross, *leaving = called(
        lambda *refs: pack_messages(part, core, *refs),
        (shape_of((block, width), bf16),) * 2
        + tuple(shape_of((block, width + 2 * LANES), bf16) for _ in masks[1:]),
        (rank, values, cot, low + high, pairing),
        16,
        scratch=[pltpu.VMEM((ranks, block, 2 * LANES), bf16)],
        specs=[SMEM] + [VMEM] * 4,
    )
    arrived = [
        lax.ppermute(message, RANK, flipped_pairs(ranks, mask))
        for message, mask in zip(leaving, masks[1:])
    ]
    far, cross = lax.optimization_barrier((far, cross))
    crossing = called(
        stack_crossing, shape_of((len(masks), block, width), bf16), (cross, *arrived), 8
    )
    crossed = lax.ppermute(crossing, RANK, flipped_pairs(ranks, core))
    normed, grads, edge_normed, edge_grads, swapped_gain = called(
        lambda *refs: prepare(core, *refs),
        (
            shape_of((strands, span, channels), bf16),
            shape_of((strands, span, LANES), bf16),
            shape_of((3, strands, HALO, channels), bf16),
            shape_of((3, strands, HALO, LANES), bf16),
            shape_of((1, channels), f32),
        ),
        (rank, home, crossed, *arrived, gain, pairing),
        16,
        specs=[SMEM] + [VMEM] * (4 + len(arrived)),
        flops=2 * ranks * positions * channels * channels,
        moved=ranks * positions * (width + 2 * channels) * 2,
    )
    sent = (owners, part + EXTRA, rows)
    halves = (len(masks), positions, width)
    sizes = (seq_blocks, dp_blocks, seq_ranks, dp_ranks)
    outgoing, own, cross = called(
        lambda *refs: main_body(sizes, *refs),
        tuple(pltpu.HBM(shape, bf16) for shape in (sent, halves, halves)),
        (place, near, far, normed, grads, edge_normed, edge_grads, gain, swapped_gain, pairing),
        40,
        scratch=[
            pltpu.VMEM((seq_blocks * dp_blocks, ranks, part, rows), bf16),
            pltpu.VMEM((taps * LANES, channels), bf16),
            pltpu.VMEM((strands, span, taps * LANES), bf16),
            pltpu.VMEM((strands, span, LANES), bf16),
            pltpu.VMEM((long, taps * LANES), f32),
            pltpu.VMEM((long, LANES), f32),
            pltpu.VMEM((wide, LANES), f32),
            pltpu.VMEM((wide, LANES), f32),
            pltpu.VMEM((taps * LANES, channels), f32),
            pltpu.VMEM((dp_ranks, span, channels), bf16),
            pltpu.VMEM(sent, bf16),
            pltpu.VMEM(halves, bf16),
            pltpu.VMEM(halves, bf16),
            pltpu.SemaphoreType.DMA((3,)),
        ],
        specs=[SMEM] + [VMEM] * 9,
        out_specs=(HBM,) * 3,
        flops=6 * strands * span * taps * LANES * channels,
    )
    terms = lax.all_to_all(outgoing, EVERY, 0, 0, tiled=True)
    crossed = lax.ppermute(cross, RANK, flipped_pairs(ranks, core))
    leaving = called(
        lambda *refs: chip_sum(part, *refs),
        tuple(shape_of((positions, channels + 4 * part), bf16) for _ in masks),
        (own, crossed),
        8,
    )
    arrived = leaving[:1] + tuple(
        lax.ppermute(message, RANK, flipped_pairs(ranks, mask))
        for message, mask in zip(leaving[1:], masks[1:])
    )
    combined, grad_input = called(
        lambda *refs: finish(part, core, *refs),
        (shape_of((positions, channels), bf16), shape_of((positions, channels), bf16)),
        (rank, values, cot, pairing, *arrived),
        16,
        scratch=[pltpu.VMEM((2, ranks, positions, LANES), bf16)],
        specs=[SMEM] + [VMEM] * (3 + len(arrived)),
    )
    order = [
        [
            ((sb * seq_ranks + sr) * dp_blocks + db) * dp_ranks + dr
            for sb in range(seq_blocks)
            for db in range(dp_blocks)
        ]
        for sr in range(seq_ranks)
        for dr in range(dp_ranks)
    ]
    grad_kernel, grad_gain = called(
        lambda *refs: collect(order, *refs),
        (shape_of((rows, channels), f32), shape_of((1, channels // owners), f32)),
        (terms,),
        16,
        scratch=[pltpu.VMEM((channels, -(-rows // LANES) * LANES), f32)],
    )
    return combined[None], grad_input[None], grad_kernel, grad_gain[0]


def solution(mesh):
    seq, dp = mesh.shape["seq"], mesh.shape["dp"]
    seq_ranks, dp_ranks = 4, 2
    grouped = Mesh(mesh.devices.reshape(seq // seq_ranks, seq_ranks, dp // dp_ranks, dp_ranks), EVERY)
    along = P(("dp_block", "dp_rank"), ("seq_block", "seq_rank"), None)
    return jax.shard_map(
        per_device,
        mesh=grouped,
        in_specs=(along, along, P(EVERY, None), P(), P()),
        out_specs=(along, along, P(EVERY, None), P(EVERY)),
        check_vma=False,
    )
```

```python
import jax
import jax.numpy as jnp
from jax import lax
from jax.experimental import pallas as pl
from jax.experimental.pallas import tpu as pltpu
from jax.sharding import Mesh, PartitionSpec as P

epsilon = 1e-06
RANK = ("seq_rank", "dp_rank")
BLOCK = ("seq_block", "dp_block")
EVERY = ("seq_block", "seq_rank", "dp_block", "dp_rank")
LANES = 128
HALO = 16
EXTRA = 16
VMEM = pl.BlockSpec(memory_space=pltpu.VMEM)
SMEM = pl.BlockSpec(memory_space=pltpu.SMEM)
HBM = pl.BlockSpec(memory_space=pltpu.HBM)
bf16 = jnp.bfloat16
f32 = jnp.float32


def called(body, outs, args, vmem, scratch=(), specs=None, out_specs=None):
    return pl.pallas_call(
        body,
        out_shape=outs,
        in_specs=specs or [VMEM] * len(args),
        out_specs=out_specs or jax.tree.map(lambda _: VMEM, outs),
        scratch_shapes=list(scratch),
        compiler_params=pltpu.CompilerParams(vmem_limit_bytes=vmem * 2**20),
        cost_estimate=pl.CostEstimate(flops=0, bytes_accessed=0, transcendentals=0),
    )(*args)


def shape_of(shape, dtype):
    return jax.ShapeDtypeStruct(shape, dtype)


def dot(a, b, contract):
    return lax.dot_general(a, b, (contract, ((), ())), preferred_element_type=f32)


def gelu_and_slope(x):
    inner = 0.7978845608028654 * (x + 0.044715 * (x * x * x))
    bend = jnp.tanh(inner)
    half_sum = 0.5 * (1.0 + bend)
    slope = half_sum + (0.5 * x) * (1.0 - bend * bend) * (
        0.7978845608028654 * (1.0 + 0.134145 * (x * x))
    )
    return x * half_sum, slope


def slot_maps(part, slots, pairing):
    shape = (slots, pairing.shape[1])
    slot = lax.broadcasted_iota(jnp.int32, shape, 0)
    lane = lax.bitwise_and(slot, LANES - 1)
    channel_of = jnp.where(lane < part, lax.div(slot, LANES) * part + lane, -1)
    channel = lax.broadcasted_iota(jnp.int32, shape, 1)
    return [jnp.where(channel_of == c, 1.0, 0.0).astype(bf16) for c in (channel, pairing)]


def swap_map(pairing):
    channels = pairing.shape[1]
    row = lax.broadcasted_iota(jnp.int32, (channels, channels), 0)
    return jnp.where(row == pairing, 1.0, 0.0).astype(bf16)


def chip_masks(ranks, core):
    return [mask for mask in range(ranks) if not mask & core]


def pack_messages(part, core, rank_ref, values_ref, cot_ref, edge_ref, pairing_ref, *refs):
    home_ref, cross_ref, leaving, slices = refs[0], refs[1], refs[2:-1], refs[-1]
    positions, channels = values_ref.shape
    ranks = slices.shape[0]
    here, edge = slice(0, positions), slice(positions, None)
    for n, map_of in enumerate(slot_maps(part, ranks * LANES, pairing_ref[...])):
        for rows, source in ((here, cot_ref[...]), (edge, edge_ref[:, channels:])):
            piece = dot(source, map_of, ((1,), (1,))).astype(bf16)
            for j in range(ranks):
                slices[j, rows, n * LANES : (n + 1) * LANES] = piece[:, j * LANES : (j + 1) * LANES]
    rank = rank_ref[0]
    two = 2 * LANES
    starts = [(home_ref, 0), (cross_ref, two)] + [(out, two) for out in leaving]
    for out, start in starts:
        out[here, start : start + channels] = values_ref[...]
        out[edge, start : start + channels] = edge_ref[:, :channels]
    home_ref[:, channels:] = slices[rank]
    cross_ref[:, :two] = slices[lax.bitwise_xor(rank, core)]
    for mask, out in zip(chip_masks(ranks, core)[1:], leaving):
        out[:, :two] = slices[lax.bitwise_xor(rank, mask | core)]
        out[:, two + channels :] = slices[lax.bitwise_xor(rank, mask)]


def stack_crossing(cross_ref, *refs):
    out_ref = refs[-1]
    width = out_ref.shape[2]
    for m, ref in enumerate((cross_ref,) + refs[:-1]):
        out_ref[m] = ref[:, :width]


def normalize(x, gain, swap):
    other = dot(x, swap, ((1,), (0,)))
    x = x.astype(f32)
    rms = lax.rsqrt(jnp.mean(x * x, -1, keepdims=True) + epsilon)
    return [(t * rms * gain).astype(bf16) for t in (x, other)]


def prepare(core, rank_ref, home_ref, crossed_ref, *refs):
    arrived = refs[:-7]
    gain_ref, pairing_ref, normed_ref, grads_ref, edge_normed_ref, edge_grads_ref, swapped_gain_ref = refs[-7:]
    dp_ranks = normed_ref.shape[0] // 2
    channels = gain_ref.shape[1]
    masks = chip_masks(2 * (len(arrived) + 1), core)
    seq_ranks = 2 * len(masks) // dp_ranks
    positions = home_ref.shape[0] - HALO
    two = 2 * LANES
    swap = swap_map(pairing_ref[...])
    blocks = [(0, home_ref, 0, channels)]
    blocks += [(mask, ref, two, two + channels) for mask, ref in zip(masks[1:], arrived)]
    blocks += [(mask | core, crossed_ref.at[m], two, 0) for m, mask in enumerate(masks)]
    for flip, ref, lane, grad_lane in blocks:
        source = lax.bitwise_xor(rank_ref[0], flip)
        b, i = lax.rem(source, dp_ranks), lax.div(source, dp_ranks)
        start = pl.multiple_of(i * positions, positions)
        side = jnp.where(i == 0, 0, jnp.where(i == seq_ranks - 1, 1, 2))
        both = normalize(ref[:, lane : lane + channels], gain_ref[...], swap)
        for n, normed in enumerate(both):
            first = grad_lane + n * LANES
            grads = (0.5 * ref[:, first : first + LANES].astype(f32)).astype(bf16)
            index = n * dp_ranks + b
            normed_ref[index, pl.ds(start, positions), :] = normed[:positions]
            grads_ref[index, pl.ds(start, positions), :] = grads[:positions]
            edge_normed_ref[side, index] = normed[positions:]
            edge_grads_ref[side, index] = grads[positions:]
    gain = gain_ref[...]
    first = gain.astype(bf16).astype(f32)
    second = (gain - first).astype(bf16).astype(f32)
    third = gain - first - second
    row = lax.broadcasted_iota(jnp.int32, (HALO, channels), 0)
    parts = jnp.where(row == 0, first, jnp.where(row == 1, second, jnp.where(row == 2, third, 0.0)))
    swapped = dot(parts.astype(bf16), swap, ((1,), (0,)))
    swapped_gain_ref[...] = swapped[0:1] + swapped[1:2] + swapped[2:3]


def main_body(sizes, place_ref, near_ref, far_ref, normed_ref, grads_ref, edge_normed_ref, edge_grads_ref, *refs):
    seq_blocks, dp_blocks, seq_ranks, dp_ranks = sizes
    blocks = seq_blocks * dp_blocks
    gain_ref, shifted_out, kernel_out, gelu_out, leaving_out = refs[:5]
    pieces, padded, terms, halves, bent, slopes, total, shifted_ref, kernel_ref, gelu_ref, leaving, sems = refs[5:]
    copies = []

    def send(source, target):
        copies.append(pltpu.make_async_copy(source, target, sems.at[len(copies)]))
        copies[-1].start()

    me = place_ref[1]
    part, rows = near_ref.shape[2:]
    strands, span, channels = normed_ref.shape
    taps = kernel_ref.shape[0] // part
    half = taps // 2
    reach = 2 * half
    wide = bent.shape[0]

    def runs(owner):
        first, last = owner * rows, (owner + 1) * rows
        while first < last:
            tap, channel = divmod(first, channels)
            count = min(last - first, channels - channel)
            yield tap, channel, count, first - owner * rows
            first += count

    for ref, first in ((near_ref, 0), (far_ref, near_ref.shape[0])):
        for j in range(ref.shape[0]):
            pieces[lax.bitwise_xor(me, first + j)] = ref[j]
    places = [
        (sb * dp_blocks + db, sr * dp_ranks + dr)
        for sb in range(seq_blocks)
        for sr in range(seq_ranks)
        for db in range(dp_blocks)
        for dr in range(dp_ranks)
    ]
    for owner, (source, piece) in enumerate(places):
        for tap, channel, count, offset in runs(owner):
            kernel_ref[tap * part : (tap + 1) * part, channel : channel + count] = pieces[
                source, piece, :, offset : offset + count
            ]
    send(kernel_ref, kernel_out)
    padded[...] = jnp.zeros_like(padded)
    for k in range(taps):
        padded[k * LANES : k * LANES + part, :] = kernel_ref[k * part : (k + 1) * part, :]
    kernel = padded[...]
    edge_normed = jnp.concatenate([edge_normed_ref[side, s] for side in range(2) for s in range(strands)], 0)
    edge_terms = dot(edge_normed, kernel, ((1,), (1,)))
    for strand in range(strands):
        forward = strand < dp_ranks
        terms[HALO : HALO + span, :] = dot(normed_ref[strand], kernel, ((1,), (1,)))
        halves[HALO : HALO + span, :] = grads_ref[strand].astype(f32)
        for side, start in enumerate((0, HALO + span)):
            first = (side * strands + strand) * HALO
            terms[start : start + HALO, :] = edge_terms[first : first + HALO]
            halves[start : start + HALO, :] = edge_grads_ref[side, strand].astype(f32)
        preact = jnp.zeros((wide, LANES), f32)
        for k in range(taps):
            start = HALO - reach + k if forward else HALO - k
            preact += terms[start : start + wide, k * LANES : (k + 1) * LANES]
        result, slope = gelu_and_slope(preact)
        bent[...] = result
        gelu_ref[strand] = bent[half : half + span, :].astype(bf16)
        slopes[...] = halves[HALO - half : HALO - half + wide, :] * slope
        for k in range(taps):
            start = reach - k if forward else k
            shifted_ref[strand, :, k * part : (k + 1) * part] = slopes[start : start + span, :part].astype(bf16)
        send(shifted_ref.at[strand], shifted_out.at[strand])
    send(gelu_ref, gelu_out)
    total[...] = dot(
        shifted_ref[...].reshape(strands * span, taps * part),
        normed_ref[...].reshape(strands * span, channels),
        ((0,), (0,)),
    )
    gain = jnp.sum(total[...] * kernel_ref[...].astype(f32), 0, keepdims=True) / gain_ref[...]
    gain_high = gain.astype(bf16).astype(f32)
    row = lax.broadcasted_iota(jnp.int32, (EXTRA, channels), 0)
    extra = jnp.where(row == 0, gain_high, jnp.where(row == 1, gain - gain_high, 0.0))
    own_gain = channels // len(places)
    for owner in range(len(places)):
        for tap, channel, count, offset in runs(owner):
            leaving[owner, :part, offset : offset + count] = total[
                tap * part : (tap + 1) * part, channel : channel + count
            ].astype(bf16)
        leaving[owner, part:, :] = jnp.zeros((EXTRA, rows), bf16)
        leaving[owner, part:, :own_gain] = extra[
            :, owner * own_gain : (owner + 1) * own_gain
        ].astype(bf16)
    send(leaving, leaving_out)
    for copy in copies:
        copy.wait()


def input_gradient(
    place_ref, shifted_ref, kernel_ref, gelu_ref, gain_ref, swapped_gain_ref, pairing_ref, own_ref, cross_ref, *scratch
):
    scaled, shifted, kernel_in, gelus, sems = scratch
    strands = shifted_ref.shape[0]
    moves = [(kernel_ref, kernel_in)]
    moves += [(shifted_ref.at[n], shifted.at[n]) for n in range(strands)]
    moves += [(gelu_ref, gelus)]
    copies = [pltpu.make_async_copy(*move, sems.at[n]) for n, move in enumerate(moves)]
    for copy in copies:
        copy.start()
    dp_ranks = strands // 2
    chips, positions, _ = own_ref.shape
    channels = gain_ref.shape[1]
    copies[0].wait()
    kernel = kernel_in[...]
    swapped = dot(kernel, swap_map(pairing_ref[...]), ((1,), (0,))).astype(bf16)
    for copy in copies[1:]:
        copy.wait()
    for b in range(dp_ranks):
        scaled[b] = (
            dot(shifted[b], kernel, ((1,), (0,))) * gain_ref[...]
            + dot(shifted[dp_ranks + b], swapped, ((1,), (0,))) * swapped_gain_ref[...]
        ).astype(bf16)
    for m, mask in enumerate(chip_masks(2 * chips, dp_ranks)):
        for out, flip in ((own_ref, mask), (cross_ref, mask | dp_ranks)):
            target = lax.bitwise_xor(place_ref[0], flip)
            b = lax.rem(target, dp_ranks)
            start = pl.multiple_of(lax.div(target, dp_ranks) * positions, positions)
            out[m, :, :channels] = scaled[b, pl.ds(start, positions), :]
            for n in range(2):
                lane = channels + n * LANES
                out[m, :, lane : lane + LANES] = gelus[n * dp_ranks + b, pl.ds(start, positions), :]


def chip_sum(part, own_ref, crossed_ref, *outs):
    channels = own_ref.shape[2] - 2 * LANES
    for m, out in enumerate(outs):
        out[:, :channels] = (
            own_ref[m, :, :channels].astype(f32) + crossed_ref[m, :, :channels].astype(f32)
        ).astype(bf16)
        for c, ref in enumerate((own_ref, crossed_ref)):
            for n in range(2):
                lane = channels + n * LANES
                start = channels + (2 * c + n) * part
                out[:, start : start + part] = ref[m, :, lane : lane + part]


def finish(part, core, rank_ref, values_ref, cot_ref, pairing_ref, *refs):
    arrived, (combined_ref, grad_ref, gelus) = refs[:-3], refs[-3:]
    channels = values_ref.shape[1]
    ranks = gelus.shape[1]
    gelus[...] = jnp.zeros_like(gelus)
    scaled = jnp.zeros(values_ref.shape, f32)
    for mask, block in zip(chip_masks(ranks, core), arrived):
        scaled += block[:, :channels].astype(f32)
        for c in range(2):
            source = lax.bitwise_xor(rank_ref[0], mask | c * core)
            for n in range(2):
                start = channels + (2 * c + n) * part
                gelus[n, source, :, :part] = block[:, start : start + part]
    joined = [jnp.concatenate([gelus[n, j] for j in range(ranks)], -1) for n in range(2)]
    maps = slot_maps(part, ranks * LANES, pairing_ref[...])
    plain, other = [dot(j, m, ((1,), (0,))) for j, m in zip(joined, maps)]
    values = values_ref[...].astype(f32)
    rms = lax.rsqrt(jnp.mean(values * values, -1, keepdims=True) + epsilon)
    reverse_out = (values + other).astype(bf16).astype(f32)
    combined_ref[...] = (0.5 * (values + plain + reverse_out)).astype(bf16)
    along = jnp.mean(scaled * values, -1, keepdims=True)
    grad_ref[...] = (cot_ref[...].astype(f32) + rms * scaled - values * (rms * rms * rms * along)).astype(bf16)


def collect(owner_of, terms_ref, kernel_ref, gain_ref, joined):
    _, height, rows = terms_ref.shape
    part = height - EXTRA
    joined[...] = jnp.zeros_like(joined)
    gain = jnp.zeros((1, rows), f32)
    for rank, owners in enumerate(owner_of):
        total = terms_ref[owners[0]].astype(f32)
        for owner in owners[1:]:
            total += terms_ref[owner].astype(f32)
        joined[rank * part : (rank + 1) * part, :rows] = total[:part]
        gain += total[part : part + 1] + total[part + 1 : part + 2]
    kernel_ref[...] = joined[...].T[:rows]
    gain_ref[...] = gain[:, : gain_ref.shape[1]]


def flipped_pairs(count, mask):
    return [(i, i ^ mask) for i in range(count)]


def per_device(activations, cotangent, weights, norm_gain, pairing):
    seq_ranks = lax.axis_size("seq_rank")
    dp_ranks = lax.axis_size("dp_rank")
    seq_blocks = lax.axis_size("seq_block")
    dp_blocks = lax.axis_size("dp_block")
    ranks = seq_ranks * dp_ranks
    owners = ranks * seq_blocks * dp_blocks
    positions, channels = activations.shape[1:]
    rows = weights.shape[0]
    taps = rows * owners // channels
    part = channels // ranks
    span = positions * seq_ranks
    long = span + 2 * HALO
    reach = taps - taps % 2
    wide = -(-(span + reach) // 8) * 8
    strands = 2 * dp_ranks
    width = channels + 2 * LANES
    rank = lax.axis_index(RANK).reshape(1)
    place = jnp.concatenate([rank, lax.axis_index(BLOCK).reshape(1)])
    values, cot = activations[0], cotangent[0]
    along = ("seq_block", "seq_rank")
    ends = [(b * seq_ranks - 1, b * seq_ranks) for b in range(1, seq_blocks)]
    both = jnp.concatenate([values, cot], -1)
    edge = jnp.where(lax.axis_index("seq_rank") == 0, both[:HALO], both[-HALO:])
    edge = lax.ppermute(edge, along, ends + [(target, source) for source, target in ends])
    edge, weights = lax.optimization_barrier((edge, weights))
    blocks = seq_blocks * dp_blocks
    slices = lax.all_to_all(weights.T.reshape(ranks, part, rows), RANK, 0, 0, tiled=True)
    far = slices[None]
    stages = [1 << bit for bit in range(blocks.bit_length() - 1)]
    for mask in stages[:-1]:
        near = far if mask == 1 else jnp.concatenate([near, far])
        far = lax.ppermute(near, BLOCK, flipped_pairs(blocks, mask))
    near = jnp.concatenate([near, far])
    pairing = pairing.reshape(1, channels)
    gain = norm_gain.reshape(1, channels)
    core = dp_ranks
    masks = chip_masks(ranks, core)
    block = positions + HALO
    home, cross, *leaving = called(
        lambda *refs: pack_messages(part, core, *refs),
        (shape_of((block, width), bf16),) * 2
        + tuple(shape_of((block, width + 2 * LANES), bf16) for _ in masks[1:]),
        (rank, values, cot, edge, pairing),
        16,
        scratch=[pltpu.VMEM((ranks, block, 2 * LANES), bf16)],
        specs=[SMEM] + [VMEM] * 4,
    )
    arrived = [
        lax.ppermute(message, RANK, flipped_pairs(ranks, mask))
        for message, mask in zip(leaving, masks[1:])
    ]
    far = lax.ppermute(near, BLOCK, flipped_pairs(blocks, stages[-1]))
    far, cross = lax.optimization_barrier((far, cross))
    crossing = called(
        stack_crossing, shape_of((len(masks), block, width), bf16), (cross, *arrived), 8
    )
    crossed = lax.ppermute(crossing, RANK, flipped_pairs(ranks, core))
    normed, grads, edge_normed, edge_grads, swapped_gain = called(
        lambda *refs: prepare(core, *refs),
        (
            shape_of((strands, span, channels), bf16),
            shape_of((strands, span, LANES), bf16),
            shape_of((3, strands, HALO, channels), bf16),
            shape_of((3, strands, HALO, LANES), bf16),
            shape_of((1, channels), f32),
        ),
        (rank, home, crossed, *arrived, gain, pairing),
        16,
        specs=[SMEM] + [VMEM] * (4 + len(arrived)),
    )
    sizes = (seq_blocks, dp_blocks, seq_ranks, dp_ranks)
    shapes = (
        (strands, span, taps * part),
        (taps * part, channels),
        (strands, span, LANES),
        (owners, part + EXTRA, rows),
    )
    shifted, kernel, gelus, outgoing = called(
        lambda *refs: main_body(sizes, *refs),
        tuple(pltpu.HBM(shape, bf16) for shape in shapes),
        (place, near, far, normed, grads, edge_normed, edge_grads, gain),
        40,
        scratch=[
            pltpu.VMEM((blocks, ranks, part, rows), bf16),
            pltpu.VMEM((taps * LANES, channels), bf16),
            pltpu.VMEM((long, taps * LANES), f32),
            pltpu.VMEM((long, LANES), f32),
            pltpu.VMEM((wide, LANES), f32),
            pltpu.VMEM((wide, LANES), f32),
            pltpu.VMEM((taps * part, channels), f32),
        ]
        + [pltpu.VMEM(shape, bf16) for shape in shapes]
        + [pltpu.SemaphoreType.DMA((strands + 3,))],
        specs=[SMEM] + [VMEM] * 7,
        out_specs=(HBM,) * 4,
    )
    terms = lax.all_to_all(outgoing, EVERY, 0, 0, tiled=True)
    halves = shape_of((len(masks), positions, width), bf16)
    kept = [pltpu.with_memory_space_constraint(x, pltpu.HBM) for x in (shifted, kernel, gelus)]
    own, cross = called(
        input_gradient,
        (halves, halves),
        (place, *kept, gain, swapped_gain, pairing),
        24,
        scratch=[pltpu.VMEM((dp_ranks, span, channels), bf16)]
        + [pltpu.VMEM(shape, bf16) for shape in shapes[:3]]
        + [pltpu.SemaphoreType.DMA((strands + 2,))],
        specs=[SMEM] + [HBM] * 3 + [VMEM] * 3,
    )
    crossed = lax.ppermute(cross, RANK, flipped_pairs(ranks, core))
    leaving = called(
        lambda *refs: chip_sum(part, *refs),
        tuple(shape_of((positions, channels + 4 * part), bf16) for _ in masks),
        (own, crossed),
        8,
    )
    arrived = leaving[:1] + tuple(
        lax.ppermute(message, RANK, flipped_pairs(ranks, mask))
        for message, mask in zip(leaving[1:], masks[1:])
    )
    combined, grad_input = called(
        lambda *refs: finish(part, core, *refs),
        (shape_of((positions, channels), bf16), shape_of((positions, channels), bf16)),
        (rank, values, cot, pairing, *arrived),
        16,
        scratch=[pltpu.VMEM((2, ranks, positions, LANES), bf16)],
        specs=[SMEM] + [VMEM] * (3 + len(arrived)),
    )
    order = [
        [
            ((sb * seq_ranks + sr) * dp_blocks + db) * dp_ranks + dr
            for sb in range(seq_blocks)
            for db in range(dp_blocks)
        ]
        for sr in range(seq_ranks)
        for dr in range(dp_ranks)
    ]
    grad_kernel, grad_gain = called(
        lambda *refs: collect(order, *refs),
        (shape_of((rows, channels), f32), shape_of((1, channels // owners), f32)),
        (terms,),
        16,
        scratch=[pltpu.VMEM((channels, -(-rows // LANES) * LANES), f32)],
    )
    return combined[None], grad_input[None], grad_kernel, grad_gain[0]


def solution(mesh):
    seq, dp = mesh.shape["seq"], mesh.shape["dp"]
    seq_ranks, dp_ranks = 4, 2
    grouped = Mesh(mesh.devices.reshape(seq // seq_ranks, seq_ranks, dp // dp_ranks, dp_ranks), EVERY)
    along = P(("dp_block", "dp_rank"), ("seq_block", "seq_rank"), None)
    return jax.shard_map(
        per_device,
        mesh=grouped,
        in_specs=(along, along, P(EVERY, None), P(), P()),
        out_specs=(along, along, P(EVERY, None), P(EVERY)),
        check_vma=False,
    )
```

```python
import jax
import jax.numpy as jnp
from jax import lax
from jax.experimental import pallas as pl
from jax.experimental.pallas import tpu as pltpu
from jax.sharding import Mesh, PartitionSpec as P

epsilon = 1e-06
RANK = ("seq_rank", "dp_rank")
BLOCK = ("seq_block", "dp_block")
EVERY = ("seq_block", "seq_rank", "dp_block", "dp_rank")
LANES = 128
HALO = 16
EXTRA = 16
VMEM = pl.BlockSpec(memory_space=pltpu.VMEM)
SMEM = pl.BlockSpec(memory_space=pltpu.SMEM)
HBM = pl.BlockSpec(memory_space=pltpu.HBM)
bf16 = jnp.bfloat16
f32 = jnp.float32


def called(body, outs, args, vmem, scratch=(), specs=None, out_specs=None):
    return pl.pallas_call(
        body,
        out_shape=outs,
        in_specs=specs or [VMEM] * len(args),
        out_specs=out_specs or jax.tree.map(lambda _: VMEM, outs),
        scratch_shapes=list(scratch),
        compiler_params=pltpu.CompilerParams(vmem_limit_bytes=vmem * 2**20),
        cost_estimate=pl.CostEstimate(flops=0, bytes_accessed=0, transcendentals=0),
    )(*args)


def shape_of(shape, dtype):
    return jax.ShapeDtypeStruct(shape, dtype)


def dot(a, b, contract):
    return lax.dot_general(a, b, (contract, ((), ())), preferred_element_type=f32)


def gelu_and_slope(x):
    inner = 0.7978845608028654 * (x + 0.044715 * (x * x * x))
    bend = jnp.tanh(inner)
    half_sum = 0.5 * (1.0 + bend)
    slope = half_sum + (0.5 * x) * (1.0 - bend * bend) * (
        0.7978845608028654 * (1.0 + 0.134145 * (x * x))
    )
    return x * half_sum, slope


def slot_maps(part, slots, pairing):
    shape = (slots, pairing.shape[1])
    slot = lax.broadcasted_iota(jnp.int32, shape, 0)
    lane = lax.bitwise_and(slot, LANES - 1)
    channel_of = jnp.where(lane < part, lax.div(slot, LANES) * part + lane, -1)
    channel = lax.broadcasted_iota(jnp.int32, shape, 1)
    return [jnp.where(channel_of == c, 1.0, 0.0).astype(bf16) for c in (channel, pairing)]


def swap_map(pairing):
    channels = pairing.shape[1]
    row = lax.broadcasted_iota(jnp.int32, (channels, channels), 0)
    return jnp.where(row == pairing, 1.0, 0.0).astype(bf16)


def chip_masks(ranks, core):
    return [mask for mask in range(ranks) if not mask & core]


class Moves:
    def __init__(self, sems):
        self.sems, self.copies = sems, []

    def start(self, source, target):
        copy = pltpu.make_async_copy(source, target, self.sems.at[len(self.copies)])
        copy.start()
        self.copies.append(copy)
        return copy

    def wait(self):
        for copy in self.copies:
            copy.wait()


def spread(piece_of, weights_ref, out_ref, square, sent, sems):
    rows, channels = weights_ref.shape
    part = out_ref.shape[1]
    square[...] = jnp.zeros_like(square)
    square[:rows] = weights_ref[...].astype(f32)
    turned = square[...].T.astype(bf16)
    for owner, piece in enumerate(piece_of):
        sent[owner] = turned[piece * part : (piece + 1) * part, :rows]
    moves = Moves(sems)
    moves.start(sent, out_ref)
    moves.wait()


def pack_messages(part, core, rank_ref, values_ref, cot_ref, edge_ref, pairing_ref, *refs):
    home_ref, cross_ref, leaving, slices = refs[0], refs[1], refs[2:-1], refs[-1]
    positions, channels = values_ref.shape
    ranks = slices.shape[0]
    here, edge = slice(0, positions), slice(positions, None)
    for n, map_of in enumerate(slot_maps(part, ranks * LANES, pairing_ref[...])):
        for rows, source in ((here, cot_ref[...]), (edge, edge_ref[:, channels:])):
            piece = dot(source, map_of, ((1,), (1,))).astype(bf16)
            for j in range(ranks):
                slices[j, rows, n * LANES : (n + 1) * LANES] = piece[:, j * LANES : (j + 1) * LANES]
    rank = rank_ref[0]
    two = 2 * LANES
    starts = [(home_ref, 0), (cross_ref, two)] + [(out, two) for out in leaving]
    for out, start in starts:
        out[here, start : start + channels] = values_ref[...]
        out[edge, start : start + channels] = edge_ref[:, :channels]
    home_ref[:, channels:] = slices[rank]
    cross_ref[:, :two] = slices[lax.bitwise_xor(rank, core)]
    for mask, out in zip(chip_masks(ranks, core)[1:], leaving):
        out[:, :two] = slices[lax.bitwise_xor(rank, mask | core)]
        out[:, two + channels :] = slices[lax.bitwise_xor(rank, mask)]


def stack_crossing(cross_ref, *refs):
    out_ref = refs[-1]
    width = out_ref.shape[2]
    for m, ref in enumerate((cross_ref,) + refs[:-1]):
        out_ref[m] = ref[:, :width]


def normalize(x, gain, swap):
    other = dot(x, swap, ((1,), (0,)))
    x = x.astype(f32)
    rms = lax.rsqrt(jnp.mean(x * x, -1, keepdims=True) + epsilon)
    return [(t * rms * gain).astype(bf16) for t in (x, other)]


def prepare(core, chips, rank_ref, home_ref, crossed_ref, *refs):
    arrived, refs = refs[: chips - 1], refs[chips - 1 :]
    gain_ref, pairing_ref, outs, refs = refs[0], refs[1], refs[2:7], refs[7:]
    normed_ref, grads_ref, edge_normed_ref, edge_grads_ref, swapped_gain_ref, sems = refs
    moves = Moves(sems)
    dp_ranks = normed_ref.shape[0] // 2
    channels = gain_ref.shape[1]
    masks = chip_masks(2 * (len(arrived) + 1), core)
    seq_ranks = 2 * len(masks) // dp_ranks
    positions = home_ref.shape[0] - HALO
    two = 2 * LANES
    swap = swap_map(pairing_ref[...])
    blocks = [(0, home_ref, 0, channels)]
    blocks += [(mask, ref, two, two + channels) for mask, ref in zip(masks[1:], arrived)]
    blocks += [(mask | core, crossed_ref.at[m], two, 0) for m, mask in enumerate(masks)]
    for flip, ref, lane, grad_lane in blocks:
        source = lax.bitwise_xor(rank_ref[0], flip)
        b, i = lax.rem(source, dp_ranks), lax.div(source, dp_ranks)
        start = pl.multiple_of(i * positions, positions)
        side = jnp.where(i == 0, 0, jnp.where(i == seq_ranks - 1, 1, 2))
        both = normalize(ref[:, lane : lane + channels], gain_ref[...], swap)
        for n, normed in enumerate(both):
            first = grad_lane + n * LANES
            grads = (0.5 * ref[:, first : first + LANES].astype(f32)).astype(bf16)
            index = n * dp_ranks + b
            normed_ref[index, pl.ds(start, positions), :] = normed[:positions]
            grads_ref[index, pl.ds(start, positions), :] = grads[:positions]
            edge_normed_ref[side, index] = normed[positions:]
            edge_grads_ref[side, index] = grads[positions:]
            place = (index, pl.ds(start, positions))
            moves.start(normed_ref.at[place], outs[0].at[place])
    moves.start(grads_ref, outs[1])
    moves.start(edge_normed_ref, outs[2])
    moves.start(edge_grads_ref, outs[3])
    gain = gain_ref[...]
    first = gain.astype(bf16).astype(f32)
    second = (gain - first).astype(bf16).astype(f32)
    third = gain - first - second
    row = lax.broadcasted_iota(jnp.int32, (HALO, channels), 0)
    parts = jnp.where(row == 0, first, jnp.where(row == 1, second, jnp.where(row == 2, third, 0.0)))
    swapped = dot(parts.astype(bf16), swap, ((1,), (0,)))
    swapped_gain_ref[...] = swapped[0:1] + swapped[1:2] + swapped[2:3]
    moves.start(swapped_gain_ref, outs[4])
    moves.wait()


def main_body(pieces_in, normed_in, grads_in, edge_normed_in, edge_grads_in, *refs):
    gain_ref, shifted_out, kernel_out, gelu_out, leaving_out = refs[:5]
    pieces, normed_ref, grads_ref, edge_normed_ref, edge_grads_ref = refs[5:10]
    padded, terms, halves, bent, slopes, total, shifted_ref, kernel_ref, gelu_ref, leaving, sems = refs[10:]
    moves = Moves(sems)
    owners, part, rows = pieces.shape
    strands = normed_ref.shape[0]
    dp_ranks = strands // 2
    got_pieces = moves.start(pieces_in, pieces)
    got_edges = [
        moves.start(edge_normed_in, edge_normed_ref),
        moves.start(edge_grads_in, edge_grads_ref),
        moves.start(grads_in, grads_ref),
    ]
    got_normed = [moves.start(normed_in.at[n], normed_ref.at[n]) for n in range(strands)]
    arrivals = len(moves.copies)
    strands, span, channels = normed_ref.shape
    taps = kernel_ref.shape[0] // part
    half = taps // 2
    reach = 2 * half
    wide = bent.shape[0]

    def runs(owner):
        first, last = owner * rows, (owner + 1) * rows
        while first < last:
            tap, channel = divmod(first, channels)
            count = min(last - first, channels - channel)
            yield tap, channel, count, first - owner * rows
            first += count

    got_pieces.wait()
    for owner in range(owners):
        for tap, channel, count, offset in runs(owner):
            kernel_ref[tap * part : (tap + 1) * part, channel : channel + count] = pieces[
                owner, :, offset : offset + count
            ]
    moves.start(kernel_ref, kernel_out)
    padded[...] = jnp.zeros_like(padded)
    for k in range(taps):
        padded[k * LANES : k * LANES + part, :] = kernel_ref[k * part : (k + 1) * part, :]
    kernel = padded[...]
    for copy in got_edges:
        copy.wait()
    edge_normed = jnp.concatenate([edge_normed_ref[side, s] for side in range(2) for s in range(strands)], 0)
    edge_terms = dot(edge_normed, kernel, ((1,), (1,)))
    for strand in range(strands):
        forward = strand < dp_ranks
        got_normed[strand].wait()
        terms[HALO : HALO + span, :] = dot(normed_ref[strand], kernel, ((1,), (1,)))
        halves[HALO : HALO + span, :] = grads_ref[strand].astype(f32)
        for side, start in enumerate((0, HALO + span)):
            first = (side * strands + strand) * HALO
            terms[start : start + HALO, :] = edge_terms[first : first + HALO]
            halves[start : start + HALO, :] = edge_grads_ref[side, strand].astype(f32)
        preact = jnp.zeros((wide, LANES), f32)
        for k in range(taps):
            start = HALO - reach + k if forward else HALO - k
            preact += terms[start : start + wide, k * LANES : (k + 1) * LANES]
        result, slope = gelu_and_slope(preact)
        bent[...] = result
        gelu_ref[strand] = bent[half : half + span, :].astype(bf16)
        slopes[...] = halves[HALO - half : HALO - half + wide, :] * slope
        for k in range(taps):
            start = reach - k if forward else k
            shifted_ref[strand, :, k * part : (k + 1) * part] = slopes[start : start + span, :part].astype(bf16)
        moves.start(shifted_ref.at[strand], shifted_out.at[strand])
    moves.start(gelu_ref, gelu_out)
    total[...] = dot(
        shifted_ref[...].reshape(strands * span, taps * part),
        normed_ref[...].reshape(strands * span, channels),
        ((0,), (0,)),
    )
    gain = jnp.sum(total[...] * kernel_ref[...].astype(f32), 0, keepdims=True) / gain_ref[...]
    gain_high = gain.astype(bf16).astype(f32)
    row = lax.broadcasted_iota(jnp.int32, (EXTRA, channels), 0)
    extra = jnp.where(row == 0, gain_high, jnp.where(row == 1, gain - gain_high, 0.0))
    own_gain = channels // owners
    for owner in range(owners):
        for tap, channel, count, offset in runs(owner):
            leaving[owner, :part, offset : offset + count] = total[
                tap * part : (tap + 1) * part, channel : channel + count
            ].astype(bf16)
        leaving[owner, part:, :] = jnp.zeros((EXTRA, rows), bf16)
        leaving[owner, part:, :own_gain] = extra[
            :, owner * own_gain : (owner + 1) * own_gain
        ].astype(bf16)
    moves.start(leaving, leaving_out)
    for copy in moves.copies[arrivals:]:
        copy.wait()


def input_gradient(
    rank_ref, shifted_ref, kernel_ref, gelu_ref, gain_ref, swapped_gain_ref, pairing_ref, own_ref, cross_ref, *scratch
):
    scaled, shifted, kernel_in, gelus, sems = scratch
    strands = shifted_ref.shape[0]
    moves = Moves(sems)
    got_kernel = moves.start(kernel_ref, kernel_in)
    got_shifted = [moves.start(shifted_ref.at[n], shifted.at[n]) for n in range(strands)]
    got_gelus = moves.start(gelu_ref, gelus)
    dp_ranks = strands // 2
    chips, positions, _ = own_ref.shape
    channels = gain_ref.shape[1]
    got_kernel.wait()
    kernel = kernel_in[...]
    swapped = dot(kernel, swap_map(pairing_ref[...]), ((1,), (0,))).astype(bf16)
    for b in range(dp_ranks):
        got_shifted[b].wait()
        got_shifted[dp_ranks + b].wait()
        scaled[b] = (
            dot(shifted[b], kernel, ((1,), (0,))) * gain_ref[...]
            + dot(shifted[dp_ranks + b], swapped, ((1,), (0,))) * swapped_gain_ref[...]
        ).astype(bf16)
    got_gelus.wait()
    for m, mask in enumerate(chip_masks(2 * chips, dp_ranks)):
        for out, flip in ((own_ref, mask), (cross_ref, mask | dp_ranks)):
            target = lax.bitwise_xor(rank_ref[0], flip)
            b = lax.rem(target, dp_ranks)
            start = pl.multiple_of(lax.div(target, dp_ranks) * positions, positions)
            out[m, :, :channels] = scaled[b, pl.ds(start, positions), :]
            for n in range(2):
                lane = channels + n * LANES
                out[m, :, lane : lane + LANES] = gelus[n * dp_ranks + b, pl.ds(start, positions), :]


def chip_sum(part, own_ref, crossed_ref, *outs):
    channels = own_ref.shape[2] - 2 * LANES
    for m, out in enumerate(outs):
        out[:, :channels] = (
            own_ref[m, :, :channels].astype(f32) + crossed_ref[m, :, :channels].astype(f32)
        ).astype(bf16)
        for c, ref in enumerate((own_ref, crossed_ref)):
            for n in range(2):
                lane = channels + n * LANES
                start = channels + (2 * c + n) * part
                out[:, start : start + part] = ref[m, :, lane : lane + part]


def finish(part, core, rank_ref, values_ref, cot_ref, pairing_ref, *refs):
    arrived, (combined_ref, grad_ref, gelus) = refs[:-3], refs[-3:]
    channels = values_ref.shape[1]
    ranks = gelus.shape[1]
    gelus[...] = jnp.zeros_like(gelus)
    scaled = jnp.zeros(values_ref.shape, f32)
    for mask, block in zip(chip_masks(ranks, core), arrived):
        scaled += block[:, :channels].astype(f32)
        for c in range(2):
            source = lax.bitwise_xor(rank_ref[0], mask | c * core)
            for n in range(2):
                start = channels + (2 * c + n) * part
                gelus[n, source, :, :part] = block[:, start : start + part]
    joined = [jnp.concatenate([gelus[n, j] for j in range(ranks)], -1) for n in range(2)]
    maps = slot_maps(part, ranks * LANES, pairing_ref[...])
    plain, other = [dot(j, m, ((1,), (0,))) for j, m in zip(joined, maps)]
    values = values_ref[...].astype(f32)
    rms = lax.rsqrt(jnp.mean(values * values, -1, keepdims=True) + epsilon)
    reverse_out = (values + other).astype(bf16).astype(f32)
    combined_ref[...] = (0.5 * (values + plain + reverse_out)).astype(bf16)
    along = jnp.mean(scaled * values, -1, keepdims=True)
    grad_ref[...] = (cot_ref[...].astype(f32) + rms * scaled - values * (rms * rms * rms * along)).astype(bf16)


def collect(owner_of, terms_ref, kernel_ref, gain_ref, joined):
    _, height, rows = terms_ref.shape
    part = height - EXTRA
    joined[...] = jnp.zeros_like(joined)
    gain = jnp.zeros((1, rows), f32)
    for rank, owners in enumerate(owner_of):
        total = terms_ref[owners[0]].astype(f32)
        for owner in owners[1:]:
            total += terms_ref[owner].astype(f32)
        joined[rank * part : (rank + 1) * part, :rows] = total[:part]
        gain += total[part : part + 1] + total[part + 1 : part + 2]
    kernel_ref[...] = joined[...].T[:rows]
    gain_ref[...] = gain[:, : gain_ref.shape[1]]


def flipped_pairs(count, mask):
    return [(i, i ^ mask) for i in range(count)]


def per_device(activations, cotangent, weights, norm_gain, pairing):
    seq_ranks = lax.axis_size("seq_rank")
    dp_ranks = lax.axis_size("dp_rank")
    seq_blocks = lax.axis_size("seq_block")
    dp_blocks = lax.axis_size("dp_block")
    ranks = seq_ranks * dp_ranks
    owners = ranks * seq_blocks * dp_blocks
    positions, channels = activations.shape[1:]
    rows = weights.shape[0]
    taps = rows * owners // channels
    part = channels // ranks
    span = positions * seq_ranks
    long = span + 2 * HALO
    reach = taps - taps % 2
    wide = -(-(span + reach) // 8) * 8
    strands = 2 * dp_ranks
    width = channels + 2 * LANES
    rank = lax.axis_index(RANK).reshape(1)
    values, cot = activations[0], cotangent[0]
    along = ("seq_block", "seq_rank")
    ends = [(b * seq_ranks - 1, b * seq_ranks) for b in range(1, seq_blocks)]
    both = jnp.concatenate([values, cot], -1)
    edge = jnp.where(lax.axis_index("seq_rank") == 0, both[:HALO], both[-HALO:])
    edge = lax.ppermute(edge, along, ends + [(target, source) for source, target in ends])
    piece_of = [
        sr * dp_ranks + dr
        for _ in range(seq_blocks)
        for sr in range(seq_ranks)
        for _ in range(dp_blocks)
        for dr in range(dp_ranks)
    ]
    square = -(-rows // LANES) * LANES
    slices = called(
        lambda *refs: spread(piece_of, *refs),
        pltpu.HBM((owners, part, rows), bf16),
        (weights,),
        16,
        scratch=[
            pltpu.VMEM((square, channels), f32),
            pltpu.VMEM((owners, part, rows), bf16),
            pltpu.SemaphoreType.DMA((1,)),
        ],
        out_specs=HBM,
    )
    slices, packed = lax.optimization_barrier((slices, values))
    pieces = lax.all_to_all(slices, EVERY, 0, 0, tiled=True)
    pairing = pairing.reshape(1, channels)
    gain = norm_gain.reshape(1, channels)
    core = dp_ranks
    masks = chip_masks(ranks, core)
    block = positions + HALO
    home, cross, *leaving = called(
        lambda *refs: pack_messages(part, core, *refs),
        (shape_of((block, width), bf16),) * 2
        + tuple(shape_of((block, width + 2 * LANES), bf16) for _ in masks[1:]),
        (rank, packed, cot, edge, pairing),
        16,
        scratch=[pltpu.VMEM((ranks, block, 2 * LANES), bf16)],
        specs=[SMEM] + [VMEM] * 4,
    )
    arrived = [
        lax.ppermute(message, RANK, flipped_pairs(ranks, mask))
        for message, mask in zip(leaving, masks[1:])
    ]
    crossing = called(
        stack_crossing, shape_of((len(masks), block, width), bf16), (cross, *arrived), 8
    )
    crossed = lax.ppermute(crossing, RANK, flipped_pairs(ranks, core))
    ready_shapes = [
        ((strands, span, channels), bf16),
        ((strands, span, LANES), bf16),
        ((3, strands, HALO, channels), bf16),
        ((3, strands, HALO, LANES), bf16),
        ((1, channels), f32),
    ]
    ready = called(
        lambda *refs: prepare(core, len(masks), *refs),
        tuple(pltpu.HBM(*shape) for shape in ready_shapes),
        (rank, home, crossed, *arrived, gain, pairing),
        24,
        scratch=[pltpu.VMEM(*shape) for shape in ready_shapes]
        + [pltpu.SemaphoreType.DMA((2 * ranks + 4,))],
        specs=[SMEM] + [VMEM] * (4 + len(arrived)),
        out_specs=(HBM,) * 5,
    )
    ready = [pltpu.with_memory_space_constraint(x, pltpu.HBM) for x in ready]
    pieces = pltpu.with_memory_space_constraint(pieces, pltpu.HBM)
    shapes = (
        (strands, span, taps * part),
        (taps * part, channels),
        (strands, span, LANES),
        (owners, part + EXTRA, rows),
    )
    shifted, kernel, gelus, outgoing = called(
        main_body,
        tuple(pltpu.HBM(shape, bf16) for shape in shapes),
        (pieces, *ready[:4], gain),
        40,
        scratch=[pltpu.VMEM(pieces.shape, bf16)]
        + [pltpu.VMEM(*shape) for shape in ready_shapes[:4]]
        + [
            pltpu.VMEM((taps * LANES, channels), bf16),
            pltpu.VMEM((long, taps * LANES), f32),
            pltpu.VMEM((long, LANES), f32),
            pltpu.VMEM((wide, LANES), f32),
            pltpu.VMEM((wide, LANES), f32),
            pltpu.VMEM((taps * part, channels), f32),
        ]
        + [pltpu.VMEM(shape, bf16) for shape in shapes]
        + [pltpu.SemaphoreType.DMA((2 * strands + 7,))],
        specs=[HBM] * 5 + [VMEM],
        out_specs=(HBM,) * 4,
    )
    terms = lax.all_to_all(outgoing, EVERY, 0, 0, tiled=True)
    halves = shape_of((len(masks), positions, width), bf16)
    kept = [pltpu.with_memory_space_constraint(x, pltpu.HBM) for x in (shifted, kernel, gelus)]
    own, cross = called(
        input_gradient,
        (halves, halves),
        (rank, *kept, gain, ready[4], pairing),
        24,
        scratch=[pltpu.VMEM((dp_ranks, span, channels), bf16)]
        + [pltpu.VMEM(shape, bf16) for shape in shapes[:3]]
        + [pltpu.SemaphoreType.DMA((strands + 2,))],
        specs=[SMEM] + [HBM] * 3 + [VMEM] * 3,
    )
    crossed = lax.ppermute(cross, RANK, flipped_pairs(ranks, core))
    leaving = called(
        lambda *refs: chip_sum(part, *refs),
        tuple(shape_of((positions, channels + 4 * part), bf16) for _ in masks),
        (own, crossed),
        8,
    )
    arrived = leaving[:1] + tuple(
        lax.ppermute(message, RANK, flipped_pairs(ranks, mask))
        for message, mask in zip(leaving[1:], masks[1:])
    )
    combined, grad_input = called(
        lambda *refs: finish(part, core, *refs),
        (shape_of((positions, channels), bf16), shape_of((positions, channels), bf16)),
        (rank, values, cot, pairing, *arrived),
        16,
        scratch=[pltpu.VMEM((2, ranks, positions, LANES), bf16)],
        specs=[SMEM] + [VMEM] * (3 + len(arrived)),
    )
    order = [
        [
            ((sb * seq_ranks + sr) * dp_blocks + db) * dp_ranks + dr
            for sb in range(seq_blocks)
            for db in range(dp_blocks)
        ]
        for sr in range(seq_ranks)
        for dr in range(dp_ranks)
    ]
    grad_kernel, grad_gain = called(
        lambda *refs: collect(order, *refs),
        (shape_of((rows, channels), f32), shape_of((1, channels // owners), f32)),
        (terms,),
        16,
        scratch=[pltpu.VMEM((channels, -(-rows // LANES) * LANES), f32)],
    )
    return combined[None], grad_input[None], grad_kernel, grad_gain[0]


def solution(mesh):
    seq, dp = mesh.shape["seq"], mesh.shape["dp"]
    seq_ranks, dp_ranks = 4, 2
    grouped = Mesh(mesh.devices.reshape(seq // seq_ranks, seq_ranks, dp // dp_ranks, dp_ranks), EVERY)
    along = P(("dp_block", "dp_rank"), ("seq_block", "seq_rank"), None)
    return jax.shard_map(
        per_device,
        mesh=grouped,
        in_specs=(along, along, P(EVERY, None), P(), P()),
        out_specs=(along, along, P(EVERY, None), P(EVERY)),
        check_vma=False,
    )
```

```python
import jax
import jax.numpy as jnp
from jax import lax
from jax.experimental import pallas as pl
from jax.experimental.pallas import tpu as pltpu
from jax.sharding import Mesh, PartitionSpec as P

epsilon = 1e-06
RANK = ("seq_rank", "dp_rank")
EVERY = ("seq_block", "seq_rank", "dp_block", "dp_rank")
LANES = 128
HALO = 16
EXTRA = 16
VMEM = pl.BlockSpec(memory_space=pltpu.VMEM)
SMEM = pl.BlockSpec(memory_space=pltpu.SMEM)
HBM = pl.BlockSpec(memory_space=pltpu.HBM)
bf16 = jnp.bfloat16
f32 = jnp.float32


def called(body, outs, args, vmem, scratch=(), specs=None, out_specs=None):
    return pl.pallas_call(
        body,
        out_shape=outs,
        in_specs=specs or [VMEM] * len(args),
        out_specs=out_specs or jax.tree.map(lambda _: VMEM, outs),
        scratch_shapes=list(scratch),
        compiler_params=pltpu.CompilerParams(vmem_limit_bytes=vmem * 2**20),
        cost_estimate=pl.CostEstimate(flops=0, bytes_accessed=0, transcendentals=0),
    )(*args)


def shape_of(shape, dtype):
    return jax.ShapeDtypeStruct(shape, dtype)


def dot(a, b, contract):
    return lax.dot_general(a, b, (contract, ((), ())), preferred_element_type=f32)


def gelu_and_slope(x):
    inner = 0.7978845608028654 * (x + 0.044715 * (x * x * x))
    bend = jnp.tanh(inner)
    half_sum = 0.5 * (1.0 + bend)
    slope = half_sum + (0.5 * x) * (1.0 - bend * bend) * (
        0.7978845608028654 * (1.0 + 0.134145 * (x * x))
    )
    return x * half_sum, slope


def slot_maps(part, slots, pairing):
    shape = (slots, pairing.shape[1])
    slot = lax.broadcasted_iota(jnp.int32, shape, 0)
    lane = lax.bitwise_and(slot, LANES - 1)
    channel_of = jnp.where(lane < part, lax.div(slot, LANES) * part + lane, -1)
    channel = lax.broadcasted_iota(jnp.int32, shape, 1)
    return [jnp.where(channel_of == c, 1.0, 0.0).astype(bf16) for c in (channel, pairing)]


def swap_map(pairing):
    channels = pairing.shape[1]
    row = lax.broadcasted_iota(jnp.int32, (channels, channels), 0)
    return jnp.where(row == pairing, 1.0, 0.0).astype(bf16)


def chip_masks(ranks, core):
    return [mask for mask in range(ranks) if not mask & core]


class Moves:
    def __init__(self, sems):
        self.sems, self.copies = sems, []

    def start(self, source, target):
        copy = pltpu.make_async_copy(source, target, self.sems.at[len(self.copies)])
        copy.start()
        self.copies.append(copy)
        return copy

    def wait(self):
        for copy in self.copies:
            copy.wait()


def spread(piece_of, weights_ref, out_ref, square, sent, sems):
    rows, channels = weights_ref.shape
    part = out_ref.shape[1]
    square[...] = jnp.zeros_like(square)
    square[:rows] = weights_ref[...].astype(f32)
    turned = square[...].T.astype(bf16)
    for owner, piece in enumerate(piece_of):
        sent[owner] = turned[piece * part : (piece + 1) * part, :rows]
    moves = Moves(sems)
    moves.start(sent, out_ref)
    moves.wait()


def pack_messages(part, core, rank_ref, values_ref, cot_ref, edge_ref, pairing_ref, *refs):
    home_ref, cross_ref, leaving, slices = refs[0], refs[1], refs[2:-1], refs[-1]
    positions, channels = values_ref.shape
    ranks = slices.shape[0]
    here, edge = slice(0, positions), slice(positions, None)
    for n, map_of in enumerate(slot_maps(part, ranks * LANES, pairing_ref[...])):
        for rows, source in ((here, cot_ref[...]), (edge, edge_ref[:, channels:])):
            piece = dot(source, map_of, ((1,), (1,))).astype(bf16)
            for j in range(ranks):
                slices[j, rows, n * part : (n + 1) * part] = piece[:, j * LANES : j * LANES + part]
    rank = rank_ref[0]
    width = home_ref.shape[1]
    for out in refs[:-1]:
        out[here, :channels] = values_ref[...]
        out[edge, :channels] = edge_ref[:, :channels]
    home_ref[:, channels:] = slices[rank]
    cross_ref[:, channels:] = slices[lax.bitwise_xor(rank, core)]
    for mask, out in zip(chip_masks(ranks, core)[1:], leaving):
        out[:, channels:width] = slices[lax.bitwise_xor(rank, mask | core)]
        out[:, width:] = slices[lax.bitwise_xor(rank, mask)]


def stack_crossing(cross_ref, *refs):
    out_ref = refs[-1]
    width = out_ref.shape[2]
    for m, ref in enumerate((cross_ref,) + refs[:-1]):
        out_ref[m] = ref[:, :width]


def normalize(x, gain, swap):
    other = dot(x, swap, ((1,), (0,)))
    x = x.astype(f32)
    rms = lax.rsqrt(jnp.mean(x * x, -1, keepdims=True) + epsilon)
    return [(t * rms * gain).astype(bf16) for t in (x, other)]


def main_body(core, chips, rank_ref, pieces_in, home_in, crossed_in, *refs):
    arrived_in, refs = refs[: chips - 1], refs[chips - 1 :]
    gain_ref, pairing_ref, shifted_out, kernel_out, gelu_out, leaving_out = refs[:6]
    pieces, home, crossed, arrived, normed_ref, grads_ref, edge_normed_ref, edge_grads_ref = refs[6:14]
    padded, terms, halves, bent, slopes, total, shifted_ref, kernel_ref, gelu_ref, leaving, sems = refs[14:]
    owners, part, rows = pieces.shape
    strands = normed_ref.shape[0]
    dp_ranks = strands // 2
    moves = Moves(sems)
    got_blocks = [moves.start(home_in, home)]
    got_blocks += [moves.start(block, arrived.at[m]) for m, block in enumerate(arrived_in)]
    got_blocks += [moves.start(crossed_in.at[m], crossed.at[m]) for m in range(chips)]
    got_pieces = moves.start(pieces_in, pieces)
    arrivals = len(moves.copies)
    masks = chip_masks(2 * chips, core)
    seq_ranks = 2 * chips // dp_ranks
    positions = home.shape[0] - HALO
    channels, width = gain_ref.shape[1], home.shape[1]
    swap = swap_map(pairing_ref[...])
    blocks = [(0, home, channels)]
    blocks += [(mask, arrived.at[m], width) for m, mask in enumerate(masks[1:])]
    blocks += [(mask | core, crossed.at[m], channels) for m, mask in enumerate(masks)]
    for got, (flip, ref, lane) in zip(got_blocks, blocks):
        got.wait()
        source = lax.bitwise_xor(rank_ref[0], flip)
        b, i = lax.rem(source, dp_ranks), lax.div(source, dp_ranks)
        start = pl.multiple_of(i * positions, positions)
        side = jnp.where(i == 0, 0, jnp.where(i == seq_ranks - 1, 1, 2))
        both = normalize(ref[:, :channels], gain_ref[...], swap)
        for n, normed in enumerate(both):
            first = lane + n * part
            grads = 0.5 * ref[:, first : first + part].astype(f32)
            index = n * dp_ranks + b
            normed_ref[index, pl.ds(start, positions), :] = normed[:positions]
            grads_ref[index, pl.ds(start, positions), :part] = grads[:positions]
            edge_normed_ref[side, index] = normed[positions:]
            edge_grads_ref[side, index, :, :part] = grads[positions:]
    span = normed_ref.shape[1]
    taps = kernel_ref.shape[0] // part
    half = taps // 2
    reach = 2 * half
    wide = bent.shape[0]

    def runs(owner):
        first, last = owner * rows, (owner + 1) * rows
        while first < last:
            tap, channel = divmod(first, channels)
            count = min(last - first, channels - channel)
            yield tap, channel, count, first - owner * rows
            first += count

    got_pieces.wait()
    for owner in range(owners):
        for tap, channel, count, offset in runs(owner):
            kernel_ref[tap * part : (tap + 1) * part, channel : channel + count] = pieces[
                owner, :, offset : offset + count
            ]
    moves.start(kernel_ref, kernel_out)
    padded[...] = jnp.zeros_like(padded)
    for k in range(taps):
        padded[k * LANES : k * LANES + part, :] = kernel_ref[k * part : (k + 1) * part, :]
    kernel = padded[...]
    edge_normed = jnp.concatenate([edge_normed_ref[side, s] for side in range(2) for s in range(strands)], 0)
    edge_terms = dot(edge_normed, kernel, ((1,), (1,)))
    for strand in range(strands):
        forward = strand < dp_ranks
        terms[HALO : HALO + span, :] = dot(normed_ref[strand], kernel, ((1,), (1,)))
        halves[HALO : HALO + span, :] = grads_ref[strand]
        for side, start in enumerate((0, HALO + span)):
            first = (side * strands + strand) * HALO
            terms[start : start + HALO, :] = edge_terms[first : first + HALO]
            halves[start : start + HALO, :] = edge_grads_ref[side, strand]
        preact = jnp.zeros((wide, LANES), f32)
        for k in range(taps):
            start = HALO - reach + k if forward else HALO - k
            preact += terms[start : start + wide, k * LANES : (k + 1) * LANES]
        result, slope = gelu_and_slope(preact)
        bent[...] = result
        gelu_ref[strand] = bent[half : half + span, :].astype(bf16)
        slopes[...] = halves[HALO - half : HALO - half + wide, :] * slope
        for k in range(taps):
            start = reach - k if forward else k
            shifted_ref[strand, :, k * part : (k + 1) * part] = slopes[start : start + span, :part].astype(bf16)
        moves.start(shifted_ref.at[strand], shifted_out.at[strand])
    moves.start(gelu_ref, gelu_out)
    total[...] = dot(
        shifted_ref[...].reshape(strands * span, taps * part),
        normed_ref[...].reshape(strands * span, channels),
        ((0,), (0,)),
    )
    gain = jnp.sum(total[...] * kernel_ref[...].astype(f32), 0, keepdims=True) / gain_ref[...]
    gain_high = gain.astype(bf16).astype(f32)
    row = lax.broadcasted_iota(jnp.int32, (EXTRA, channels), 0)
    extra = jnp.where(row == 0, gain_high, jnp.where(row == 1, gain - gain_high, 0.0))
    own_gain = channels // owners
    for owner in range(owners):
        for tap, channel, count, offset in runs(owner):
            leaving[owner, :part, offset : offset + count] = total[
                tap * part : (tap + 1) * part, channel : channel + count
            ].astype(bf16)
        leaving[owner, part:, :] = jnp.zeros((EXTRA, rows), bf16)
        leaving[owner, part:, :own_gain] = extra[
            :, owner * own_gain : (owner + 1) * own_gain
        ].astype(bf16)
    moves.start(leaving, leaving_out)
    for copy in moves.copies[arrivals:]:
        copy.wait()


def input_gradient(
    rank_ref, shifted_ref, kernel_ref, gelu_ref, gain_ref, pairing_ref, own_ref, cross_ref, *scratch
):
    scaled, shifted, kernel_in, gelus, sems = scratch
    strands = shifted_ref.shape[0]
    moves = Moves(sems)
    got_kernel = moves.start(kernel_ref, kernel_in)
    got_shifted = [moves.start(shifted_ref.at[n], shifted.at[n]) for n in range(strands)]
    got_gelus = moves.start(gelu_ref, gelus)
    dp_ranks = strands // 2
    chips, positions, _ = own_ref.shape
    channels = gain_ref.shape[1]
    got_kernel.wait()
    kernel = kernel_in[...]
    swap = swap_map(pairing_ref[...])
    swapped = dot(kernel, swap, ((1,), (0,))).astype(bf16)
    gain = gain_ref[...]
    first = gain.astype(bf16).astype(f32)
    second = (gain - first).astype(bf16).astype(f32)
    third = gain - first - second
    row = lax.broadcasted_iota(jnp.int32, (HALO, channels), 0)
    parts = jnp.where(row == 0, first, jnp.where(row == 1, second, jnp.where(row == 2, third, 0.0)))
    swapped_gain = dot(parts.astype(bf16), swap, ((1,), (0,)))
    swapped_gain = swapped_gain[0:1] + swapped_gain[1:2] + swapped_gain[2:3]
    for b in range(dp_ranks):
        got_shifted[b].wait()
        got_shifted[dp_ranks + b].wait()
        scaled[b] = (
            dot(shifted[b], kernel, ((1,), (0,))) * gain_ref[...]
            + dot(shifted[dp_ranks + b], swapped, ((1,), (0,))) * swapped_gain
        ).astype(bf16)
    got_gelus.wait()
    for m, mask in enumerate(chip_masks(2 * chips, dp_ranks)):
        for out, flip in ((own_ref, mask), (cross_ref, mask | dp_ranks)):
            target = lax.bitwise_xor(rank_ref[0], flip)
            b = lax.rem(target, dp_ranks)
            start = pl.multiple_of(lax.div(target, dp_ranks) * positions, positions)
            out[m, :, :channels] = scaled[b, pl.ds(start, positions), :]
            for n in range(2):
                lane = channels + n * LANES
                out[m, :, lane : lane + LANES] = gelus[n * dp_ranks + b, pl.ds(start, positions), :]


def chip_sum(part, own_ref, crossed_ref, *outs):
    channels = own_ref.shape[2] - 2 * LANES
    for m, out in enumerate(outs):
        out[:, :channels] = (
            own_ref[m, :, :channels].astype(f32) + crossed_ref[m, :, :channels].astype(f32)
        ).astype(bf16)
        for c, ref in enumerate((own_ref, crossed_ref)):
            for n in range(2):
                lane = channels + n * LANES
                start = channels + (2 * c + n) * part
                out[:, start : start + part] = ref[m, :, lane : lane + part]


def finish(part, core, rank_ref, values_ref, cot_ref, pairing_ref, *refs):
    arrived, (combined_ref, grad_ref, gelus) = refs[:-3], refs[-3:]
    channels = values_ref.shape[1]
    ranks = gelus.shape[1]
    gelus[...] = jnp.zeros_like(gelus)
    scaled = jnp.zeros(values_ref.shape, f32)
    for mask, block in zip(chip_masks(ranks, core), arrived):
        scaled += block[:, :channels].astype(f32)
        for c in range(2):
            source = lax.bitwise_xor(rank_ref[0], mask | c * core)
            for n in range(2):
                start = channels + (2 * c + n) * part
                gelus[n, source, :, :part] = block[:, start : start + part]
    joined = [jnp.concatenate([gelus[n, j] for j in range(ranks)], -1) for n in range(2)]
    maps = slot_maps(part, ranks * LANES, pairing_ref[...])
    plain, other = [dot(j, m, ((1,), (0,))) for j, m in zip(joined, maps)]
    values = values_ref[...].astype(f32)
    rms = lax.rsqrt(jnp.mean(values * values, -1, keepdims=True) + epsilon)
    reverse_out = (values + other).astype(bf16).astype(f32)
    combined_ref[...] = (0.5 * (values + plain + reverse_out)).astype(bf16)
    along = jnp.mean(scaled * values, -1, keepdims=True)
    grad_ref[...] = (cot_ref[...].astype(f32) + rms * scaled - values * (rms * rms * rms * along)).astype(bf16)


def collect(owner_of, terms_ref, kernel_ref, gain_ref, joined):
    _, height, rows = terms_ref.shape
    part = height - EXTRA
    joined[...] = jnp.zeros_like(joined)
    gain = jnp.zeros((1, rows), f32)
    for rank, owners in enumerate(owner_of):
        total = terms_ref[owners[0]].astype(f32)
        for owner in owners[1:]:
            total += terms_ref[owner].astype(f32)
        joined[rank * part : (rank + 1) * part, :rows] = total[:part]
        gain += total[part : part + 1] + total[part + 1 : part + 2]
    kernel_ref[...] = joined[...].T[:rows]
    gain_ref[...] = gain[:, : gain_ref.shape[1]]


def flipped_pairs(count, mask):
    return [(i, i ^ mask) for i in range(count)]


def per_device(activations, cotangent, weights, norm_gain, pairing):
    seq_ranks = lax.axis_size("seq_rank")
    dp_ranks = lax.axis_size("dp_rank")
    seq_blocks = lax.axis_size("seq_block")
    dp_blocks = lax.axis_size("dp_block")
    ranks = seq_ranks * dp_ranks
    owners = ranks * seq_blocks * dp_blocks
    positions, channels = activations.shape[1:]
    rows = weights.shape[0]
    taps = rows * owners // channels
    part = channels // ranks
    span = positions * seq_ranks
    long = span + 2 * HALO
    reach = taps - taps % 2
    wide = -(-(span + reach) // 8) * 8
    strands = 2 * dp_ranks
    width = channels + 2 * LANES
    slim = channels + 2 * part
    rank = lax.axis_index(RANK).reshape(1)
    values, cot = activations[0], cotangent[0]
    along = ("seq_block", "seq_rank")
    ends = [(b * seq_ranks - 1, b * seq_ranks) for b in range(1, seq_blocks)]
    both = jnp.concatenate([values, cot], -1)
    edge = jnp.where(lax.axis_index("seq_rank") == 0, both[:HALO], both[-HALO:])
    edge = lax.ppermute(edge, along, ends + [(target, source) for source, target in ends])
    piece_of = [
        sr * dp_ranks + dr
        for _ in range(seq_blocks)
        for sr in range(seq_ranks)
        for _ in range(dp_blocks)
        for dr in range(dp_ranks)
    ]
    square = -(-rows // LANES) * LANES
    slices = called(
        lambda *refs: spread(piece_of, *refs),
        pltpu.HBM((owners, part, rows), bf16),
        (weights,),
        16,
        scratch=[
            pltpu.VMEM((square, channels), f32),
            pltpu.VMEM((owners, part, rows), bf16),
            pltpu.SemaphoreType.DMA((1,)),
        ],
        out_specs=HBM,
    )
    slices, packed = lax.optimization_barrier((slices, values))
    pieces = lax.all_to_all(slices, EVERY, 0, 0, tiled=True)
    pairing = pairing.reshape(1, channels)
    gain = norm_gain.reshape(1, channels)
    core = dp_ranks
    masks = chip_masks(ranks, core)
    block = positions + HALO
    home, cross, *leaving = called(
        lambda *refs: pack_messages(part, core, *refs),
        (pltpu.HBM((block, slim), bf16), shape_of((block, slim), bf16))
        + tuple(shape_of((block, slim + 2 * part), bf16) for _ in masks[1:]),
        (rank, packed, cot, edge, pairing),
        16,
        scratch=[pltpu.VMEM((ranks, block, 2 * part), bf16)],
        specs=[SMEM] + [VMEM] * 4,
    )
    arrived = [
        lax.ppermute(message, RANK, flipped_pairs(ranks, mask))
        for message, mask in zip(leaving, masks[1:])
    ]
    crossing = called(
        stack_crossing, shape_of((len(masks), block, slim), bf16), (cross, *arrived), 8
    )
    crossed = lax.ppermute(crossing, RANK, flipped_pairs(ranks, core))
    held = (pieces, home, crossed, *arrived)
    shapes = (
        (strands, span, taps * part),
        (taps * part, channels),
        (strands, span, LANES),
        (owners, part + EXTRA, rows),
    )
    shifted, kernel, gelus, outgoing = called(
        lambda *refs: main_body(core, len(masks), *refs),
        tuple(pltpu.HBM(shape, bf16) for shape in shapes),
        (rank, *held, gain, pairing),
        40,
        scratch=[
            pltpu.VMEM(pieces.shape, bf16),
            pltpu.VMEM(home.shape, bf16),
            pltpu.VMEM(crossed.shape, bf16),
            pltpu.VMEM((len(arrived), *arrived[0].shape), bf16),
            pltpu.VMEM((strands, span, channels), bf16),
            pltpu.VMEM((strands, span, LANES), f32),
            pltpu.VMEM((3, strands, HALO, channels), bf16),
            pltpu.VMEM((3, strands, HALO, LANES), f32),
            pltpu.VMEM((taps * LANES, channels), bf16),
            pltpu.VMEM((long, taps * LANES), f32),
            pltpu.VMEM((long, LANES), f32),
            pltpu.VMEM((wide, LANES), f32),
            pltpu.VMEM((wide, LANES), f32),
            pltpu.VMEM((taps * part, channels), f32),
        ]
        + [pltpu.VMEM(shape, bf16) for shape in shapes]
        + [pltpu.SemaphoreType.DMA((ranks + strands + 4,))],
        specs=[SMEM] + [pl.BlockSpec(memory_space=pl.ANY)] * len(held) + [VMEM] * 2,
        out_specs=(HBM,) * 4,
    )
    terms = lax.all_to_all(outgoing, EVERY, 0, 0, tiled=True)
    halves = shape_of((len(masks), positions, width), bf16)
    kept = [pltpu.with_memory_space_constraint(x, pltpu.HBM) for x in (shifted, kernel, gelus)]
    own, cross = called(
        input_gradient,
        (halves, halves),
        (rank, *kept, gain, pairing),
        24,
        scratch=[pltpu.VMEM((dp_ranks, span, channels), bf16)]
        + [pltpu.VMEM(shape, bf16) for shape in shapes[:3]]
        + [pltpu.SemaphoreType.DMA((strands + 2,))],
        specs=[SMEM] + [HBM] * 3 + [VMEM] * 2,
    )
    crossed = lax.ppermute(cross, RANK, flipped_pairs(ranks, core))
    leaving = called(
        lambda *refs: chip_sum(part, *refs),
        tuple(shape_of((positions, channels + 4 * part), bf16) for _ in masks),
        (own, crossed),
        8,
    )
    arrived = leaving[:1] + tuple(
        lax.ppermute(message, RANK, flipped_pairs(ranks, mask))
        for message, mask in zip(leaving[1:], masks[1:])
    )
    combined, grad_input = called(
        lambda *refs: finish(part, core, *refs),
        (shape_of((positions, channels), bf16), shape_of((positions, channels), bf16)),
        (rank, values, cot, pairing, *arrived),
        16,
        scratch=[pltpu.VMEM((2, ranks, positions, LANES), bf16)],
        specs=[SMEM] + [VMEM] * (3 + len(arrived)),
    )
    order = [
        [
            ((sb * seq_ranks + sr) * dp_blocks + db) * dp_ranks + dr
            for sb in range(seq_blocks)
            for db in range(dp_blocks)
        ]
        for sr in range(seq_ranks)
        for dr in range(dp_ranks)
    ]
    grad_kernel, grad_gain = called(
        lambda *refs: collect(order, *refs),
        (shape_of((rows, channels), f32), shape_of((1, channels // owners), f32)),
        (terms,),
        16,
        scratch=[pltpu.VMEM((channels, -(-rows // LANES) * LANES), f32)],
    )
    return combined[None], grad_input[None], grad_kernel, grad_gain[0]


def solution(mesh):
    seq, dp = mesh.shape["seq"], mesh.shape["dp"]
    seq_ranks, dp_ranks = 4, 2
    grouped = Mesh(mesh.devices.reshape(seq // seq_ranks, seq_ranks, dp // dp_ranks, dp_ranks), EVERY)
    along = P(("dp_block", "dp_rank"), ("seq_block", "seq_rank"), None)
    return jax.shard_map(
        per_device,
        mesh=grouped,
        in_specs=(along, along, P(EVERY, None), P(), P()),
        out_specs=(along, along, P(EVERY, None), P(EVERY)),
        check_vma=False,
    )
```

```python
import jax
import jax.numpy as jnp
from jax import lax
from jax.experimental import pallas as pl
from jax.experimental.pallas import tpu as pltpu
from jax.sharding import Mesh, PartitionSpec as P

epsilon = 1e-06
RANK = ("seq_rank", "dp_rank")
EVERY = ("seq_block", "seq_rank", "dp_block", "dp_rank")
LANES = 128
HALO = 16
EXTRA = 16
VMEM = pl.BlockSpec(memory_space=pltpu.VMEM)
SMEM = pl.BlockSpec(memory_space=pltpu.SMEM)
HBM = pl.BlockSpec(memory_space=pltpu.HBM)
bf16 = jnp.bfloat16
f32 = jnp.float32


def called(body, outs, args, vmem, scratch=(), specs=None, out_specs=None):
    return pl.pallas_call(
        body,
        out_shape=outs,
        in_specs=specs or [VMEM] * len(args),
        out_specs=out_specs or jax.tree.map(lambda _: VMEM, outs),
        scratch_shapes=list(scratch),
        compiler_params=pltpu.CompilerParams(vmem_limit_bytes=vmem * 2**20),
        cost_estimate=pl.CostEstimate(flops=0, bytes_accessed=0, transcendentals=0),
    )(*args)


def shape_of(shape, dtype):
    return jax.ShapeDtypeStruct(shape, dtype)


def dot(a, b, contract):
    return lax.dot_general(a, b, (contract, ((), ())), preferred_element_type=f32)


def gelu_and_slope(x):
    inner = 0.7978845608028654 * (x + 0.044715 * (x * x * x))
    bend = jnp.tanh(inner)
    half_sum = 0.5 * (1.0 + bend)
    slope = half_sum + (0.5 * x) * (1.0 - bend * bend) * (
        0.7978845608028654 * (1.0 + 0.134145 * (x * x))
    )
    return x * half_sum, slope


def slot_maps(part, slots, pairing):
    shape = (slots, pairing.shape[1])
    slot = lax.broadcasted_iota(jnp.int32, shape, 0)
    lane = lax.bitwise_and(slot, LANES - 1)
    channel_of = jnp.where(lane < part, lax.div(slot, LANES) * part + lane, -1)
    channel = lax.broadcasted_iota(jnp.int32, shape, 1)
    return [jnp.where(channel_of == c, 1.0, 0.0).astype(bf16) for c in (channel, pairing)]


def swap_map(pairing):
    channels = pairing.shape[1]
    row = lax.broadcasted_iota(jnp.int32, (channels, channels), 0)
    return jnp.where(row == pairing, 1.0, 0.0).astype(bf16)


def chip_masks(ranks, core):
    return [mask for mask in range(ranks) if not mask & core]


class Moves:
    def __init__(self, sems):
        self.sems, self.copies = sems, []

    def start(self, source, target):
        copy = pltpu.make_async_copy(source, target, self.sems.at[len(self.copies)])
        copy.start()
        self.copies.append(copy)
        return copy

    def wait(self):
        for copy in self.copies:
            copy.wait()


def spread(piece_of, weights_ref, out_ref, square, sent, sems):
    rows, channels = weights_ref.shape
    part = out_ref.shape[1]
    square[...] = jnp.zeros_like(square)
    square[:rows] = weights_ref[...].astype(f32)
    turned = square[...].T.astype(bf16)
    for owner, piece in enumerate(piece_of):
        sent[owner] = turned[piece * part : (piece + 1) * part, :rows]
    moves = Moves(sems)
    moves.start(sent, out_ref)
    moves.wait()


def pack_messages(part, core, rank_ref, values_ref, cot_ref, edge_ref, pairing_ref, *outs):
    positions, channels = values_ref.shape
    home_ref, cross_ref, leaving = outs[0], outs[1], outs[2:]
    masks = chip_masks(2 * (len(leaving) + 1), core)
    flips = [mask | c for mask in masks[1:] for c in (core, 0)] + [0, core]
    shape = (part, channels)
    row = lax.broadcasted_iota(jnp.int32, shape, 0)
    column = lax.broadcasted_iota(jnp.int32, shape, 1)
    offsets = [column - row, pairing_ref[...] - row]
    maps = [
        jnp.where(offset == lax.bitwise_xor(rank_ref[0], flip) * part, 1.0, 0.0).astype(bf16)
        for flip in flips
        for offset in offsets
    ]
    maps = jnp.concatenate(maps, 0)
    for rows, kept, cot in (
        (slice(0, positions), values_ref[...], cot_ref[...]),
        (slice(positions, None), edge_ref[:, :channels], edge_ref[:, channels:]),
    ):
        slices = dot(cot, maps, ((1,), (1,))).astype(bf16)
        lane = 0
        for out in (*leaving, home_ref, cross_ref):
            count = out.shape[1] - channels
            out[rows, :channels] = kept
            out[rows, channels:] = slices[:, lane : lane + count]
            lane += count


def stack_crossing(*refs):
    out_ref = refs[-1]
    width = out_ref.shape[2]
    for m, ref in enumerate(refs[:-1]):
        out_ref[m] = ref[:, :width]


def normalize(x, gain, swap):
    other = dot(x, swap, ((1,), (0,)))
    x = x.astype(f32)
    rms = lax.rsqrt(jnp.mean(x * x, -1, keepdims=True) + epsilon)
    return [(t * rms * gain).astype(bf16) for t in (x, other)]


def main_body(core, chips, groups, rank_ref, pieces_in, home_in, *refs):
    arrived_in, refs = refs[: chips - 1], refs[chips - 1 :]
    crossed_in, refs = refs[:groups], refs[groups:]
    gain_ref, pairing_ref, leaving_out, cross_out, own_out = refs[:5]
    pieces, home, crossed, arrived, normed_ref, grads_ref, edge_normed_ref, edge_grads_ref = refs[5:13]
    padded, terms, halves, bent, slopes, total, shifted_ref, kernel_ref, gelu_ref = refs[13:22]
    scaled, leaving, cross, own, sems = refs[22:]
    owners, part, rows = pieces.shape
    strands = normed_ref.shape[0]
    dp_ranks = strands // 2
    moves = Moves(sems)
    got_blocks = [moves.start(home_in, home)]
    got_blocks += [moves.start(block, arrived.at[m]) for m, block in enumerate(arrived_in)]
    per = chips // groups
    got_blocks += [moves.start(crossed_in[m // per].at[m % per], crossed.at[m]) for m in range(chips)]
    got_pieces = moves.start(pieces_in, pieces)
    arrivals = len(moves.copies)
    masks = chip_masks(2 * chips, core)
    seq_ranks = 2 * chips // dp_ranks
    positions = home.shape[0] - HALO
    channels, width = gain_ref.shape[1], home.shape[1]
    swap = swap_map(pairing_ref[...])
    blocks = [(0, home, channels)]
    blocks += [(mask, arrived.at[m], width) for m, mask in enumerate(masks[1:])]
    blocks += [(mask | core, crossed.at[m], channels) for m, mask in enumerate(masks)]
    for got, (flip, ref, lane) in zip(got_blocks, blocks):
        got.wait()
        source = lax.bitwise_xor(rank_ref[0], flip)
        b, i = lax.rem(source, dp_ranks), lax.div(source, dp_ranks)
        start = pl.multiple_of(i * positions, positions)
        side = jnp.where(i == 0, 0, jnp.where(i == seq_ranks - 1, 1, 2))
        both = normalize(ref[:, :channels], gain_ref[...], swap)
        for n, normed in enumerate(both):
            first = lane + n * part
            grads = 0.5 * ref[:, first : first + part].astype(f32)
            index = n * dp_ranks + b
            normed_ref[index, pl.ds(start, positions), :] = normed[:positions]
            grads_ref[index, pl.ds(start, positions), :part] = grads[:positions]
            edge_normed_ref[side, index] = normed[positions:]
            edge_grads_ref[side, index, :, :part] = grads[positions:]
    span = normed_ref.shape[1]
    taps = kernel_ref.shape[0] // part
    half = taps // 2
    reach = 2 * half
    wide = bent.shape[0]

    def runs(owner):
        first, last = owner * rows, (owner + 1) * rows
        while first < last:
            tap, channel = divmod(first, channels)
            count = min(last - first, channels - channel)
            yield tap, channel, count, first - owner * rows
            first += count

    got_pieces.wait()
    for owner in range(owners):
        for tap, channel, count, offset in runs(owner):
            kernel_ref[tap * part : (tap + 1) * part, channel : channel + count] = pieces[
                owner, :, offset : offset + count
            ]
    padded[...] = jnp.zeros_like(padded)
    for k in range(taps):
        padded[k * LANES : k * LANES + part, :] = kernel_ref[k * part : (k + 1) * part, :]
    kernel = padded[...]
    edge_normed = jnp.concatenate([edge_normed_ref[side, s] for side in range(2) for s in range(strands)], 0)
    edge_terms = dot(edge_normed, kernel, ((1,), (1,)))
    for strand in range(strands):
        forward = strand < dp_ranks
        terms[HALO : HALO + span, :] = dot(normed_ref[strand], kernel, ((1,), (1,)))
        halves[HALO : HALO + span, :] = grads_ref[strand]
        for side, start in enumerate((0, HALO + span)):
            first = (side * strands + strand) * HALO
            terms[start : start + HALO, :] = edge_terms[first : first + HALO]
            halves[start : start + HALO, :] = edge_grads_ref[side, strand]
        preact = jnp.zeros((wide, LANES), f32)
        for k in range(taps):
            start = HALO - reach + k if forward else HALO - k
            preact += terms[start : start + wide, k * LANES : (k + 1) * LANES]
        result, slope = gelu_and_slope(preact)
        bent[...] = result
        gelu_ref[strand] = bent[half : half + span, :].astype(bf16)
        slopes[...] = halves[HALO - half : HALO - half + wide, :] * slope
        for k in range(taps):
            start = reach - k if forward else k
            shifted_ref[strand, :, k * part : (k + 1) * part] = slopes[start : start + span, :part].astype(bf16)
    total[...] = dot(
        shifted_ref[...].reshape(strands * span, taps * part),
        normed_ref[...].reshape(strands * span, channels),
        ((0,), (0,)),
    )
    gain = jnp.sum(total[...] * kernel_ref[...].astype(f32), 0, keepdims=True) / gain_ref[...]
    gain_high = gain.astype(bf16).astype(f32)
    row = lax.broadcasted_iota(jnp.int32, (EXTRA, channels), 0)
    extra = jnp.where(row == 0, gain_high, jnp.where(row == 1, gain - gain_high, 0.0))
    own_gain = channels // owners
    for owner in range(owners):
        for tap, channel, count, offset in runs(owner):
            leaving[owner, :part, offset : offset + count] = total[
                tap * part : (tap + 1) * part, channel : channel + count
            ].astype(bf16)
        leaving[owner, part:, :] = jnp.zeros((EXTRA, rows), bf16)
        leaving[owner, part:, :own_gain] = extra[
            :, owner * own_gain : (owner + 1) * own_gain
        ].astype(bf16)
    moves.start(leaving, leaving_out)
    kernel = kernel_ref[...]
    swapped = dot(kernel, swap, ((1,), (0,))).astype(bf16)
    gain = gain_ref[...]
    first = gain.astype(bf16).astype(f32)
    second = (gain - first).astype(bf16).astype(f32)
    third = gain - first - second
    parts = jnp.where(row == 0, first, jnp.where(row == 1, second, jnp.where(row == 2, third, 0.0)))
    swapped_gain = dot(parts.astype(bf16), swap, ((1,), (0,)))
    swapped_gain = swapped_gain[0:1] + swapped_gain[1:2] + swapped_gain[2:3]
    for b in range(dp_ranks):
        scaled[b] = (
            dot(shifted_ref[b], kernel, ((1,), (0,))) * gain
            + dot(shifted_ref[dp_ranks + b], swapped, ((1,), (0,))) * swapped_gain
        ).astype(bf16)
    for out, target_out, flip in ((cross, cross_out, core), (own, own_out, 0)):
        for m, mask in enumerate(masks):
            target = lax.bitwise_xor(rank_ref[0], mask | flip)
            b = lax.rem(target, dp_ranks)
            start = pl.multiple_of(lax.div(target, dp_ranks) * positions, positions)
            out[m, :, :channels] = scaled[b, pl.ds(start, positions), :]
            for n in range(2):
                lane = channels + n * LANES
                out[m, :, lane : lane + LANES] = gelu_ref[n * dp_ranks + b, pl.ds(start, positions), :]
        moves.start(out, target_out)
    for copy in moves.copies[arrivals:]:
        copy.wait()


def chip_sum(part, own_ref, crossed_ref, *outs):
    channels = own_ref.shape[2] - 2 * LANES
    for m, out in enumerate(outs):
        out[:, :channels] = (
            own_ref[m, :, :channels].astype(f32) + crossed_ref[m, :, :channels].astype(f32)
        ).astype(bf16)
        for c, ref in enumerate((own_ref, crossed_ref)):
            for n in range(2):
                lane = channels + n * LANES
                start = channels + (2 * c + n) * part
                out[:, start : start + part] = ref[m, :, lane : lane + part]


def finish(part, core, rank_ref, values_ref, cot_ref, pairing_ref, *refs):
    arrived, (combined_ref, grad_ref, gelus) = refs[:-3], refs[-3:]
    channels = values_ref.shape[1]
    ranks = gelus.shape[1]
    gelus[...] = jnp.zeros_like(gelus)
    scaled = jnp.zeros(values_ref.shape, f32)
    for mask, block in zip(chip_masks(ranks, core), arrived):
        scaled += block[:, :channels].astype(f32)
        for c in range(2):
            source = lax.bitwise_xor(rank_ref[0], mask | c * core)
            for n in range(2):
                start = channels + (2 * c + n) * part
                gelus[n, source, :, :part] = block[:, start : start + part]
    joined = [jnp.concatenate([gelus[n, j] for j in range(ranks)], -1) for n in range(2)]
    maps = slot_maps(part, ranks * LANES, pairing_ref[...])
    plain, other = [dot(j, m, ((1,), (0,))) for j, m in zip(joined, maps)]
    values = values_ref[...].astype(f32)
    rms = lax.rsqrt(jnp.mean(values * values, -1, keepdims=True) + epsilon)
    reverse_out = (values + other).astype(bf16).astype(f32)
    combined_ref[...] = (0.5 * (values + plain + reverse_out)).astype(bf16)
    along = jnp.mean(scaled * values, -1, keepdims=True)
    grad_ref[...] = (cot_ref[...].astype(f32) + rms * scaled - values * (rms * rms * rms * along)).astype(bf16)


def collect(owner_of, terms_ref, kernel_ref, gain_ref, joined):
    _, height, rows = terms_ref.shape
    part = height - EXTRA
    joined[...] = jnp.zeros_like(joined)
    gain = jnp.zeros((1, rows), f32)
    for rank, owners in enumerate(owner_of):
        total = terms_ref[owners[0]].astype(f32)
        for owner in owners[1:]:
            total += terms_ref[owner].astype(f32)
        joined[rank * part : (rank + 1) * part, :rows] = total[:part]
        gain += total[part : part + 1] + total[part + 1 : part + 2]
    kernel_ref[...] = joined[...].T[:rows]
    gain_ref[...] = gain[:, : gain_ref.shape[1]]


def flipped_pairs(count, mask):
    return [(i, i ^ mask) for i in range(count)]


def per_device(activations, cotangent, weights, norm_gain, pairing):
    seq_ranks = lax.axis_size("seq_rank")
    dp_ranks = lax.axis_size("dp_rank")
    seq_blocks = lax.axis_size("seq_block")
    dp_blocks = lax.axis_size("dp_block")
    ranks = seq_ranks * dp_ranks
    owners = ranks * seq_blocks * dp_blocks
    positions, channels = activations.shape[1:]
    rows = weights.shape[0]
    taps = rows * owners // channels
    part = channels // ranks
    span = positions * seq_ranks
    long = span + 2 * HALO
    reach = taps - taps % 2
    wide = -(-(span + reach) // 8) * 8
    strands = 2 * dp_ranks
    width = channels + 2 * LANES
    slim = channels + 2 * part
    rank = lax.axis_index(RANK).reshape(1)
    values, cot = activations[0], cotangent[0]
    along = ("seq_block", "seq_rank")
    ends = [(b * seq_ranks - 1, b * seq_ranks) for b in range(1, seq_blocks)]
    both = jnp.concatenate([values, cot], -1)
    edge = jnp.where(lax.axis_index("seq_rank") == 0, both[:HALO], both[-HALO:])
    edge = lax.ppermute(edge, along, ends + [(target, source) for source, target in ends])
    piece_of = [
        sr * dp_ranks + dr
        for _ in range(seq_blocks)
        for sr in range(seq_ranks)
        for _ in range(dp_blocks)
        for dr in range(dp_ranks)
    ]
    square = -(-rows // LANES) * LANES
    slices = called(
        lambda *refs: spread(piece_of, *refs),
        pltpu.HBM((owners, part, rows), bf16),
        (weights,),
        16,
        scratch=[
            pltpu.VMEM((square, channels), f32),
            pltpu.VMEM((owners, part, rows), bf16),
            pltpu.SemaphoreType.DMA((1,)),
        ],
        out_specs=HBM,
    )
    slices, packed = lax.optimization_barrier((slices, values))
    pieces = lax.all_to_all(slices, EVERY, 0, 0, tiled=True)
    pairing = pairing.reshape(1, channels)
    gain = norm_gain.reshape(1, channels)
    core = dp_ranks
    masks = chip_masks(ranks, core)
    block = positions + HALO
    home, cross, *leaving = called(
        lambda *refs: pack_messages(part, core, *refs),
        (pltpu.HBM((block, slim), bf16), shape_of((block, slim), bf16))
        + tuple(shape_of((block, slim + 2 * part), bf16) for _ in masks[1:]),
        (rank, packed, cot, edge, pairing),
        16,
        specs=[SMEM] + [VMEM] * 4,
    )
    arrived = [
        lax.ppermute(message, RANK, flipped_pairs(ranks, mask))
        for message, mask in zip(leaving, masks[1:])
    ]
    both_cores = []
    for first in range(0, len(masks), 2):
        group = (cross, *arrived)[first : first + 2]
        crossing = called(stack_crossing, shape_of((len(group), block, slim), bf16), group, 8)
        both_cores.append(lax.ppermute(crossing, RANK, flipped_pairs(ranks, core)))
    held = (pieces, home, *arrived, *both_cores)
    halves = (len(masks), positions, width)
    shapes = ((owners, part + EXTRA, rows), halves, halves)
    groups = len(both_cores)
    outgoing, cross, own = called(
        lambda *refs: main_body(core, len(masks), groups, *refs),
        tuple(pltpu.HBM(shape, bf16) for shape in shapes),
        (rank, *held, gain, pairing),
        44,
        scratch=[
            pltpu.VMEM(pieces.shape, bf16),
            pltpu.VMEM(home.shape, bf16),
            pltpu.VMEM((len(masks), block, slim), bf16),
            pltpu.VMEM((len(arrived), *arrived[0].shape), bf16),
            pltpu.VMEM((strands, span, channels), bf16),
            pltpu.VMEM((strands, span, LANES), f32),
            pltpu.VMEM((3, strands, HALO, channels), bf16),
            pltpu.VMEM((3, strands, HALO, LANES), f32),
            pltpu.VMEM((taps * LANES, channels), bf16),
            pltpu.VMEM((long, taps * LANES), f32),
            pltpu.VMEM((long, LANES), f32),
            pltpu.VMEM((wide, LANES), f32),
            pltpu.VMEM((wide, LANES), f32),
            pltpu.VMEM((taps * part, channels), f32),
            pltpu.VMEM((strands, span, taps * part), bf16),
            pltpu.VMEM((taps * part, channels), bf16),
            pltpu.VMEM((strands, span, LANES), bf16),
            pltpu.VMEM((dp_ranks, span, channels), bf16),
        ]
        + [pltpu.VMEM(shape, bf16) for shape in shapes]
        + [pltpu.SemaphoreType.DMA((ranks + 4,))],
        specs=[SMEM] + [pl.BlockSpec(memory_space=pl.ANY)] * len(held) + [VMEM] * 2,
        out_specs=(HBM,) * 3,
    )
    terms = lax.all_to_all(outgoing, EVERY, 0, 0, tiled=True)
    crossed = lax.ppermute(cross, RANK, flipped_pairs(ranks, core))
    leaving = called(
        lambda *refs: chip_sum(part, *refs),
        tuple(shape_of((positions, channels + 4 * part), bf16) for _ in masks),
        (own, crossed),
        8,
    )
    arrived = leaving[:1] + tuple(
        lax.ppermute(message, RANK, flipped_pairs(ranks, mask))
        for message, mask in zip(leaving[1:], masks[1:])
    )
    order = [
        [
            ((sb * seq_ranks + sr) * dp_blocks + db) * dp_ranks + dr
            for sb in range(seq_blocks)
            for db in range(dp_blocks)
        ]
        for sr in range(seq_ranks)
        for dr in range(dp_ranks)
    ]
    grad_kernel, grad_gain = called(
        lambda *refs: collect(order, *refs),
        (shape_of((rows, channels), f32), shape_of((1, channels // owners), f32)),
        (terms,),
        16,
        scratch=[pltpu.VMEM((channels, -(-rows // LANES) * LANES), f32)],
    )
    grad_kernel, home, *arrived = lax.optimization_barrier((grad_kernel, *arrived))
    combined, grad_input = called(
        lambda *refs: finish(part, core, *refs),
        (shape_of((positions, channels), bf16), shape_of((positions, channels), bf16)),
        (rank, values, cot, pairing, home, *arrived),
        16,
        scratch=[pltpu.VMEM((2, ranks, positions, LANES), bf16)],
        specs=[SMEM] + [VMEM] * (4 + len(arrived)),
    )
    return combined[None], grad_input[None], grad_kernel, grad_gain[0]


def solution(mesh):
    seq, dp = mesh.shape["seq"], mesh.shape["dp"]
    seq_ranks, dp_ranks = 4, 2
    grouped = Mesh(mesh.devices.reshape(seq // seq_ranks, seq_ranks, dp // dp_ranks, dp_ranks), EVERY)
    along = P(("dp_block", "dp_rank"), ("seq_block", "seq_rank"), None)
    return jax.shard_map(
        per_device,
        mesh=grouped,
        in_specs=(along, along, P(EVERY, None), P(), P()),
        out_specs=(along, along, P(EVERY, None), P(EVERY)),
        check_vma=False,
    )
```

```python
import jax
import jax.numpy as jnp
from jax import lax
from jax.experimental import pallas as pl
from jax.experimental.pallas import tpu as pltpu
from jax.sharding import Mesh, PartitionSpec as P

epsilon = 1e-06
RANK = ("seq_rank", "dp_rank")
EVERY = ("seq_block", "seq_rank", "dp_block", "dp_rank")
LANES = 128
HALO = 16
EXTRA = 16
VMEM = pl.BlockSpec(memory_space=pltpu.VMEM)
SMEM = pl.BlockSpec(memory_space=pltpu.SMEM)
HBM = pl.BlockSpec(memory_space=pltpu.HBM)
bf16 = jnp.bfloat16
f32 = jnp.float32


def called(body, outs, args, vmem, scratch=(), specs=None, out_specs=None):
    return pl.pallas_call(
        body,
        out_shape=outs,
        in_specs=specs or [VMEM] * len(args),
        out_specs=out_specs or jax.tree.map(lambda _: VMEM, outs),
        scratch_shapes=list(scratch),
        compiler_params=pltpu.CompilerParams(vmem_limit_bytes=vmem * 2**20),
        cost_estimate=pl.CostEstimate(flops=0, bytes_accessed=0, transcendentals=0),
    )(*args)


def shape_of(shape, dtype):
    return jax.ShapeDtypeStruct(shape, dtype)


def dot(a, b, contract):
    return lax.dot_general(a, b, (contract, ((), ())), preferred_element_type=f32)


def gelu_and_slope(x):
    inner = 0.7978845608028654 * (x + 0.044715 * (x * x * x))
    bend = jnp.tanh(inner)
    half_sum = 0.5 * (1.0 + bend)
    slope = half_sum + (0.5 * x) * (1.0 - bend * bend) * (
        0.7978845608028654 * (1.0 + 0.134145 * (x * x))
    )
    return x * half_sum, slope


def slot_maps(part, slots, pairing):
    shape = (slots, pairing.shape[1])
    slot = lax.broadcasted_iota(jnp.int32, shape, 0)
    lane = lax.bitwise_and(slot, LANES - 1)
    channel_of = jnp.where(lane < part, lax.div(slot, LANES) * part + lane, -1)
    channel = lax.broadcasted_iota(jnp.int32, shape, 1)
    return [jnp.where(channel_of == c, 1.0, 0.0).astype(bf16) for c in (channel, pairing)]


def swap_map(pairing):
    channels = pairing.shape[1]
    row = lax.broadcasted_iota(jnp.int32, (channels, channels), 0)
    return jnp.where(row == pairing, 1.0, 0.0).astype(bf16)


def chip_masks(ranks, core):
    return [mask for mask in range(ranks) if not mask & core]


class Moves:
    def __init__(self, sems):
        self.sems, self.copies = sems, []

    def start(self, source, target):
        copy = pltpu.make_async_copy(source, target, self.sems.at[len(self.copies)])
        copy.start()
        self.copies.append(copy)
        return copy

    def wait(self):
        for copy in self.copies:
            copy.wait()


def spread(piece_of, weights_ref, out_ref, square, sent, sems):
    rows, channels = weights_ref.shape
    part = out_ref.shape[1]
    square[...] = jnp.zeros_like(square)
    square[:rows] = weights_ref[...].astype(f32)
    turned = square[...].T.astype(bf16)
    for owner, piece in enumerate(piece_of):
        sent[owner] = turned[piece * part : (piece + 1) * part, :rows]
    moves = Moves(sems)
    moves.start(sent, out_ref)
    moves.wait()


def pack_messages(part, core, rank_ref, values_ref, cot_ref, edge_ref, pairing_ref, *outs):
    positions, channels = values_ref.shape
    home_ref, cross_ref, leaving = outs[0], outs[1], outs[2:]
    masks = chip_masks(2 * (len(leaving) + 1), core)
    flips = [mask | c for mask in masks[1:] for c in (core, 0)] + [0, core]
    shape = (part, channels)
    row = lax.broadcasted_iota(jnp.int32, shape, 0)
    column = lax.broadcasted_iota(jnp.int32, shape, 1)
    offsets = [column - row, pairing_ref[...] - row]
    maps = [
        jnp.where(offset == lax.bitwise_xor(rank_ref[0], flip) * part, 1.0, 0.0).astype(bf16)
        for flip in flips
        for offset in offsets
    ]
    maps = jnp.concatenate(maps, 0)
    for rows, kept, cot in (
        (slice(0, positions), values_ref[...], cot_ref[...]),
        (slice(positions, None), edge_ref[:, :channels], edge_ref[:, channels:]),
    ):
        slices = dot(cot, maps, ((1,), (1,))).astype(bf16)
        lane = 0
        for out in (*leaving, home_ref, cross_ref):
            count = out.shape[1] - channels
            out[rows, :channels] = kept
            out[rows, channels:] = slices[:, lane : lane + count]
            lane += count


def stack_crossing(*refs):
    out_ref = refs[-1]
    width = out_ref.shape[2]
    for m, ref in enumerate(refs[:-1]):
        out_ref[m] = ref[:, :width]


def normalize(x, gain, swap):
    other = dot(x, swap, ((1,), (0,)))
    x = x.astype(f32)
    rms = lax.rsqrt(jnp.mean(x * x, -1, keepdims=True) + epsilon)
    return [(t * rms * gain).astype(bf16) for t in (x, other)]


def main_body(core, chips, groups, rank_ref, pieces_in, home_in, *refs):
    arrived_in, refs = refs[: chips - 1], refs[chips - 1 :]
    crossed_in, refs = refs[:groups], refs[groups:]
    gain_ref, pairing_ref, leaving_out, cross_out, own_out = refs[:5]
    pieces, home, crossed, arrived, normed_ref, grads_ref, edge_normed_ref, edge_grads_ref = refs[5:13]
    padded, terms, halves, bent, slopes, total, shifted_ref, kernel_ref, gelu_ref = refs[13:22]
    scaled, leaving, cross, own, sems = refs[22:]
    owners, part, rows = pieces.shape
    strands = normed_ref.shape[0]
    dp_ranks = strands // 2
    moves = Moves(sems)
    got_blocks = [moves.start(home_in, home)]
    got_blocks += [moves.start(block, arrived.at[m]) for m, block in enumerate(arrived_in)]
    per = chips // groups
    got_blocks += [moves.start(crossed_in[m // per].at[m % per], crossed.at[m]) for m in range(chips)]
    got_pieces = moves.start(pieces_in, pieces)
    arrivals = len(moves.copies)
    masks = chip_masks(2 * chips, core)
    seq_ranks = 2 * chips // dp_ranks
    positions = home.shape[0] - HALO
    channels, width = gain_ref.shape[1], home.shape[1]
    swap = swap_map(pairing_ref[...])
    blocks = [(0, home, channels)]
    blocks += [(mask, arrived.at[m], width) for m, mask in enumerate(masks[1:])]
    blocks += [(mask | core, crossed.at[m], channels) for m, mask in enumerate(masks)]
    for got, (flip, ref, lane) in zip(got_blocks, blocks):
        got.wait()
        source = lax.bitwise_xor(rank_ref[0], flip)
        b, i = lax.rem(source, dp_ranks), lax.div(source, dp_ranks)
        start = pl.multiple_of(i * positions, positions)
        side = jnp.where(i == 0, 0, jnp.where(i == seq_ranks - 1, 1, 2))
        both = normalize(ref[:, :channels], gain_ref[...], swap)
        for n, normed in enumerate(both):
            first = lane + n * part
            grads = 0.5 * ref[:, first : first + part].astype(f32)
            index = n * dp_ranks + b
            normed_ref[index, pl.ds(start, positions), :] = normed[:positions]
            grads_ref[index, pl.ds(start, positions), :part] = grads[:positions]
            edge_normed_ref[side, index] = normed[positions:]
            edge_grads_ref[side, index, :, :part] = grads[positions:]
    span = normed_ref.shape[1]
    taps = kernel_ref.shape[0] // part
    half = taps // 2
    reach = 2 * half
    wide = bent.shape[0]

    def runs(owner):
        first, last = owner * rows, (owner + 1) * rows
        while first < last:
            tap, channel = divmod(first, channels)
            count = min(last - first, channels - channel)
            yield tap, channel, count, first - owner * rows
            first += count

    got_pieces.wait()
    for owner in range(owners):
        for tap, channel, count, offset in runs(owner):
            kernel_ref[tap * part : (tap + 1) * part, channel : channel + count] = pieces[
                owner, :, offset : offset + count
            ]
    padded[...] = jnp.zeros_like(padded)
    for k in range(taps):
        padded[k * LANES : k * LANES + part, :] = kernel_ref[k * part : (k + 1) * part, :]
    kernel = padded[...]
    edge_normed = jnp.concatenate([edge_normed_ref[side, s] for side in range(2) for s in range(strands)], 0)
    edge_terms = dot(edge_normed, kernel, ((1,), (1,)))
    for strand in range(strands):
        forward = strand < dp_ranks
        terms[HALO : HALO + span, :] = dot(normed_ref[strand], kernel, ((1,), (1,)))
        halves[HALO : HALO + span, :] = grads_ref[strand]
        for side, start in enumerate((0, HALO + span)):
            first = (side * strands + strand) * HALO
            terms[start : start + HALO, :] = edge_terms[first : first + HALO]
            halves[start : start + HALO, :] = edge_grads_ref[side, strand]
        preact = jnp.zeros((wide, LANES), f32)
        for k in range(taps):
            start = HALO - reach + k if forward else HALO - k
            preact += terms[start : start + wide, k * LANES : (k + 1) * LANES]
        result, slope = gelu_and_slope(preact)
        bent[...] = result
        gelu_ref[strand] = bent[half : half + span, :].astype(bf16)
        slopes[...] = halves[HALO - half : HALO - half + wide, :] * slope
        for k in range(taps):
            start = reach - k if forward else k
            shifted_ref[strand, :, k * part : (k + 1) * part] = slopes[start : start + span, :part].astype(bf16)
    total[...] = dot(
        shifted_ref[...].reshape(strands * span, taps * part),
        normed_ref[...].reshape(strands * span, channels),
        ((0,), (0,)),
    )
    gain = jnp.sum(total[...] * kernel_ref[...].astype(f32), 0, keepdims=True) / gain_ref[...]
    gain_high = gain.astype(bf16).astype(f32)
    row = lax.broadcasted_iota(jnp.int32, (EXTRA, channels), 0)
    extra = jnp.where(row == 0, gain_high, jnp.where(row == 1, gain - gain_high, 0.0))
    own_gain = channels // owners
    for owner in range(owners):
        for tap, channel, count, offset in runs(owner):
            leaving[owner, :part, offset : offset + count] = total[
                tap * part : (tap + 1) * part, channel : channel + count
            ].astype(bf16)
        leaving[owner, part:, :] = jnp.zeros((EXTRA, rows), bf16)
        leaving[owner, part:, :own_gain] = extra[
            :, owner * own_gain : (owner + 1) * own_gain
        ].astype(bf16)
    moves.start(leaving, leaving_out)
    kernel = kernel_ref[...]
    swapped = dot(kernel, swap, ((1,), (0,))).astype(bf16)
    gain = gain_ref[...]
    first = gain.astype(bf16).astype(f32)
    second = (gain - first).astype(bf16).astype(f32)
    third = gain - first - second
    parts = jnp.where(row == 0, first, jnp.where(row == 1, second, jnp.where(row == 2, third, 0.0)))
    swapped_gain = dot(parts.astype(bf16), swap, ((1,), (0,)))
    swapped_gain = swapped_gain[0:1] + swapped_gain[1:2] + swapped_gain[2:3]
    for b in range(dp_ranks):
        scaled[b] = (
            dot(shifted_ref[b], kernel, ((1,), (0,))) * gain
            + dot(shifted_ref[dp_ranks + b], swapped, ((1,), (0,))) * swapped_gain
        ).astype(bf16)
    for out, target_out, flip in ((cross, cross_out, core), (own, own_out, 0)):
        for m, mask in enumerate(masks):
            target = lax.bitwise_xor(rank_ref[0], mask | flip)
            b = lax.rem(target, dp_ranks)
            start = pl.multiple_of(lax.div(target, dp_ranks) * positions, positions)
            out[m, :, :channels] = scaled[b, pl.ds(start, positions), :]
            for n in range(2):
                lane = channels + n * LANES
                out[m, :, lane : lane + LANES] = gelu_ref[n * dp_ranks + b, pl.ds(start, positions), :]
        moves.start(out, target_out)
    for copy in moves.copies[arrivals:]:
        copy.wait()


def chip_sum(part, own_ref, crossed_ref, *outs):
    channels = own_ref.shape[2] - 2 * LANES
    for m, out in enumerate(outs):
        out[:, :channels] = (
            own_ref[m, :, :channels].astype(f32) + crossed_ref[m, :, :channels].astype(f32)
        ).astype(bf16)
        for c, ref in enumerate((own_ref, crossed_ref)):
            for n in range(2):
                lane = channels + n * LANES
                start = channels + (2 * c + n) * part
                out[:, start : start + part] = ref[m, :, lane : lane + part]


def finish(part, core, rank_ref, values_ref, cot_ref, pairing_ref, *refs):
    arrived, (combined_ref, grad_ref, gelus) = refs[:-3], refs[-3:]
    channels = values_ref.shape[1]
    ranks = gelus.shape[1]
    gelus[...] = jnp.zeros_like(gelus)
    scaled = jnp.zeros(values_ref.shape, f32)
    for mask, block in zip(chip_masks(ranks, core), arrived):
        scaled += block[:, :channels].astype(f32)
        for c in range(2):
            source = lax.bitwise_xor(rank_ref[0], mask | c * core)
            for n in range(2):
                start = channels + (2 * c + n) * part
                gelus[n, source, :, :part] = block[:, start : start + part]
    joined = [jnp.concatenate([gelus[n, j] for j in range(ranks)], -1) for n in range(2)]
    maps = slot_maps(part, ranks * LANES, pairing_ref[...])
    plain, other = [dot(j, m, ((1,), (0,))) for j, m in zip(joined, maps)]
    values = values_ref[...].astype(f32)
    rms = lax.rsqrt(jnp.mean(values * values, -1, keepdims=True) + epsilon)
    reverse_out = (values + other).astype(bf16).astype(f32)
    combined_ref[...] = (0.5 * (values + plain + reverse_out)).astype(bf16)
    along = jnp.mean(scaled * values, -1, keepdims=True)
    grad_ref[...] = (cot_ref[...].astype(f32) + rms * scaled - values * (rms * rms * rms * along)).astype(bf16)


def collect(owner_of, terms_ref, kernel_ref, gain_ref, joined):
    _, height, rows = terms_ref.shape
    part = height - EXTRA
    joined[...] = jnp.zeros_like(joined)
    gain = jnp.zeros((1, rows), f32)
    for rank, owners in enumerate(owner_of):
        total = terms_ref[owners[0]].astype(f32)
        for owner in owners[1:]:
            total += terms_ref[owner].astype(f32)
        joined[rank * part : (rank + 1) * part, :rows] = total[:part]
        gain += total[part : part + 1] + total[part + 1 : part + 2]
    kernel_ref[...] = joined[...].T[:rows]
    gain_ref[...] = gain[:, : gain_ref.shape[1]]


def flipped_pairs(count, mask):
    return [(i, i ^ mask) for i in range(count)]


def per_device(activations, cotangent, weights, norm_gain, pairing):
    seq_ranks = lax.axis_size("seq_rank")
    dp_ranks = lax.axis_size("dp_rank")
    seq_blocks = lax.axis_size("seq_block")
    dp_blocks = lax.axis_size("dp_block")
    ranks = seq_ranks * dp_ranks
    owners = ranks * seq_blocks * dp_blocks
    positions, channels = activations.shape[1:]
    rows = weights.shape[0]
    taps = rows * owners // channels
    part = channels // ranks
    span = positions * seq_ranks
    long = span + 2 * HALO
    reach = taps - taps % 2
    wide = -(-(span + reach) // 8) * 8
    strands = 2 * dp_ranks
    width = channels + 2 * LANES
    slim = channels + 2 * part
    rank = lax.axis_index(RANK).reshape(1)
    values, cot = activations[0], cotangent[0]
    along = ("seq_block", "seq_rank")
    ends = [(b * seq_ranks - 1, b * seq_ranks) for b in range(1, seq_blocks)]
    both = jnp.concatenate([values, cot], -1)
    edge = jnp.where(lax.axis_index("seq_rank") == 0, both[:HALO], both[-HALO:])
    edge = lax.ppermute(edge, along, ends + [(target, source) for source, target in ends])
    piece_of = [
        sr * dp_ranks + dr
        for _ in range(seq_blocks)
        for sr in range(seq_ranks)
        for _ in range(dp_blocks)
        for dr in range(dp_ranks)
    ]
    square = -(-rows // LANES) * LANES
    slices = called(
        lambda *refs: spread(piece_of, *refs),
        pltpu.HBM((owners, part, rows), bf16),
        (weights,),
        16,
        scratch=[
            pltpu.VMEM((square, channels), f32),
            pltpu.VMEM((owners, part, rows), bf16),
            pltpu.SemaphoreType.DMA((1,)),
        ],
        out_specs=HBM,
    )
    slices, edge, packed = lax.optimization_barrier((slices, edge, values))
    pieces = lax.all_to_all(slices, EVERY, 0, 0, tiled=True)
    pairing = pairing.reshape(1, channels)
    gain = norm_gain.reshape(1, channels)
    core = dp_ranks
    masks = chip_masks(ranks, core)
    block = positions + HALO
    home, cross, *leaving = called(
        lambda *refs: pack_messages(part, core, *refs),
        (pltpu.HBM((block, slim), bf16), shape_of((block, slim), bf16))
        + tuple(shape_of((block, slim + 2 * part), bf16) for _ in masks[1:]),
        (rank, packed, cot, edge, pairing),
        16,
        specs=[SMEM] + [VMEM] * 4,
    )
    arrived = [
        lax.ppermute(message, RANK, flipped_pairs(ranks, mask))
        for message, mask in zip(leaving, masks[1:])
    ]
    both_cores = []
    for first in range(0, len(masks), 2):
        group = (cross, *arrived)[first : first + 2]
        crossing = called(stack_crossing, shape_of((len(group), block, slim), bf16), group, 8)
        both_cores.append(lax.ppermute(crossing, RANK, flipped_pairs(ranks, core)))
    held = (pieces, home, *arrived, *both_cores)
    halves = (len(masks), positions, width)
    shapes = ((owners, part + EXTRA, rows), halves, halves)
    groups = len(both_cores)
    outgoing, cross, own = called(
        lambda *refs: main_body(core, len(masks), groups, *refs),
        tuple(pltpu.HBM(shape, bf16) for shape in shapes),
        (rank, *held, gain, pairing),
        44,
        scratch=[
            pltpu.VMEM(pieces.shape, bf16),
            pltpu.VMEM(home.shape, bf16),
            pltpu.VMEM((len(masks), block, slim), bf16),
            pltpu.VMEM((len(arrived), *arrived[0].shape), bf16),
            pltpu.VMEM((strands, span, channels), bf16),
            pltpu.VMEM((strands, span, LANES), f32),
            pltpu.VMEM((3, strands, HALO, channels), bf16),
            pltpu.VMEM((3, strands, HALO, LANES), f32),
            pltpu.VMEM((taps * LANES, channels), bf16),
            pltpu.VMEM((long, taps * LANES), f32),
            pltpu.VMEM((long, LANES), f32),
            pltpu.VMEM((wide, LANES), f32),
            pltpu.VMEM((wide, LANES), f32),
            pltpu.VMEM((taps * part, channels), f32),
            pltpu.VMEM((strands, span, taps * part), bf16),
            pltpu.VMEM((taps * part, channels), bf16),
            pltpu.VMEM((strands, span, LANES), bf16),
            pltpu.VMEM((dp_ranks, span, channels), bf16),
        ]
        + [pltpu.VMEM(shape, bf16) for shape in shapes]
        + [pltpu.SemaphoreType.DMA((ranks + 4,))],
        specs=[SMEM] + [pl.BlockSpec(memory_space=pl.ANY)] * len(held) + [VMEM] * 2,
        out_specs=(HBM,) * 3,
    )
    terms = lax.all_to_all(outgoing, EVERY, 0, 0, tiled=True)
    crossed = lax.ppermute(cross, RANK, flipped_pairs(ranks, core))
    leaving = called(
        lambda *refs: chip_sum(part, *refs),
        tuple(shape_of((positions, channels + 4 * part), bf16) for _ in masks),
        (own, crossed),
        8,
    )
    arrived = leaving[:1] + tuple(
        lax.ppermute(message, RANK, flipped_pairs(ranks, mask))
        for message, mask in zip(leaving[1:], masks[1:])
    )
    order = [
        [
            ((sb * seq_ranks + sr) * dp_blocks + db) * dp_ranks + dr
            for sb in range(seq_blocks)
            for db in range(dp_blocks)
        ]
        for sr in range(seq_ranks)
        for dr in range(dp_ranks)
    ]
    grad_kernel, grad_gain = called(
        lambda *refs: collect(order, *refs),
        (shape_of((rows, channels), f32), shape_of((1, channels // owners), f32)),
        (terms,),
        16,
        scratch=[pltpu.VMEM((channels, -(-rows // LANES) * LANES), f32)],
    )
    grad_kernel, home, *arrived = lax.optimization_barrier((grad_kernel, *arrived))
    combined, grad_input = called(
        lambda *refs: finish(part, core, *refs),
        (shape_of((positions, channels), bf16), shape_of((positions, channels), bf16)),
        (rank, values, cot, pairing, home, *arrived),
        16,
        scratch=[pltpu.VMEM((2, ranks, positions, LANES), bf16)],
        specs=[SMEM] + [VMEM] * (4 + len(arrived)),
    )
    return combined[None], grad_input[None], grad_kernel, grad_gain[0]


def solution(mesh):
    seq, dp = mesh.shape["seq"], mesh.shape["dp"]
    seq_ranks, dp_ranks = 4, 2
    grouped = Mesh(mesh.devices.reshape(seq // seq_ranks, seq_ranks, dp // dp_ranks, dp_ranks), EVERY)
    along = P(("dp_block", "dp_rank"), ("seq_block", "seq_rank"), None)
    return jax.shard_map(
        per_device,
        mesh=grouped,
        in_specs=(along, along, P(EVERY, None), P(), P()),
        out_specs=(along, along, P(EVERY, None), P(EVERY)),
        check_vma=False,
    )
```

```python
import jax
import jax.numpy as jnp
from jax import lax
from jax.experimental import pallas as pl
from jax.experimental.pallas import tpu as pltpu
from jax.sharding import Mesh, PartitionSpec as P

epsilon = 1e-06
RANK = ("seq_rank", "dp_rank")
EVERY = ("seq_block", "seq_rank", "dp_block", "dp_rank")
LANES = 128
HALO = 16
EXTRA = 2
VMEM = pl.BlockSpec(memory_space=pltpu.VMEM)
SMEM = pl.BlockSpec(memory_space=pltpu.SMEM)
HBM = pl.BlockSpec(memory_space=pltpu.HBM)
ANY = pl.BlockSpec(memory_space=pl.ANY)
bf16 = jnp.bfloat16
f32 = jnp.float32


def called(body, outs, args, vmem, scratch=(), specs=None, out_specs=None):
    return pl.pallas_call(
        body,
        out_shape=outs,
        in_specs=specs or [VMEM] * len(args),
        out_specs=out_specs or jax.tree.map(lambda _: VMEM, outs),
        scratch_shapes=list(scratch),
        compiler_params=pltpu.CompilerParams(vmem_limit_bytes=vmem * 2**20),
        cost_estimate=pl.CostEstimate(flops=0, bytes_accessed=0, transcendentals=0),
    )(*args)


def shape_of(shape, dtype):
    return jax.ShapeDtypeStruct(shape, dtype)


def dot(a, b, contract):
    return lax.dot_general(a, b, (contract, ((), ())), preferred_element_type=f32)


def gelu_and_slope(x):
    inner = 0.7978845608028654 * (x + 0.044715 * (x * x * x))
    bend = jnp.tanh(inner)
    half_sum = 0.5 * (1.0 + bend)
    slope = half_sum + (0.5 * x) * (1.0 - bend * bend) * (
        0.7978845608028654 * (1.0 + 0.134145 * (x * x))
    )
    return x * half_sum, slope


def slot_maps(part, slots, pairing):
    shape = (slots, pairing.shape[1])
    slot = lax.broadcasted_iota(jnp.int32, shape, 0)
    lane = lax.bitwise_and(slot, LANES - 1)
    channel_of = jnp.where(lane < part, lax.div(slot, LANES) * part + lane, -1)
    channel = lax.broadcasted_iota(jnp.int32, shape, 1)
    return [jnp.where(channel_of == c, 1.0, 0.0).astype(bf16) for c in (channel, pairing)]


def swap_map(pairing):
    channels = pairing.shape[1]
    row = lax.broadcasted_iota(jnp.int32, (channels, channels), 0)
    return jnp.where(row == pairing, 1.0, 0.0).astype(bf16)


def chip_masks(ranks, core):
    return [mask for mask in range(ranks) if not mask & core]


class Moves:
    def __init__(self, sems):
        self.sems, self.copies = sems, []

    def start(self, source, target):
        copy = pltpu.make_async_copy(source, target, self.sems.at[len(self.copies)])
        copy.start()
        self.copies.append(copy)
        return copy

    def wait(self):
        for copy in self.copies:
            copy.wait()


def spread(piece_of, weights_ref, out_ref, square, sent, sems):
    rows, channels = weights_ref.shape
    part = out_ref.shape[1]
    square[...] = jnp.zeros_like(square)
    square[:rows] = weights_ref[...].astype(f32)
    turned = square[...].T.astype(bf16)
    for owner, piece in enumerate(piece_of):
        sent[owner] = turned[piece * part : (piece + 1) * part, :rows]
    moves = Moves(sems)
    moves.start(sent, out_ref)
    moves.wait()


def pack_messages(part, core, rank_ref, values_ref, cot_ref, edge_ref, pairing_ref, *outs):
    positions, channels = values_ref.shape
    home_ref, cross_ref, leaving = outs[0], outs[1], outs[2:]
    masks = chip_masks(2 * (len(leaving) + 1), core)
    flips = [mask | c for mask in masks[1:] for c in (core, 0)] + [0, core]
    shape = (part, channels)
    row = lax.broadcasted_iota(jnp.int32, shape, 0)
    column = lax.broadcasted_iota(jnp.int32, shape, 1)
    offsets = [column - row, pairing_ref[...] - row]
    maps = [
        jnp.where(offset == lax.bitwise_xor(rank_ref[0], flip) * part, 1.0, 0.0).astype(bf16)
        for flip in flips
        for offset in offsets
    ]
    maps = jnp.concatenate(maps, 0)
    for rows, kept, cot in (
        (slice(0, positions), values_ref[...], cot_ref[...]),
        (slice(positions, None), edge_ref[:, :channels], edge_ref[:, channels:]),
    ):
        slices = dot(cot, maps, ((1,), (1,))).astype(bf16)
        lane = 0
        for out in (*leaving, home_ref, cross_ref):
            count = out.shape[1] - channels
            out[rows, :channels] = kept
            out[rows, channels:] = slices[:, lane : lane + count]
            lane += count


def stack_crossing(*refs):
    out_ref = refs[-1]
    width = out_ref.shape[2]
    for m, ref in enumerate(refs[:-1]):
        out_ref[m] = ref[:, :width]


def normalize(x, gain, swap):
    other = dot(x, swap, ((1,), (0,)))
    x = x.astype(f32)
    rms = lax.rsqrt(jnp.mean(x * x, -1, keepdims=True) + epsilon)
    return [(t * rms * gain).astype(bf16) for t in (x, other)]


def main_body(core, chips, groups, rank_ref, pieces_in, home_in, *refs):
    arrived_in, refs = refs[: chips - 1], refs[chips - 1 :]
    crossed_in, refs = refs[:groups], refs[groups:]
    gain_ref, pairing_ref, leaving_out, cross_out, own_out = refs[:5]
    pieces, home, crossed, arrived, normed_ref, grads_ref, edge_normed_ref, edge_grads_ref = refs[5:13]
    padded, terms, halves, bent, slopes, total, shifted_ref, kernel_ref, gelu_ref = refs[13:22]
    scaled, leaving, cross, own, sems = refs[22:]
    owners, part, rows = pieces.shape
    strands = normed_ref.shape[0]
    dp_ranks = strands // 2
    moves = Moves(sems)
    got_blocks = [moves.start(home_in, home)]
    got_blocks += [moves.start(block, arrived.at[m]) for m, block in enumerate(arrived_in)]
    per = chips // groups
    got_blocks += [moves.start(crossed_in[m // per].at[m % per], crossed.at[m]) for m in range(chips)]
    got_pieces = moves.start(pieces_in, pieces)
    arrivals = len(moves.copies)
    masks = chip_masks(2 * chips, core)
    seq_ranks = 2 * chips // dp_ranks
    positions = home.shape[0] - HALO
    channels, width = gain_ref.shape[1], home.shape[1]
    swap = swap_map(pairing_ref[...])
    blocks = [(0, home, channels)]
    blocks += [(mask, arrived.at[m], width) for m, mask in enumerate(masks[1:])]
    blocks += [(mask | core, crossed.at[m], channels) for m, mask in enumerate(masks)]
    for got, (flip, ref, lane) in zip(got_blocks, blocks):
        got.wait()
        source = lax.bitwise_xor(rank_ref[0], flip)
        b, i = lax.rem(source, dp_ranks), lax.div(source, dp_ranks)
        start = pl.multiple_of(i * positions, positions)
        side = jnp.where(i == 0, 0, jnp.where(i == seq_ranks - 1, 1, 2))
        both = normalize(ref[:, :channels], gain_ref[...], swap)
        for n, normed in enumerate(both):
            first = lane + n * part
            grads = 0.5 * ref[:, first : first + part].astype(f32)
            index = n * dp_ranks + b
            normed_ref[index, pl.ds(start, positions), :] = normed[:positions]
            grads_ref[index, pl.ds(start, positions), :part] = grads[:positions]
            edge_normed_ref[side, index] = normed[positions:]
            edge_grads_ref[side, index, :, :part] = grads[positions:]
    span = normed_ref.shape[1]
    taps = kernel_ref.shape[0] // part
    half = taps // 2
    reach = 2 * half
    wide = bent.shape[0]

    def runs(owner):
        first, last = owner * rows, (owner + 1) * rows
        while first < last:
            tap, channel = divmod(first, channels)
            count = min(last - first, channels - channel)
            yield tap, channel, count, first - owner * rows
            first += count

    got_pieces.wait()
    for owner in range(owners):
        for tap, channel, count, offset in runs(owner):
            kernel_ref[tap * part : (tap + 1) * part, channel : channel + count] = pieces[
                owner, :, offset : offset + count
            ]
    padded[...] = jnp.zeros_like(padded)
    for k in range(taps):
        padded[k * LANES : k * LANES + part, :] = kernel_ref[k * part : (k + 1) * part, :]
    kernel = padded[...]
    edge_normed = jnp.concatenate([edge_normed_ref[side, s] for side in range(2) for s in range(strands)], 0)
    edge_terms = dot(edge_normed, kernel, ((1,), (1,)))
    for strand in range(strands):
        forward = strand < dp_ranks
        terms[HALO : HALO + span, :] = dot(normed_ref[strand], kernel, ((1,), (1,)))
        halves[HALO : HALO + span, :] = grads_ref[strand]
        for side, start in enumerate((0, HALO + span)):
            first = (side * strands + strand) * HALO
            terms[start : start + HALO, :] = edge_terms[first : first + HALO]
            halves[start : start + HALO, :] = edge_grads_ref[side, strand]
        preact = jnp.zeros((wide, LANES), f32)
        for k in range(taps):
            start = HALO - reach + k if forward else HALO - k
            preact += terms[start : start + wide, k * LANES : (k + 1) * LANES]
        result, slope = gelu_and_slope(preact)
        bent[...] = result
        gelu_ref[strand] = bent[half : half + span, :].astype(bf16)
        slopes[...] = halves[HALO - half : HALO - half + wide, :] * slope
        for k in range(taps):
            start = reach - k if forward else k
            shifted_ref[strand, :, k * part : (k + 1) * part] = slopes[start : start + span, :part].astype(bf16)
    total[...] = dot(
        shifted_ref[...].reshape(strands * span, taps * part),
        normed_ref[...].reshape(strands * span, channels),
        ((0,), (0,)),
    )
    gain = jnp.sum(total[...] * kernel_ref[...].astype(f32), 0, keepdims=True) / gain_ref[...]
    gain_high = gain.astype(bf16).astype(f32)
    row = lax.broadcasted_iota(jnp.int32, (HALO, channels), 0)
    extra = jnp.where(row == 0, gain_high, jnp.where(row == 1, gain - gain_high, 0.0)).T
    own_gain = channels // owners
    for owner in range(owners):
        for tap, channel, count, offset in runs(owner):
            leaving[owner, :, offset : offset + count] = total[
                tap * part : (tap + 1) * part, channel : channel + count
            ].astype(bf16)
        leaving[owner, :, rows:] = jnp.zeros((part, EXTRA), bf16)
        leaving[owner, :own_gain, rows:] = extra[
            owner * own_gain : (owner + 1) * own_gain, :EXTRA
        ].astype(bf16)
    moves.start(leaving, leaving_out)
    kernel = kernel_ref[...]
    swapped = dot(kernel, swap, ((1,), (0,))).astype(bf16)
    gain = gain_ref[...]
    first = gain.astype(bf16).astype(f32)
    second = (gain - first).astype(bf16).astype(f32)
    third = gain - first - second
    parts = jnp.where(row == 0, first, jnp.where(row == 1, second, jnp.where(row == 2, third, 0.0)))
    swapped_gain = dot(parts.astype(bf16), swap, ((1,), (0,)))
    swapped_gain = swapped_gain[0:1] + swapped_gain[1:2] + swapped_gain[2:3]
    for b in range(dp_ranks):
        scaled[b] = (
            dot(shifted_ref[b], kernel, ((1,), (0,))) * gain
            + dot(shifted_ref[dp_ranks + b], swapped, ((1,), (0,))) * swapped_gain
        ).astype(bf16)
    for out, target_out, flip in ((cross, cross_out, core), (own, own_out, 0)):
        for m, mask in enumerate(masks):
            target = lax.bitwise_xor(rank_ref[0], mask | flip)
            b = lax.rem(target, dp_ranks)
            start = pl.multiple_of(lax.div(target, dp_ranks) * positions, positions)
            out[m, :, :channels] = scaled[b, pl.ds(start, positions), :]
            for n in range(2):
                lane = channels + n * LANES
                out[m, :, lane : lane + LANES] = gelu_ref[n * dp_ranks + b, pl.ds(start, positions), :]
        moves.start(out, target_out)
    for copy in moves.copies[arrivals:]:
        copy.wait()


def chip_sum(part, own_ref, crossed_ref, *outs):
    channels = own_ref.shape[2] - 2 * LANES
    for m, out in enumerate(outs):
        out[:, :channels] = (
            own_ref[m, :, :channels].astype(f32) + crossed_ref[m, :, :channels].astype(f32)
        ).astype(bf16)
        for c, ref in enumerate((own_ref, crossed_ref)):
            for n in range(2):
                lane = channels + n * LANES
                start = channels + (2 * c + n) * part
                out[:, start : start + part] = ref[m, :, lane : lane + part]


def finish(part, core, rank_ref, values_ref, cot_ref, pairing_ref, *refs):
    arrived, (combined_ref, grad_ref, gelus) = refs[:-3], refs[-3:]
    channels = values_ref.shape[1]
    ranks = gelus.shape[1]
    gelus[...] = jnp.zeros_like(gelus)
    scaled = jnp.zeros(values_ref.shape, f32)
    for mask, block in zip(chip_masks(ranks, core), arrived):
        scaled += block[:, :channels].astype(f32)
        for c in range(2):
            source = lax.bitwise_xor(rank_ref[0], mask | c * core)
            for n in range(2):
                start = channels + (2 * c + n) * part
                gelus[n, source, :, :part] = block[:, start : start + part]
    joined = [jnp.concatenate([gelus[n, j] for j in range(ranks)], -1) for n in range(2)]
    maps = slot_maps(part, ranks * LANES, pairing_ref[...])
    plain, other = [dot(j, m, ((1,), (0,))) for j, m in zip(joined, maps)]
    values = values_ref[...].astype(f32)
    rms = lax.rsqrt(jnp.mean(values * values, -1, keepdims=True) + epsilon)
    reverse_out = (values + other).astype(bf16).astype(f32)
    combined_ref[...] = (0.5 * (values + plain + reverse_out)).astype(bf16)
    along = jnp.mean(scaled * values, -1, keepdims=True)
    grad_ref[...] = (cot_ref[...].astype(f32) + rms * scaled - values * (rms * rms * rms * along)).astype(bf16)


def collect(owner_of, terms_ref, kernel_ref, gain_ref, joined):
    part = terms_ref.shape[1]
    rows = kernel_ref.shape[0]
    own_gain = gain_ref.shape[0]
    joined[...] = jnp.zeros_like(joined)
    gain = jnp.zeros((own_gain, EXTRA), f32)
    for rank, owners in enumerate(owner_of):
        total = terms_ref[owners[0]].astype(f32)
        for owner in owners[1:]:
            total += terms_ref[owner].astype(f32)
        joined[rank * part : (rank + 1) * part, :rows] = total[:, :rows]
        gain += total[:own_gain, rows:]
    kernel_ref[...] = joined[...].T[:rows]
    gain_ref[...] = jnp.sum(gain, -1, keepdims=True)


def flipped_pairs(count, mask):
    return [(i, i ^ mask) for i in range(count)]


def per_device(activations, cotangent, weights, norm_gain, pairing):
    seq_ranks = lax.axis_size("seq_rank")
    dp_ranks = lax.axis_size("dp_rank")
    seq_blocks = lax.axis_size("seq_block")
    dp_blocks = lax.axis_size("dp_block")
    ranks = seq_ranks * dp_ranks
    owners = ranks * seq_blocks * dp_blocks
    positions, channels = activations.shape[1:]
    rows = weights.shape[0]
    taps = rows * owners // channels
    part = channels // ranks
    span = positions * seq_ranks
    long = span + 2 * HALO
    reach = taps - taps % 2
    wide = -(-(span + reach) // 8) * 8
    strands = 2 * dp_ranks
    width = channels + 2 * LANES
    slim = channels + 2 * part
    rank = lax.axis_index(RANK).reshape(1)
    values, cot = activations[0], cotangent[0]
    along = ("seq_block", "seq_rank")
    ends = [(b * seq_ranks - 1, b * seq_ranks) for b in range(1, seq_blocks)]
    both = jnp.concatenate([values, cot], -1)
    edge = jnp.where(lax.axis_index("seq_rank") == 0, both[:HALO], both[-HALO:])
    edge = lax.ppermute(edge, along, ends + [(target, source) for source, target in ends])
    piece_of = [
        sr * dp_ranks + dr
        for _ in range(seq_blocks)
        for sr in range(seq_ranks)
        for _ in range(dp_blocks)
        for dr in range(dp_ranks)
    ]
    square = -(-rows // LANES) * LANES
    slices = called(
        lambda *refs: spread(piece_of, *refs),
        pltpu.HBM((owners, part, rows), bf16),
        (weights,),
        16,
        scratch=[
            pltpu.VMEM((square, channels), f32),
            pltpu.VMEM((owners, part, rows), bf16),
            pltpu.SemaphoreType.DMA((1,)),
        ],
        out_specs=HBM,
    )
    slices, packed = lax.optimization_barrier((slices, values))
    pieces = lax.all_to_all(slices, EVERY, 0, 0, tiled=True)
    pairing = pairing.reshape(1, channels)
    gain = norm_gain.reshape(1, channels)
    core = dp_ranks
    masks = chip_masks(ranks, core)
    block = positions + HALO
    home, cross, *leaving = called(
        lambda *refs: pack_messages(part, core, *refs),
        (pltpu.HBM((block, slim), bf16), shape_of((block, slim), bf16))
        + tuple(shape_of((block, slim + 2 * part), bf16) for _ in masks[1:]),
        (rank, packed, cot, edge, pairing),
        16,
        specs=[SMEM] + [VMEM] * 4,
    )
    arrived = [
        lax.ppermute(message, RANK, flipped_pairs(ranks, mask))
        for message, mask in zip(leaving, masks[1:])
    ]
    both_cores = []
    for group in ((cross, *arrived),):
        crossing = called(stack_crossing, shape_of((len(group), block, slim), bf16), group, 8)
        both_cores.append(lax.ppermute(crossing, RANK, flipped_pairs(ranks, core)))
    home = pltpu.with_memory_space_constraint(home, pltpu.HBM)
    held = (pieces, home, *arrived, *both_cores)
    halves = (len(masks), positions, width)
    shapes = ((owners, part, rows + EXTRA), halves, halves)
    groups = len(both_cores)
    outgoing, cross, own = called(
        lambda *refs: main_body(core, len(masks), groups, *refs),
        tuple(pltpu.HBM(shape, bf16) for shape in shapes),
        (rank, *held, gain, pairing),
        44,
        scratch=[
            pltpu.VMEM(pieces.shape, bf16),
            pltpu.VMEM(home.shape, bf16),
            pltpu.VMEM((len(masks), block, slim), bf16),
            pltpu.VMEM((len(arrived), *arrived[0].shape), bf16),
            pltpu.VMEM((strands, span, channels), bf16),
            pltpu.VMEM((strands, span, LANES), f32),
            pltpu.VMEM((3, strands, HALO, channels), bf16),
            pltpu.VMEM((3, strands, HALO, LANES), f32),
            pltpu.VMEM((taps * LANES, channels), bf16),
            pltpu.VMEM((long, taps * LANES), f32),
            pltpu.VMEM((long, LANES), f32),
            pltpu.VMEM((wide, LANES), f32),
            pltpu.VMEM((wide, LANES), f32),
            pltpu.VMEM((taps * part, channels), f32),
            pltpu.VMEM((strands, span, taps * part), bf16),
            pltpu.VMEM((taps * part, channels), bf16),
            pltpu.VMEM((strands, span, LANES), bf16),
            pltpu.VMEM((dp_ranks, span, channels), bf16),
        ]
        + [pltpu.VMEM(shape, bf16) for shape in shapes]
        + [pltpu.SemaphoreType.DMA((ranks + 4,))],
        specs=[SMEM, ANY, HBM] + [ANY] * (len(held) - 2) + [VMEM] * 2,
        out_specs=(HBM,) * 3,
    )
    terms = lax.all_to_all(outgoing, EVERY, 0, 0, tiled=True)
    crossed = lax.ppermute(cross, RANK, flipped_pairs(ranks, core))
    leaving = called(
        lambda *refs: chip_sum(part, *refs),
        tuple(shape_of((positions, channels + 4 * part), bf16) for _ in masks),
        (own, crossed),
        8,
    )
    arrived = leaving[:1] + tuple(
        lax.ppermute(message, RANK, flipped_pairs(ranks, mask))
        for message, mask in zip(leaving[1:], masks[1:])
    )
    order = [
        [
            ((sb * seq_ranks + sr) * dp_blocks + db) * dp_ranks + dr
            for sb in range(seq_blocks)
            for db in range(dp_blocks)
        ]
        for sr in range(seq_ranks)
        for dr in range(dp_ranks)
    ]
    grad_kernel, grad_gain = called(
        lambda *refs: collect(order, *refs),
        (shape_of((rows, channels), f32), shape_of((channels // owners, 1), f32)),
        (terms,),
        16,
        scratch=[pltpu.VMEM((channels, -(-rows // LANES) * LANES), f32)],
    )
    grad_kernel, home, *arrived = lax.optimization_barrier((grad_kernel, *arrived))
    combined, grad_input = called(
        lambda *refs: finish(part, core, *refs),
        (shape_of((positions, channels), bf16), shape_of((positions, channels), bf16)),
        (rank, values, cot, pairing, home, *arrived),
        16,
        scratch=[pltpu.VMEM((2, ranks, positions, LANES), bf16)],
        specs=[SMEM] + [VMEM] * (4 + len(arrived)),
    )
    return combined[None], grad_input[None], grad_kernel, grad_gain[:, 0]


def solution(mesh):
    seq, dp = mesh.shape["seq"], mesh.shape["dp"]
    seq_ranks, dp_ranks = 4, 2
    grouped = Mesh(mesh.devices.reshape(seq // seq_ranks, seq_ranks, dp // dp_ranks, dp_ranks), EVERY)
    along = P(("dp_block", "dp_rank"), ("seq_block", "seq_rank"), None)
    return jax.shard_map(
        per_device,
        mesh=grouped,
        in_specs=(along, along, P(EVERY, None), P(), P()),
        out_specs=(along, along, P(EVERY, None), P(EVERY)),
        check_vma=False,
    )
```

```python
import jax
import jax.numpy as jnp
from jax import lax
from jax.experimental import pallas as pl
from jax.experimental.pallas import tpu as pltpu
from jax.sharding import Mesh, PartitionSpec as P

epsilon = 1e-06
RANK = ("seq_rank", "dp_rank")
EVERY = ("seq_block", "seq_rank", "dp_block", "dp_rank")
LANES = 128
HALO = 16
EXTRA = 2
VMEM = pl.BlockSpec(memory_space=pltpu.VMEM)
SMEM = pl.BlockSpec(memory_space=pltpu.SMEM)
HBM = pl.BlockSpec(memory_space=pltpu.HBM)
ANY = pl.BlockSpec(memory_space=pl.ANY)
bf16 = jnp.bfloat16
f32 = jnp.float32


def called(body, outs, args, vmem, scratch=(), specs=None, out_specs=None):
    return pl.pallas_call(
        body,
        out_shape=outs,
        in_specs=specs or [VMEM] * len(args),
        out_specs=out_specs or jax.tree.map(lambda _: VMEM, outs),
        scratch_shapes=list(scratch),
        compiler_params=pltpu.CompilerParams(vmem_limit_bytes=vmem * 2**20),
        cost_estimate=pl.CostEstimate(flops=0, bytes_accessed=0, transcendentals=0),
    )(*args)


def shape_of(shape, dtype):
    return jax.ShapeDtypeStruct(shape, dtype)


def dot(a, b, contract):
    return lax.dot_general(a, b, (contract, ((), ())), preferred_element_type=f32)


def gelu_and_slope(x):
    inner = 0.7978845608028654 * (x + 0.044715 * (x * x * x))
    bend = jnp.tanh(inner)
    half_sum = 0.5 * (1.0 + bend)
    slope = half_sum + (0.5 * x) * (1.0 - bend * bend) * (
        0.7978845608028654 * (1.0 + 0.134145 * (x * x))
    )
    return x * half_sum, slope


def slot_maps(part, slots, pairing):
    shape = (slots, pairing.shape[1])
    slot = lax.broadcasted_iota(jnp.int32, shape, 0)
    lane = lax.bitwise_and(slot, LANES - 1)
    channel_of = jnp.where(lane < part, lax.div(slot, LANES) * part + lane, -1)
    channel = lax.broadcasted_iota(jnp.int32, shape, 1)
    return [jnp.where(channel_of == c, 1.0, 0.0).astype(bf16) for c in (channel, pairing)]


def swap_map(pairing):
    channels = pairing.shape[1]
    row = lax.broadcasted_iota(jnp.int32, (channels, channels), 0)
    return jnp.where(row == pairing, 1.0, 0.0).astype(bf16)


def chip_masks(ranks, core):
    return [mask for mask in range(ranks) if not mask & core]


class Moves:
    def __init__(self, sems):
        self.sems, self.copies = sems, []

    def start(self, source, target):
        copy = pltpu.make_async_copy(source, target, self.sems.at[len(self.copies)])
        copy.start()
        self.copies.append(copy)
        return copy

    def wait(self):
        for copy in self.copies:
            copy.wait()


def spread(piece_of, weights_ref, out_ref, square, sent, sems):
    rows, channels = weights_ref.shape
    part = out_ref.shape[1]
    square[...] = jnp.zeros_like(square)
    square[:rows] = weights_ref[...].astype(f32)
    turned = square[...].T.astype(bf16)
    for owner, piece in enumerate(piece_of):
        sent[owner] = turned[piece * part : (piece + 1) * part, :rows]
    moves = Moves(sems)
    moves.start(sent, out_ref)
    moves.wait()


def pack_messages(part, core, rank_ref, values_ref, cot_ref, edge_ref, pairing_ref, *outs):
    positions, channels = values_ref.shape
    home_ref, cross_ref, leaving = outs[0], outs[1], outs[2:]
    masks = chip_masks(2 * (len(leaving) + 1), core)
    flips = [mask | c for mask in masks[1:] for c in (core, 0)] + [0, core]
    shape = (part, channels)
    row = lax.broadcasted_iota(jnp.int32, shape, 0)
    column = lax.broadcasted_iota(jnp.int32, shape, 1)
    offsets = [column - row, pairing_ref[...].reshape(1, -1) - row]
    maps = [
        jnp.where(offset == lax.bitwise_xor(rank_ref[0], flip) * part, 1.0, 0.0).astype(bf16)
        for flip in flips
        for offset in offsets
    ]
    maps = jnp.concatenate(maps, 0)
    for rows, kept, cot in (
        (slice(0, positions), values_ref[...], cot_ref[...]),
        (slice(positions, None), edge_ref[:, :channels], edge_ref[:, channels:]),
    ):
        slices = dot(cot, maps, ((1,), (1,))).astype(bf16)
        lane = 0
        for out in (*leaving, home_ref, cross_ref):
            count = out.shape[1] - channels
            out[rows, :channels] = kept
            out[rows, channels:] = slices[:, lane : lane + count]
            lane += count


def stack_crossing(*refs):
    out_ref = refs[-1]
    width = out_ref.shape[2]
    for m, ref in enumerate(refs[:-1]):
        out_ref[m] = ref[:, :width]


def normalize(x, gains):
    x = x.astype(f32)
    x = x * lax.rsqrt(jnp.mean(x * x, -1, keepdims=True) + epsilon)
    return [(x * gain).astype(bf16) for gain in gains]


def swapped_row(row, swap):
    first = row.astype(bf16).astype(f32)
    second = (row - first).astype(bf16).astype(f32)
    third = row - first - second
    index = lax.broadcasted_iota(jnp.int32, (HALO, row.shape[1]), 0)
    parts = jnp.where(index == 0, first, jnp.where(index == 1, second, jnp.where(index == 2, third, 0.0)))
    result = dot(parts.astype(bf16), swap, ((1,), (0,)))
    return result[0:1] + result[1:2] + result[2:3]


def main_body(core, chips, groups, rank_ref, pieces_in, home_in, *refs):
    arrived_in, refs = refs[: chips - 1], refs[chips - 1 :]
    crossed_in, refs = refs[:groups], refs[groups:]
    gain_ref, pairing_ref, leaving_out, cross_out, own_out = refs[:5]
    pieces, home, crossed, arrived, normed_ref, grads_ref, edge_normed_ref, edge_grads_ref = refs[5:13]
    padded, terms, halves, bent, slopes, total, shifted_ref, kernel_ref, gelu_ref = refs[13:22]
    scaled, leaving, cross, own, sems = refs[22:]
    owners, part, rows = pieces.shape
    strands = normed_ref.shape[0]
    dp_ranks = strands // 2
    moves = Moves(sems)
    got_blocks = [moves.start(home_in, home)]
    got_blocks += [moves.start(block, arrived.at[m]) for m, block in enumerate(arrived_in)]
    per = chips // groups
    got_blocks += [moves.start(crossed_in[m // per].at[m % per], crossed.at[m]) for m in range(chips)]
    got_pieces = moves.start(pieces_in, pieces)
    arrivals = len(moves.copies)
    masks = chip_masks(2 * chips, core)
    seq_ranks = 2 * chips // dp_ranks
    positions = home.shape[0] - HALO
    channels, width = gain_ref.shape[1], home.shape[1]
    swap = swap_map(pairing_ref[...].reshape(1, -1))
    gains = [gain_ref[...], swapped_row(gain_ref[...], swap)]
    blocks = [(0, home, channels)]
    blocks += [(mask, arrived.at[m], width) for m, mask in enumerate(masks[1:])]
    blocks += [(mask | core, crossed.at[m], channels) for m, mask in enumerate(masks)]
    for got, (flip, ref, lane) in zip(got_blocks, blocks):
        got.wait()
        source = lax.bitwise_xor(rank_ref[0], flip)
        b, i = lax.rem(source, dp_ranks), lax.div(source, dp_ranks)
        start = pl.multiple_of(i * positions, positions)
        side = jnp.where(i == 0, 0, jnp.where(i == seq_ranks - 1, 1, 2))
        both = normalize(ref[:, :channels], gains)
        for n, normed in enumerate(both):
            first = lane + n * part
            grads = 0.5 * ref[:, first : first + part].astype(f32)
            index = n * dp_ranks + b
            normed_ref[index, pl.ds(start, positions), :] = normed[:positions]
            grads_ref[index, pl.ds(start, positions), :part] = grads[:positions]
            edge_normed_ref[side, index] = normed[positions:]
            edge_grads_ref[side, index, :, :part] = grads[positions:]
    span = normed_ref.shape[1]
    taps = kernel_ref.shape[0] // part
    half = taps // 2
    reach = 2 * half
    wide = bent.shape[0]

    def runs(owner):
        first, last = owner * rows, (owner + 1) * rows
        while first < last:
            tap, channel = divmod(first, channels)
            count = min(last - first, channels - channel)
            yield tap, channel, count, first - owner * rows
            first += count

    got_pieces.wait()
    for owner in range(owners):
        for tap, channel, count, offset in runs(owner):
            kernel_ref[tap * part : (tap + 1) * part, channel : channel + count] = pieces[
                owner, :, offset : offset + count
            ]
    kernel = kernel_ref[...]
    kernels = [kernel, dot(kernel, swap, ((1,), (0,))).astype(bf16)]
    padded[...] = jnp.zeros_like(padded)
    for n in range(2):
        for k in range(taps):
            padded[n, k * LANES : k * LANES + part, :] = kernels[n][k * part : (k + 1) * part, :]
    edge_terms = []
    for n in range(2):
        edges = [
            edge_normed_ref[side, n * dp_ranks + b] for side in range(2) for b in range(dp_ranks)
        ]
        edge_terms.append(dot(jnp.concatenate(edges, 0), padded[n], ((1,), (1,))))
    for strand in range(strands):
        forward = strand < dp_ranks
        n, b = divmod(strand, dp_ranks)
        terms[HALO : HALO + span, :] = dot(normed_ref[strand], padded[n], ((1,), (1,)))
        halves[HALO : HALO + span, :] = grads_ref[strand]
        for side, start in enumerate((0, HALO + span)):
            first = (side * dp_ranks + b) * HALO
            terms[start : start + HALO, :] = edge_terms[n][first : first + HALO]
            halves[start : start + HALO, :] = edge_grads_ref[side, strand]
        preact = jnp.zeros((wide, LANES), f32)
        for k in range(taps):
            start = HALO - reach + k if forward else HALO - k
            preact += terms[start : start + wide, k * LANES : (k + 1) * LANES]
        result, slope = gelu_and_slope(preact)
        bent[...] = result
        gelu_ref[strand] = bent[half : half + span, :].astype(bf16)
        slopes[...] = halves[HALO - half : HALO - half + wide, :] * slope
        for k in range(taps):
            start = reach - k if forward else k
            shifted_ref[strand, :, k * part : (k + 1) * part] = slopes[start : start + span, :part].astype(bf16)
    plain, other = [
        dot(
            shifted_ref[n * dp_ranks : (n + 1) * dp_ranks].reshape(dp_ranks * span, taps * part),
            normed_ref[n * dp_ranks : (n + 1) * dp_ranks].reshape(dp_ranks * span, channels),
            ((0,), (0,)),
        )
        for n in range(2)
    ]
    total[...] = plain + dot(other.astype(bf16), swap, ((1,), (0,)))
    gain = jnp.sum(total[...] * kernel.astype(f32), 0, keepdims=True) / gain_ref[...]
    gain_high = gain.astype(bf16).astype(f32)
    row = lax.broadcasted_iota(jnp.int32, (HALO, channels), 0)
    extra = jnp.where(row == 0, gain_high, jnp.where(row == 1, gain - gain_high, 0.0)).T
    own_gain = channels // owners
    for owner in range(owners):
        for tap, channel, count, offset in runs(owner):
            leaving[owner, :, offset : offset + count] = total[
                tap * part : (tap + 1) * part, channel : channel + count
            ].astype(bf16)
        leaving[owner, :, rows:] = jnp.zeros((part, EXTRA), bf16)
        leaving[owner, :own_gain, rows:] = extra[
            owner * own_gain : (owner + 1) * own_gain, :EXTRA
        ].astype(bf16)
    moves.start(leaving, leaving_out)
    for b in range(dp_ranks):
        scaled[b] = (
            dot(shifted_ref[b], kernels[0], ((1,), (0,))) * gains[0]
            + dot(shifted_ref[dp_ranks + b], kernels[1], ((1,), (0,))) * gains[1]
        ).astype(bf16)
    for out, target_out, flip in ((cross, cross_out, core), (own, own_out, 0)):
        for m, mask in enumerate(masks):
            target = lax.bitwise_xor(rank_ref[0], mask | flip)
            b = lax.rem(target, dp_ranks)
            start = pl.multiple_of(lax.div(target, dp_ranks) * positions, positions)
            out[m, :, :channels] = scaled[b, pl.ds(start, positions), :]
            for n in range(2):
                lane = channels + n * LANES
                out[m, :, lane : lane + LANES] = gelu_ref[n * dp_ranks + b, pl.ds(start, positions), :]
        moves.start(out, target_out)
    for copy in moves.copies[arrivals:]:
        copy.wait()


def chip_sum(part, own_ref, crossed_ref, *outs):
    channels = own_ref.shape[2] - 2 * LANES
    for m, out in enumerate(outs):
        out[:, :channels] = (
            own_ref[m, :, :channels].astype(f32) + crossed_ref[m, :, :channels].astype(f32)
        ).astype(bf16)
        for c, ref in enumerate((own_ref, crossed_ref)):
            for n in range(2):
                lane = channels + n * LANES
                start = channels + (2 * c + n) * part
                out[:, start : start + part] = ref[m, :, lane : lane + part]


def finish(part, core, rank_ref, values_ref, cot_ref, pairing_ref, *refs):
    arrived, (combined_ref, grad_ref, gelus) = refs[:-3], refs[-3:]
    channels = values_ref.shape[1]
    ranks = gelus.shape[1]
    gelus[...] = jnp.zeros_like(gelus)
    scaled = jnp.zeros(values_ref.shape, f32)
    for mask, block in zip(chip_masks(ranks, core), arrived):
        scaled += block[:, :channels].astype(f32)
        for c in range(2):
            source = lax.bitwise_xor(rank_ref[0], mask | c * core)
            for n in range(2):
                start = channels + (2 * c + n) * part
                gelus[n, source, :, :part] = block[:, start : start + part]
    joined = [jnp.concatenate([gelus[n, j] for j in range(ranks)], -1) for n in range(2)]
    maps = slot_maps(part, ranks * LANES, pairing_ref[...].reshape(1, -1))
    plain, other = [dot(j, m, ((1,), (0,))) for j, m in zip(joined, maps)]
    values = values_ref[...].astype(f32)
    rms = lax.rsqrt(jnp.mean(values * values, -1, keepdims=True) + epsilon)
    reverse_out = (values + other).astype(bf16).astype(f32)
    combined_ref[...] = (0.5 * (values + plain + reverse_out)).astype(bf16)
    along = jnp.mean(scaled * values, -1, keepdims=True)
    grad_ref[...] = (cot_ref[...].astype(f32) + rms * scaled - values * (rms * rms * rms * along)).astype(bf16)


def collect(owner_of, terms_ref, kernel_ref, gain_ref, joined):
    part = terms_ref.shape[1]
    rows = kernel_ref.shape[0]
    own_gain = gain_ref.shape[1]
    joined[...] = jnp.zeros_like(joined)
    gain = jnp.zeros((own_gain, EXTRA), f32)
    for rank, owners in enumerate(owner_of):
        total = terms_ref[owners[0]].astype(f32)
        for owner in owners[1:]:
            total += terms_ref[owner].astype(f32)
        joined[rank * part : (rank + 1) * part, :rows] = total[:, :rows]
        gain += total[:own_gain, rows:]
    channels = kernel_ref.shape[1]
    joined[channels : channels + own_gain, :EXTRA] = gain
    turned = joined[...].T
    kernel_ref[...] = turned[:rows, :channels]
    gain_ref[...] = sum(turned[n : n + 1, channels : channels + own_gain] for n in range(EXTRA))


def flipped_pairs(count, mask):
    return [(i, i ^ mask) for i in range(count)]


def per_device(activations, cotangent, weights, norm_gain, pairing):
    seq_ranks = lax.axis_size("seq_rank")
    dp_ranks = lax.axis_size("dp_rank")
    seq_blocks = lax.axis_size("seq_block")
    dp_blocks = lax.axis_size("dp_block")
    ranks = seq_ranks * dp_ranks
    owners = ranks * seq_blocks * dp_blocks
    positions, channels = activations.shape[1:]
    rows = weights.shape[0]
    taps = rows * owners // channels
    part = channels // ranks
    span = positions * seq_ranks
    long = span + 2 * HALO
    reach = taps - taps % 2
    wide = -(-(span + reach) // 8) * 8
    strands = 2 * dp_ranks
    width = channels + 2 * LANES
    slim = channels + 2 * part
    rank = lax.axis_index(RANK).reshape(1)
    values, cot = activations[0], cotangent[0]
    along = ("seq_block", "seq_rank")
    ends = [(b * seq_ranks - 1, b * seq_ranks) for b in range(1, seq_blocks)]
    both = jnp.concatenate([values, cot], -1)
    edge = jnp.where(lax.axis_index("seq_rank") == 0, both[:HALO], both[-HALO:])
    edge = lax.ppermute(edge, along, ends + [(target, source) for source, target in ends])
    piece_of = [
        sr * dp_ranks + dr
        for _ in range(seq_blocks)
        for sr in range(seq_ranks)
        for _ in range(dp_blocks)
        for dr in range(dp_ranks)
    ]
    square = -(-rows // LANES) * LANES
    slices = called(
        lambda *refs: spread(piece_of, *refs),
        pltpu.HBM((owners, part, rows), bf16),
        (weights,),
        16,
        scratch=[
            pltpu.VMEM((square, channels), f32),
            pltpu.VMEM((owners, part, rows), bf16),
            pltpu.SemaphoreType.DMA((1,)),
        ],
        out_specs=HBM,
    )
    slices, packed = lax.optimization_barrier((slices, values))
    pieces = lax.all_to_all(slices, EVERY, 0, 0, tiled=True)
    gain = norm_gain.reshape(1, channels)
    core = dp_ranks
    masks = chip_masks(ranks, core)
    block = positions + HALO
    home, cross, *leaving = called(
        lambda *refs: pack_messages(part, core, *refs),
        (pltpu.HBM((block, slim), bf16), shape_of((block, slim), bf16))
        + tuple(shape_of((block, slim + 2 * part), bf16) for _ in masks[1:]),
        (rank, packed, cot, edge, pairing),
        16,
        specs=[SMEM] + [VMEM] * 4,
    )
    arrived = [
        lax.ppermute(message, RANK, flipped_pairs(ranks, mask))
        for message, mask in zip(leaving, masks[1:])
    ]
    both_cores = []
    for group in ((cross, *arrived),):
        crossing = called(stack_crossing, shape_of((len(group), block, slim), bf16), group, 8)
        both_cores.append(lax.ppermute(crossing, RANK, flipped_pairs(ranks, core)))
    home = pltpu.with_memory_space_constraint(home, pltpu.HBM)
    held = (pieces, home, *arrived, *both_cores)
    halves = (len(masks), positions, width)
    shapes = ((owners, part, rows + EXTRA), halves, halves)
    groups = len(both_cores)
    outgoing, cross, own = called(
        lambda *refs: main_body(core, len(masks), groups, *refs),
        tuple(pltpu.HBM(shape, bf16) for shape in shapes),
        (rank, *held, gain, pairing),
        44,
        scratch=[
            pltpu.VMEM(pieces.shape, bf16),
            pltpu.VMEM(home.shape, bf16),
            pltpu.VMEM((len(masks), block, slim), bf16),
            pltpu.VMEM((len(arrived), *arrived[0].shape), bf16),
            pltpu.VMEM((strands, span, channels), bf16),
            pltpu.VMEM((strands, span, LANES), f32),
            pltpu.VMEM((3, strands, HALO, channels), bf16),
            pltpu.VMEM((3, strands, HALO, LANES), f32),
            pltpu.VMEM((2, taps * LANES, channels), bf16),
            pltpu.VMEM((long, taps * LANES), f32),
            pltpu.VMEM((long, LANES), f32),
            pltpu.VMEM((wide, LANES), f32),
            pltpu.VMEM((wide, LANES), f32),
            pltpu.VMEM((taps * part, channels), f32),
            pltpu.VMEM((strands, span, taps * part), bf16),
            pltpu.VMEM((taps * part, channels), bf16),
            pltpu.VMEM((strands, span, LANES), bf16),
            pltpu.VMEM((dp_ranks, span, channels), bf16),
        ]
        + [pltpu.VMEM(shape, bf16) for shape in shapes]
        + [pltpu.SemaphoreType.DMA((ranks + 4,))],
        specs=[SMEM, ANY, HBM] + [ANY] * (len(held) - 2) + [VMEM] * 2,
        out_specs=(HBM,) * 3,
    )
    terms = lax.all_to_all(outgoing, EVERY, 0, 0, tiled=True)
    crossed = lax.ppermute(cross, RANK, flipped_pairs(ranks, core))
    leaving = called(
        lambda *refs: chip_sum(part, *refs),
        tuple(shape_of((positions, channels + 4 * part), bf16) for _ in masks),
        (own, crossed),
        8,
    )
    arrived = leaving[:1] + tuple(
        lax.ppermute(message, RANK, flipped_pairs(ranks, mask))
        for message, mask in zip(leaving[1:], masks[1:])
    )
    order = [
        [
            ((sb * seq_ranks + sr) * dp_blocks + db) * dp_ranks + dr
            for sb in range(seq_blocks)
            for db in range(dp_blocks)
        ]
        for sr in range(seq_ranks)
        for dr in range(dp_ranks)
    ]
    grad_kernel, grad_gain = called(
        lambda *refs: collect(order, *refs),
        (shape_of((rows, channels), f32), shape_of((1, channels // owners), f32)),
        (terms,),
        16,
        scratch=[pltpu.VMEM((channels + LANES, -(-rows // LANES) * LANES), f32)],
    )
    grad_kernel, home, *arrived = lax.optimization_barrier((grad_kernel, *arrived))
    combined, grad_input = called(
        lambda *refs: finish(part, core, *refs),
        (shape_of((positions, channels), bf16), shape_of((positions, channels), bf16)),
        (rank, values, cot, pairing, home, *arrived),
        16,
        scratch=[pltpu.VMEM((2, ranks, positions, LANES), bf16)],
        specs=[SMEM] + [VMEM] * (4 + len(arrived)),
    )
    return combined[None], grad_input[None], grad_kernel, grad_gain[0]


def solution(mesh):
    seq, dp = mesh.shape["seq"], mesh.shape["dp"]
    seq_ranks, dp_ranks = 4, 2
    grouped = Mesh(mesh.devices.reshape(seq // seq_ranks, seq_ranks, dp // dp_ranks, dp_ranks), EVERY)
    along = P(("dp_block", "dp_rank"), ("seq_block", "seq_rank"), None)
    return jax.shard_map(
        per_device,
        mesh=grouped,
        in_specs=(along, along, P(EVERY, None), P(), P()),
        out_specs=(along, along, P(EVERY, None), P(EVERY)),
        check_vma=False,
    )
```

```python
import jax
import jax.numpy as jnp
from jax import lax
from jax.experimental import pallas as pl
from jax.experimental.pallas import tpu as pltpu
from jax.sharding import Mesh, PartitionSpec as P

epsilon = 1e-06
RANK = ("seq_rank", "dp_rank")
EVERY = ("seq_block", "seq_rank", "dp_block", "dp_rank")
LANES = 128
HALO = 16
EXTRA = 2
VMEM = pl.BlockSpec(memory_space=pltpu.VMEM)
SMEM = pl.BlockSpec(memory_space=pltpu.SMEM)
HBM = pl.BlockSpec(memory_space=pltpu.HBM)
ANY = pl.BlockSpec(memory_space=pl.ANY)
bf16 = jnp.bfloat16
f32 = jnp.float32


def called(body, outs, args, vmem, scratch=(), specs=None, out_specs=None):
    return pl.pallas_call(
        body,
        out_shape=outs,
        in_specs=specs or [VMEM] * len(args),
        out_specs=out_specs or jax.tree.map(lambda _: VMEM, outs),
        scratch_shapes=list(scratch),
        compiler_params=pltpu.CompilerParams(vmem_limit_bytes=vmem * 2**20),
        cost_estimate=pl.CostEstimate(flops=0, bytes_accessed=0, transcendentals=0),
    )(*args)


def shape_of(shape, dtype):
    return jax.ShapeDtypeStruct(shape, dtype)


def dot(a, b, contract):
    return lax.dot_general(a, b, (contract, ((), ())), preferred_element_type=f32)


def gelu_and_slope(x):
    inner = 0.7978845608028654 * (x + 0.044715 * (x * x * x))
    bend = jnp.tanh(inner)
    half_sum = 0.5 * (1.0 + bend)
    slope = half_sum + (0.5 * x) * (1.0 - bend * bend) * (
        0.7978845608028654 * (1.0 + 0.134145 * (x * x))
    )
    return x * half_sum, slope


def swap_map(pairing):
    channels = pairing.shape[1]
    row = lax.broadcasted_iota(jnp.int32, (channels, channels), 0)
    return jnp.where(row == pairing, 1.0, 0.0).astype(bf16)


def chip_masks(ranks, core):
    masks = [mask for mask in range(ranks) if not mask & core]
    return masks[:1] + sorted(masks[1:], key=lambda mask: -mask.bit_count())


class Moves:
    def __init__(self, sems):
        self.sems, self.copies = sems, []

    def start(self, source, target):
        copy = pltpu.make_async_copy(source, target, self.sems.at[len(self.copies)])
        copy.start()
        self.copies.append(copy)
        return copy

    def wait(self):
        for copy in self.copies:
            copy.wait()


def spread(piece_of, weights_ref, out_ref, square, sent, sems):
    rows, channels = weights_ref.shape
    part = out_ref.shape[1]
    square[...] = jnp.zeros_like(square)
    square[:rows] = weights_ref[...].astype(f32)
    turned = square[...].T.astype(bf16)
    for owner, piece in enumerate(piece_of):
        sent[owner] = turned[piece * part : (piece + 1) * part, :rows]
    moves = Moves(sems)
    moves.start(sent, out_ref)
    moves.wait()


def pack_messages(part, core, rank_ref, values_ref, cot_ref, edge_ref, pairing_ref, *outs):
    positions, channels = values_ref.shape
    home_ref, cross_ref, leaving = outs[0], outs[1], outs[2:]
    masks = chip_masks(2 * (len(leaving) + 1), core)
    flips = [mask | c for mask in masks[1:] for c in (core, 0)] + [0, core]
    shape = (part, channels)
    row = lax.broadcasted_iota(jnp.int32, shape, 0)
    column = lax.broadcasted_iota(jnp.int32, shape, 1)
    offsets = [column - row, pairing_ref[...].reshape(1, -1) - row]
    maps = [
        jnp.where(offset == lax.bitwise_xor(rank_ref[0], flip) * part, 1.0, 0.0).astype(bf16)
        for flip in flips
        for offset in offsets
    ]
    maps = jnp.concatenate(maps, 0)
    cot = jnp.concatenate([cot_ref[...], edge_ref[:, channels:]], 0)
    slices = dot(cot, maps, ((1,), (1,))).astype(bf16)
    lane = 0
    for out in (*leaving, home_ref, cross_ref):
        count = out.shape[1] - channels
        out[:positions, :channels] = values_ref[...]
        out[positions:, :channels] = edge_ref[:, :channels]
        out[:, channels:] = slices[:, lane : lane + count]
        lane += count


def stack_crossing(*refs):
    out_ref = refs[-1]
    width = out_ref.shape[2]
    for m, ref in enumerate(refs[:-1]):
        out_ref[m] = ref[:, :width]


def normalize(x, gains):
    x = x.astype(f32)
    x = x * lax.rsqrt(jnp.mean(x * x, -1, keepdims=True) + epsilon)
    return [(x * gain).astype(bf16) for gain in gains]


def swapped_row(row, swap):
    first = row.astype(bf16).astype(f32)
    second = (row - first).astype(bf16).astype(f32)
    third = row - first - second
    index = lax.broadcasted_iota(jnp.int32, (HALO, row.shape[1]), 0)
    parts = jnp.where(index == 0, first, jnp.where(index == 1, second, jnp.where(index == 2, third, 0.0)))
    result = dot(parts.astype(bf16), swap, ((1,), (0,)))
    return result[0:1] + result[1:2] + result[2:3]


def main_body(core, chips, groups, rank_ref, pieces_in, home_in, *refs):
    arrived_in, refs = refs[: chips - 1], refs[chips - 1 :]
    crossed_in, refs = refs[:groups], refs[groups:]
    gain_ref, pairing_ref, leaving_out, cross_out, own_out = refs[:5]
    pieces, home, crossed, arrived, normed_ref, grads_ref, edge_normed_ref, edge_grads_ref = refs[5:13]
    padded, terms, halves, bent, slopes, total, shifted_ref, kernel_ref, gelu_ref = refs[13:22]
    scaled, leaving, cross, own, sems = refs[22:]
    owners, part, rows = pieces.shape
    strands = normed_ref.shape[0]
    dp_ranks = strands // 2
    moves = Moves(sems)
    got_blocks = [moves.start(home_in, home)]
    got_blocks += [moves.start(block, arrived.at[m]) for m, block in enumerate(arrived_in)]
    per = chips // groups
    got_blocks += [moves.start(crossed_in[m // per].at[m % per], crossed.at[m]) for m in range(chips)]
    got_pieces = moves.start(pieces_in, pieces)
    arrivals = len(moves.copies)
    masks = chip_masks(2 * chips, core)
    seq_ranks = 2 * chips // dp_ranks
    positions = home.shape[0] - HALO
    channels, width = gain_ref.shape[1], home.shape[1]
    swap = swap_map(pairing_ref[...].reshape(1, -1))
    gains = [gain_ref[...], swapped_row(gain_ref[...], swap)]
    blocks = [(0, home, channels)]
    blocks += [(mask, arrived.at[m], width) for m, mask in enumerate(masks[1:])]
    blocks += [(mask | core, crossed.at[m], channels) for m, mask in enumerate(masks)]
    for got, (flip, ref, lane) in zip(got_blocks, blocks):
        got.wait()
        source = lax.bitwise_xor(rank_ref[0], flip)
        b, i = lax.rem(source, dp_ranks), lax.div(source, dp_ranks)
        start = pl.multiple_of(i * positions, positions)
        side = jnp.where(i == 0, 0, jnp.where(i == seq_ranks - 1, 1, 2))
        both = normalize(ref[:, :channels], gains)
        for n, normed in enumerate(both):
            first = lane + n * part
            grads = 0.5 * ref[:, first : first + part].astype(f32)
            index = n * dp_ranks + b
            normed_ref[index, pl.ds(start, positions), :] = normed[:positions]
            grads_ref[index, pl.ds(start, positions), :part] = grads[:positions]
            edge_normed_ref[side, index] = normed[positions:]
            edge_grads_ref[side, index, :, :part] = grads[positions:]
    span = normed_ref.shape[1]
    taps = kernel_ref.shape[0] // part
    half = taps // 2
    reach = 2 * half
    wide = bent.shape[0]

    def runs(owner):
        first, last = owner * rows, (owner + 1) * rows
        while first < last:
            tap, channel = divmod(first, channels)
            count = min(last - first, channels - channel)
            yield tap, channel, count, first - owner * rows
            first += count

    got_pieces.wait()
    for owner in range(owners):
        for tap, channel, count, offset in runs(owner):
            kernel_ref[tap * part : (tap + 1) * part, channel : channel + count] = pieces[
                owner, :, offset : offset + count
            ]
    kernel = kernel_ref[...]
    kernels = [kernel, dot(kernel, swap, ((1,), (0,))).astype(bf16)]
    padded[...] = jnp.zeros_like(padded)
    for n in range(2):
        for k in range(taps):
            padded[n, k * LANES : k * LANES + part, :] = kernels[n][k * part : (k + 1) * part, :]
    edge_terms = []
    for n in range(2):
        edges = [
            edge_normed_ref[side, n * dp_ranks + b] for side in range(2) for b in range(dp_ranks)
        ]
        edge_terms.append(dot(jnp.concatenate(edges, 0), padded[n], ((1,), (1,))))
    for strand in range(strands):
        forward = strand < dp_ranks
        n, b = divmod(strand, dp_ranks)
        terms[HALO : HALO + span, :] = dot(normed_ref[strand], padded[n], ((1,), (1,)))
        halves[HALO : HALO + span, :] = grads_ref[strand]
        for side, start in enumerate((0, HALO + span)):
            first = (side * dp_ranks + b) * HALO
            terms[start : start + HALO, :] = edge_terms[n][first : first + HALO]
            halves[start : start + HALO, :] = edge_grads_ref[side, strand]
        preact = jnp.zeros((wide, LANES), f32)
        for k in range(taps):
            start = HALO - reach + k if forward else HALO - k
            preact += terms[start : start + wide, k * LANES : (k + 1) * LANES]
        result, slope = gelu_and_slope(preact)
        bent[...] = result
        gelu_ref[strand] = bent[half : half + span, :].astype(bf16)
        slopes[...] = halves[HALO - half : HALO - half + wide, :] * slope
        for k in range(taps):
            start = reach - k if forward else k
            shifted_ref[strand, :, k * part : (k + 1) * part] = slopes[start : start + span, :part].astype(bf16)
    plain, other = [
        dot(
            shifted_ref[n * dp_ranks : (n + 1) * dp_ranks].reshape(dp_ranks * span, taps * part),
            normed_ref[n * dp_ranks : (n + 1) * dp_ranks].reshape(dp_ranks * span, channels),
            ((0,), (0,)),
        )
        for n in range(2)
    ]
    total[...] = plain + dot(other.astype(bf16), swap, ((1,), (0,)))
    gain = jnp.sum(total[...] * kernel.astype(f32), 0, keepdims=True) / gain_ref[...]
    gain_high = gain.astype(bf16).astype(f32)
    row = lax.broadcasted_iota(jnp.int32, (HALO, channels), 0)
    extra = jnp.where(row == 0, gain_high, jnp.where(row == 1, gain - gain_high, 0.0)).T
    own_gain = channels // owners
    for owner in range(owners):
        for tap, channel, count, offset in runs(owner):
            leaving[owner, :, offset : offset + count] = total[
                tap * part : (tap + 1) * part, channel : channel + count
            ].astype(bf16)
        leaving[owner, :, rows:] = jnp.zeros((part, EXTRA), bf16)
        leaving[owner, :own_gain, rows:] = extra[
            owner * own_gain : (owner + 1) * own_gain, :EXTRA
        ].astype(bf16)
    moves.start(leaving, leaving_out)
    for b in range(dp_ranks):
        scaled[b] = (
            dot(shifted_ref[b], kernels[0], ((1,), (0,))) * gains[0]
            + dot(shifted_ref[dp_ranks + b], kernels[1], ((1,), (0,))) * gains[1]
        ).astype(bf16)
    for out, target_out, flip in ((cross, cross_out, core), (own, own_out, 0)):
        for m, mask in enumerate(masks):
            target = lax.bitwise_xor(rank_ref[0], mask | flip)
            b = lax.rem(target, dp_ranks)
            start = pl.multiple_of(lax.div(target, dp_ranks) * positions, positions)
            out[m, :, :channels] = scaled[b, pl.ds(start, positions), :]
            for n in range(2):
                lane = channels + n * LANES
                out[m, :, lane : lane + LANES] = gelu_ref[n * dp_ranks + b, pl.ds(start, positions), :]
        moves.start(out, target_out)
    for copy in moves.copies[arrivals:]:
        copy.wait()


def chip_sum(part, own_ref, crossed_ref, *outs):
    channels = own_ref.shape[2] - 2 * LANES
    for m, out in enumerate(outs):
        out[:, :channels] = (
            own_ref[m, :, :channels].astype(f32) + crossed_ref[m, :, :channels].astype(f32)
        ).astype(bf16)
        for c, ref in enumerate((own_ref, crossed_ref)):
            for n in range(2):
                lane = channels + n * LANES
                start = channels + (2 * c + n) * part
                out[:, start : start + part] = ref[m, :, lane : lane + part]


def finish(part, core, rank_ref, values_ref, cot_ref, pairing_ref, *refs):
    arrived, (combined_ref, grad_ref, gelus) = refs[:-3], refs[-3:]
    channels = values_ref.shape[1]
    ranks = gelus.shape[1]
    scaled = jnp.zeros(values_ref.shape, f32)
    for mask, block in zip(chip_masks(ranks, core), arrived):
        scaled += block[:, :channels].astype(f32)
        for c in range(2):
            source = lax.bitwise_xor(rank_ref[0], mask | c * core)
            for n in range(2):
                start = channels + (2 * c + n) * part
                gelus[n, source] = block[:, start : start + part]
    plain, other = [jnp.concatenate([gelus[n, j] for j in range(ranks)], -1) for n in range(2)]
    plain = plain.astype(f32)
    other = dot(other, swap_map(pairing_ref[...].reshape(1, -1)), ((1,), (0,)))
    values = values_ref[...].astype(f32)
    rms = lax.rsqrt(jnp.mean(values * values, -1, keepdims=True) + epsilon)
    reverse_out = (values + other).astype(bf16).astype(f32)
    combined_ref[...] = (0.5 * (values + plain + reverse_out)).astype(bf16)
    along = jnp.mean(scaled * values, -1, keepdims=True)
    grad_ref[...] = (cot_ref[...].astype(f32) + rms * scaled - values * (rms * rms * rms * along)).astype(bf16)


def collect(owner_of, terms_ref, kernel_ref, gain_ref, joined):
    part = terms_ref.shape[1]
    rows = kernel_ref.shape[0]
    own_gain = gain_ref.shape[1]
    joined[...] = jnp.zeros_like(joined)
    gain = jnp.zeros((own_gain, EXTRA), f32)
    for rank, owners in enumerate(owner_of):
        total = terms_ref[owners[0]].astype(f32)
        for owner in owners[1:]:
            total += terms_ref[owner].astype(f32)
        joined[rank * part : (rank + 1) * part, :rows] = total[:, :rows]
        gain += total[:own_gain, rows:]
    channels = kernel_ref.shape[1]
    joined[channels : channels + own_gain, :EXTRA] = gain
    turned = joined[...].T
    kernel_ref[...] = turned[:rows, :channels]
    gain_ref[...] = sum(turned[n : n + 1, channels : channels + own_gain] for n in range(EXTRA))


def flipped_pairs(count, mask):
    return [(i, i ^ mask) for i in range(count)]


def per_device(activations, cotangent, weights, norm_gain, pairing):
    seq_ranks = lax.axis_size("seq_rank")
    dp_ranks = lax.axis_size("dp_rank")
    seq_blocks = lax.axis_size("seq_block")
    dp_blocks = lax.axis_size("dp_block")
    ranks = seq_ranks * dp_ranks
    owners = ranks * seq_blocks * dp_blocks
    positions, channels = activations.shape[1:]
    rows = weights.shape[0]
    taps = rows * owners // channels
    part = channels // ranks
    span = positions * seq_ranks
    long = span + 2 * HALO
    reach = taps - taps % 2
    wide = -(-(span + reach) // 8) * 8
    strands = 2 * dp_ranks
    width = channels + 2 * LANES
    slim = channels + 2 * part
    rank = lax.axis_index(RANK).reshape(1)
    values, cot = activations[0], cotangent[0]
    along = ("seq_block", "seq_rank")
    ends = [(b * seq_ranks - 1, b * seq_ranks) for b in range(1, seq_blocks)]
    both = jnp.concatenate([values, cot], -1)
    edge = jnp.where(lax.axis_index("seq_rank") == 0, both[:HALO], both[-HALO:])
    edge = lax.ppermute(edge, along, ends + [(target, source) for source, target in ends])
    piece_of = [
        sr * dp_ranks + dr
        for _ in range(seq_blocks)
        for sr in range(seq_ranks)
        for _ in range(dp_blocks)
        for dr in range(dp_ranks)
    ]
    square = -(-rows // LANES) * LANES
    slices = called(
        lambda *refs: spread(piece_of, *refs),
        pltpu.HBM((owners, part, rows), bf16),
        (weights,),
        16,
        scratch=[
            pltpu.VMEM((square, channels), f32),
            pltpu.VMEM((owners, part, rows), bf16),
            pltpu.SemaphoreType.DMA((1,)),
        ],
        out_specs=HBM,
    )
    slices, packed = lax.optimization_barrier((slices, values))
    pieces = lax.all_to_all(slices, EVERY, 0, 0, tiled=True)
    gain = norm_gain.reshape(1, channels)
    core = dp_ranks
    masks = chip_masks(ranks, core)
    block = positions + HALO
    home, cross, *leaving = called(
        lambda *refs: pack_messages(part, core, *refs),
        (pltpu.HBM((block, slim), bf16), shape_of((block, slim), bf16))
        + tuple(shape_of((block, slim + 2 * part), bf16) for _ in masks[1:]),
        (rank, packed, cot, edge, pairing),
        16,
        specs=[SMEM] + [VMEM] * 4,
    )
    arrived = [
        lax.ppermute(message, RANK, flipped_pairs(ranks, mask))
        for message, mask in zip(leaving, masks[1:])
    ]
    both_cores = []
    for group in ((cross, *arrived),):
        crossing = called(stack_crossing, shape_of((len(group), block, slim), bf16), group, 8)
        both_cores.append(lax.ppermute(crossing, RANK, flipped_pairs(ranks, core)))
    home = pltpu.with_memory_space_constraint(home, pltpu.HBM)
    held = (pieces, home, *arrived, *both_cores)
    halves = (len(masks), positions, width)
    shapes = ((owners, part, rows + EXTRA), halves, halves)
    groups = len(both_cores)
    outgoing, cross, own = called(
        lambda *refs: main_body(core, len(masks), groups, *refs),
        tuple(pltpu.HBM(shape, bf16) for shape in shapes),
        (rank, *held, gain, pairing),
        44,
        scratch=[
            pltpu.VMEM(pieces.shape, bf16),
            pltpu.VMEM(home.shape, bf16),
            pltpu.VMEM((len(masks), block, slim), bf16),
            pltpu.VMEM((len(arrived), *arrived[0].shape), bf16),
            pltpu.VMEM((strands, span, channels), bf16),
            pltpu.VMEM((strands, span, LANES), f32),
            pltpu.VMEM((3, strands, HALO, channels), bf16),
            pltpu.VMEM((3, strands, HALO, LANES), f32),
            pltpu.VMEM((2, taps * LANES, channels), bf16),
            pltpu.VMEM((long, taps * LANES), f32),
            pltpu.VMEM((long, LANES), f32),
            pltpu.VMEM((wide, LANES), f32),
            pltpu.VMEM((wide, LANES), f32),
            pltpu.VMEM((taps * part, channels), f32),
            pltpu.VMEM((strands, span, taps * part), bf16),
            pltpu.VMEM((taps * part, channels), bf16),
            pltpu.VMEM((strands, span, LANES), bf16),
            pltpu.VMEM((dp_ranks, span, channels), bf16),
        ]
        + [pltpu.VMEM(shape, bf16) for shape in shapes]
        + [pltpu.SemaphoreType.DMA((ranks + 4,))],
        specs=[SMEM, ANY, HBM] + [ANY] * (len(held) - 2) + [VMEM] * 2,
        out_specs=(HBM,) * 3,
    )
    terms = lax.all_to_all(outgoing, EVERY, 0, 0, tiled=True)
    crossed = lax.ppermute(cross, RANK, flipped_pairs(ranks, core))
    leaving = called(
        lambda *refs: chip_sum(part, *refs),
        tuple(shape_of((positions, channels + 4 * part), bf16) for _ in masks),
        (own, crossed),
        8,
    )
    arrived = leaving[:1] + tuple(
        lax.ppermute(message, RANK, flipped_pairs(ranks, mask))
        for message, mask in zip(leaving[1:], masks[1:])
    )
    order = [
        [
            ((sb * seq_ranks + sr) * dp_blocks + db) * dp_ranks + dr
            for sb in range(seq_blocks)
            for db in range(dp_blocks)
        ]
        for sr in range(seq_ranks)
        for dr in range(dp_ranks)
    ]
    grad_kernel, grad_gain = called(
        lambda *refs: collect(order, *refs),
        (shape_of((rows, channels), f32), shape_of((1, channels // owners), f32)),
        (terms,),
        16,
        scratch=[pltpu.VMEM((channels + LANES, -(-rows // LANES) * LANES), f32)],
    )
    grad_kernel, home, *arrived = lax.optimization_barrier((grad_kernel, *arrived))
    combined, grad_input = called(
        lambda *refs: finish(part, core, *refs),
        (shape_of((positions, channels), bf16), shape_of((positions, channels), bf16)),
        (rank, values, cot, pairing, home, *arrived),
        16,
        scratch=[pltpu.VMEM((2, ranks, positions, part), bf16)],
        specs=[SMEM] + [VMEM] * (4 + len(arrived)),
    )
    return combined[None], grad_input[None], grad_kernel, grad_gain[0]


def solution(mesh):
    seq, dp = mesh.shape["seq"], mesh.shape["dp"]
    seq_ranks, dp_ranks = 4, 2
    grouped = Mesh(mesh.devices.reshape(seq // seq_ranks, seq_ranks, dp // dp_ranks, dp_ranks), EVERY)
    along = P(("dp_block", "dp_rank"), ("seq_block", "seq_rank"), None)
    return jax.shard_map(
        per_device,
        mesh=grouped,
        in_specs=(along, along, P(EVERY, None), P(), P()),
        out_specs=(along, along, P(EVERY, None), P(EVERY)),
        check_vma=False,
    )
```

```python
import jax
import jax.numpy as jnp
from jax import lax
from jax.experimental import pallas as pl
from jax.experimental.pallas import tpu as pltpu
from jax.sharding import Mesh, PartitionSpec as P

epsilon = 1e-06
RANK = ("seq_rank", "dp_rank")
EVERY = ("seq_block", "seq_rank", "dp_block", "dp_rank")
LANES = 128
HALO = 16
EXTRA = 2
VMEM = pl.BlockSpec(memory_space=pltpu.VMEM)
SMEM = pl.BlockSpec(memory_space=pltpu.SMEM)
HBM = pl.BlockSpec(memory_space=pltpu.HBM)
ANY = pl.BlockSpec(memory_space=pl.ANY)
bf16 = jnp.bfloat16
f32 = jnp.float32


def called(body, outs, args, vmem, scratch=(), specs=None, out_specs=None):
    return pl.pallas_call(
        body,
        out_shape=outs,
        in_specs=specs or [VMEM] * len(args),
        out_specs=out_specs or jax.tree.map(lambda _: VMEM, outs),
        scratch_shapes=list(scratch),
        compiler_params=pltpu.CompilerParams(vmem_limit_bytes=vmem * 2**20),
        cost_estimate=pl.CostEstimate(flops=0, bytes_accessed=0, transcendentals=0),
    )(*args)


def shape_of(shape, dtype):
    return jax.ShapeDtypeStruct(shape, dtype)


def dot(a, b, contract):
    return lax.dot_general(a, b, (contract, ((), ())), preferred_element_type=f32)


def gelu_and_slope(x):
    inner = 0.7978845608028654 * (x + 0.044715 * (x * x * x))
    bend = jnp.tanh(inner)
    half_sum = 0.5 * (1.0 + bend)
    slope = half_sum + (0.5 * x) * (1.0 - bend * bend) * (
        0.7978845608028654 * (1.0 + 0.134145 * (x * x))
    )
    return x * half_sum, slope


def swap_map(pairing):
    channels = pairing.shape[1]
    row = lax.broadcasted_iota(jnp.int32, (channels, channels), 0)
    return jnp.where(row == pairing, 1.0, 0.0).astype(bf16)


def chip_masks(ranks, core):
    masks = [mask for mask in range(ranks) if not mask & core]
    return masks[:1] + sorted(masks[1:], key=lambda mask: -mask.bit_count())


class Moves:
    def __init__(self, sems):
        self.sems, self.copies = sems, []

    def start(self, source, target):
        copy = pltpu.make_async_copy(source, target, self.sems.at[len(self.copies)])
        copy.start()
        self.copies.append(copy)
        return copy

    def wait(self):
        for copy in self.copies:
            copy.wait()


def spread(piece_of, weights_ref, out_ref, square, sent, sems):
    rows, channels = weights_ref.shape
    part = out_ref.shape[1]
    square[...] = jnp.zeros_like(square)
    square[:rows] = weights_ref[...].astype(f32)
    turned = square[...].T.astype(bf16)
    for owner, piece in enumerate(piece_of):
        sent[owner] = turned[piece * part : (piece + 1) * part, :rows]
    moves = Moves(sems)
    moves.start(sent, out_ref)
    moves.wait()


def pack_messages(part, core, rank_ref, values_ref, cot_ref, edge_ref, pairing_ref, *outs):
    positions, channels = values_ref.shape
    home_ref, cross_ref, leaving = outs[0], outs[1], outs[2:]
    masks = chip_masks(2 * (len(leaving) + 1), core)
    flips = [mask | c for mask in masks[1:] for c in (core, 0)] + [0, core]
    shape = (part, channels)
    row = lax.broadcasted_iota(jnp.int32, shape, 0)
    column = lax.broadcasted_iota(jnp.int32, shape, 1)
    offsets = [column - row, pairing_ref[...].reshape(1, -1) - row]
    maps = [
        jnp.where(offset == lax.bitwise_xor(rank_ref[0], flip) * part, 1.0, 0.0).astype(bf16)
        for flip in flips
        for offset in offsets
    ]
    maps = jnp.concatenate(maps, 0)
    cot = jnp.concatenate([cot_ref[...], edge_ref[:, channels:]], 0)
    slices = dot(cot, maps, ((1,), (1,))).astype(bf16)
    lane = 0
    for out in (*leaving, home_ref, cross_ref):
        count = out.shape[1] - channels
        out[:positions, :channels] = values_ref[...]
        out[positions:, :channels] = edge_ref[:, :channels]
        out[:, channels:] = slices[:, lane : lane + count]
        lane += count


def stack_crossing(*refs):
    out_ref = refs[-1]
    width = out_ref.shape[2]
    for m, ref in enumerate(refs[:-1]):
        out_ref[m] = ref[:, :width]


def normalize(x, gains):
    x = x.astype(f32)
    x = x * lax.rsqrt(jnp.mean(x * x, -1, keepdims=True) + epsilon)
    return [(x * gain).astype(bf16) for gain in gains]


def swapped_row(row, swap):
    first = row.astype(bf16).astype(f32)
    second = (row - first).astype(bf16).astype(f32)
    third = row - first - second
    index = lax.broadcasted_iota(jnp.int32, (HALO, row.shape[1]), 0)
    parts = jnp.where(index == 0, first, jnp.where(index == 1, second, jnp.where(index == 2, third, 0.0)))
    result = dot(parts.astype(bf16), swap, ((1,), (0,)))
    return result[0:1] + result[1:2] + result[2:3]


def main_body(core, chips, groups, rank_ref, pieces_in, home_in, *refs):
    arrived_in, refs = refs[: chips - 1], refs[chips - 1 :]
    crossed_in, refs = refs[:groups], refs[groups:]
    gain_ref, pairing_ref, leaving_out, cross_out, own_out = refs[:5]
    pieces, home, crossed, arrived, normed_ref, grads_ref, edge_normed_ref, edge_grads_ref = refs[5:13]
    padded, terms, halves, bent, slopes, total, shifted_ref, kernel_ref, gelu_ref = refs[13:22]
    scaled, leaving, cross, own, sems = refs[22:]
    owners, part, rows = pieces.shape
    strands = normed_ref.shape[0]
    dp_ranks = strands // 2
    moves = Moves(sems)
    got_blocks = [moves.start(home_in, home)]
    got_blocks += [moves.start(block, arrived.at[m]) for m, block in enumerate(arrived_in)]
    per = chips // groups
    got_blocks += [moves.start(crossed_in[m // per].at[m % per], crossed.at[m]) for m in range(chips)]
    got_pieces = None
    masks = chip_masks(2 * chips, core)
    seq_ranks = 2 * chips // dp_ranks
    positions = home.shape[0] - HALO
    channels, width = gain_ref.shape[1], home.shape[1]
    swap = swap_map(pairing_ref[...].reshape(1, -1))
    gains = [gain_ref[...], swapped_row(gain_ref[...], swap)]
    blocks = [(0, home, channels)]
    blocks += [(mask, arrived.at[m], width) for m, mask in enumerate(masks[1:])]
    blocks += [(mask | core, crossed.at[m], channels) for m, mask in enumerate(masks)]
    for got, (flip, ref, lane) in zip(got_blocks, blocks):
        got.wait()
        if got is got_blocks[1]:
            got_pieces = moves.start(pieces_in, pieces)
        source = lax.bitwise_xor(rank_ref[0], flip)
        b, i = lax.rem(source, dp_ranks), lax.div(source, dp_ranks)
        start = pl.multiple_of(i * positions, positions)
        side = jnp.where(i == 0, 0, jnp.where(i == seq_ranks - 1, 1, 2))
        both = normalize(ref[:, :channels], gains)
        for n, normed in enumerate(both):
            first = lane + n * part
            grads = 0.5 * ref[:, first : first + part].astype(f32)
            index = n * dp_ranks + b
            normed_ref[index, pl.ds(start, positions), :] = normed[:positions]
            grads_ref[index, pl.ds(start, positions), :part] = grads[:positions]
            edge_normed_ref[side, index] = normed[positions:]
            edge_grads_ref[side, index, :, :part] = grads[positions:]
    span = normed_ref.shape[1]
    taps = kernel_ref.shape[0] // part
    half = taps // 2
    reach = 2 * half
    wide = bent.shape[0]

    def runs(owner):
        first, last = owner * rows, (owner + 1) * rows
        while first < last:
            tap, channel = divmod(first, channels)
            count = min(last - first, channels - channel)
            yield tap, channel, count, first - owner * rows
            first += count

    got_pieces.wait()
    arrivals = len(moves.copies)
    for owner in range(owners):
        for tap, channel, count, offset in runs(owner):
            kernel_ref[tap * part : (tap + 1) * part, channel : channel + count] = pieces[
                owner, :, offset : offset + count
            ]
    kernel = kernel_ref[...]
    kernels = [kernel, dot(kernel, swap, ((1,), (0,))).astype(bf16)]
    padded[...] = jnp.zeros_like(padded)
    for n in range(2):
        for k in range(taps):
            padded[n, k * LANES : k * LANES + part, :] = kernels[n][k * part : (k + 1) * part, :]
    edge_terms = []
    for n in range(2):
        edges = [
            edge_normed_ref[side, n * dp_ranks + b] for side in range(2) for b in range(dp_ranks)
        ]
        edge_terms.append(dot(jnp.concatenate(edges, 0), padded[n], ((1,), (1,))))
    for strand in range(strands):
        forward = strand < dp_ranks
        n, b = divmod(strand, dp_ranks)
        terms[HALO : HALO + span, :] = dot(normed_ref[strand], padded[n], ((1,), (1,)))
        halves[HALO : HALO + span, :] = grads_ref[strand]
        for side, start in enumerate((0, HALO + span)):
            first = (side * dp_ranks + b) * HALO
            terms[start : start + HALO, :] = edge_terms[n][first : first + HALO]
            halves[start : start + HALO, :] = edge_grads_ref[side, strand]
        preact = jnp.zeros((wide, LANES), f32)
        for k in range(taps):
            start = HALO - reach + k if forward else HALO - k
            preact += terms[start : start + wide, k * LANES : (k + 1) * LANES]
        result, slope = gelu_and_slope(preact)
        bent[...] = result
        gelu_ref[strand] = bent[half : half + span, :].astype(bf16)
        slopes[...] = halves[HALO - half : HALO - half + wide, :] * slope
        for k in range(taps):
            start = reach - k if forward else k
            shifted_ref[strand, :, k * part : (k + 1) * part] = slopes[start : start + span, :part].astype(bf16)
    plain, other = [
        dot(
            shifted_ref[n * dp_ranks : (n + 1) * dp_ranks].reshape(dp_ranks * span, taps * part),
            normed_ref[n * dp_ranks : (n + 1) * dp_ranks].reshape(dp_ranks * span, channels),
            ((0,), (0,)),
        )
        for n in range(2)
    ]
    total[...] = plain + dot(other.astype(bf16), swap, ((1,), (0,)))
    gain = jnp.sum(total[...] * kernel.astype(f32), 0, keepdims=True) / gain_ref[...]
    gain_high = gain.astype(bf16).astype(f32)
    row = lax.broadcasted_iota(jnp.int32, (HALO, channels), 0)
    extra = jnp.where(row == 0, gain_high, jnp.where(row == 1, gain - gain_high, 0.0)).T
    own_gain = channels // owners
    for owner in range(owners):
        for tap, channel, count, offset in runs(owner):
            leaving[owner, :, offset : offset + count] = total[
                tap * part : (tap + 1) * part, channel : channel + count
            ].astype(bf16)
        leaving[owner, :, rows:] = jnp.zeros((part, EXTRA), bf16)
        leaving[owner, :own_gain, rows:] = extra[
            owner * own_gain : (owner + 1) * own_gain, :EXTRA
        ].astype(bf16)
    moves.start(leaving, leaving_out)
    for b in range(dp_ranks):
        scaled[b] = (
            dot(shifted_ref[b], kernels[0], ((1,), (0,))) * gains[0]
            + dot(shifted_ref[dp_ranks + b], kernels[1], ((1,), (0,))) * gains[1]
        ).astype(bf16)
    order = [*range(1, chips), 0]
    for out, target_out, flip in ((cross, cross_out, core), (own, own_out, 0)):
        for m, mask in [(m, masks[m]) for m in order]:
            target = lax.bitwise_xor(rank_ref[0], mask | flip)
            b = lax.rem(target, dp_ranks)
            start = pl.multiple_of(lax.div(target, dp_ranks) * positions, positions)
            out[m, :, :channels] = scaled[b, pl.ds(start, positions), :]
            for n in range(2):
                lane = channels + n * LANES
                out[m, :, lane : lane + LANES] = gelu_ref[n * dp_ranks + b, pl.ds(start, positions), :]
            moves.start(out.at[m], target_out.at[m])
    for copy in moves.copies[arrivals:]:
        copy.wait()


def chip_sum(part, own_in, crossed_in, *refs):
    outs, (own, crossed, sems) = refs[:-3], refs[-3:]
    channels = own.shape[2] - 2 * LANES
    moves = Moves(sems)
    order = [*range(1, len(outs)), 0]
    got = {m: (moves.start(own_in.at[m], own.at[m]), moves.start(crossed_in.at[m], crossed.at[m])) for m in order}
    for m in order:
        for copy in got[m]:
            copy.wait()
        out = outs[m]
        out[:, :channels] = (own[m, :, :channels].astype(f32) + crossed[m, :, :channels].astype(f32)).astype(bf16)
        for c, ref in enumerate((own, crossed)):
            for n in range(2):
                lane = channels + n * LANES
                start = channels + (2 * c + n) * part
                out[:, start : start + part] = ref[m, :, lane : lane + part]


def finish(part, core, rank_ref, values_ref, cot_ref, pairing_ref, *refs):
    arrived, (combined_ref, grad_ref, gelus) = refs[:-3], refs[-3:]
    channels = values_ref.shape[1]
    ranks = gelus.shape[1]
    scaled = jnp.zeros(values_ref.shape, f32)
    for mask, block in zip(chip_masks(ranks, core), arrived):
        scaled += block[:, :channels].astype(f32)
        for c in range(2):
            source = lax.bitwise_xor(rank_ref[0], mask | c * core)
            for n in range(2):
                start = channels + (2 * c + n) * part
                gelus[n, source] = block[:, start : start + part]
    plain, other = [jnp.concatenate([gelus[n, j] for j in range(ranks)], -1) for n in range(2)]
    plain = plain.astype(f32)
    other = dot(other, swap_map(pairing_ref[...].reshape(1, -1)), ((1,), (0,)))
    values = values_ref[...].astype(f32)
    rms = lax.rsqrt(jnp.mean(values * values, -1, keepdims=True) + epsilon)
    reverse_out = (values + other).astype(bf16).astype(f32)
    combined_ref[...] = (0.5 * (values + plain + reverse_out)).astype(bf16)
    along = jnp.mean(scaled * values, -1, keepdims=True)
    grad_ref[...] = (cot_ref[...].astype(f32) + rms * scaled - values * (rms * rms * rms * along)).astype(bf16)


def collect(owner_of, terms_ref, kernel_ref, gain_ref, joined):
    part = terms_ref.shape[1]
    rows = kernel_ref.shape[0]
    own_gain = gain_ref.shape[1]
    joined[...] = jnp.zeros_like(joined)
    gain = jnp.zeros((own_gain, EXTRA), f32)
    for rank, owners in enumerate(owner_of):
        total = terms_ref[owners[0]].astype(f32)
        for owner in owners[1:]:
            total += terms_ref[owner].astype(f32)
        joined[rank * part : (rank + 1) * part, :rows] = total[:, :rows]
        gain += total[:own_gain, rows:]
    channels = kernel_ref.shape[1]
    joined[channels : channels + own_gain, :EXTRA] = gain
    turned = joined[...].T
    kernel_ref[...] = turned[:rows, :channels]
    gain_ref[...] = sum(turned[n : n + 1, channels : channels + own_gain] for n in range(EXTRA))


def flipped_pairs(count, mask):
    return [(i, i ^ mask) for i in range(count)]


def per_device(activations, cotangent, weights, norm_gain, pairing):
    seq_ranks = lax.axis_size("seq_rank")
    dp_ranks = lax.axis_size("dp_rank")
    seq_blocks = lax.axis_size("seq_block")
    dp_blocks = lax.axis_size("dp_block")
    ranks = seq_ranks * dp_ranks
    owners = ranks * seq_blocks * dp_blocks
    positions, channels = activations.shape[1:]
    rows = weights.shape[0]
    taps = rows * owners // channels
    part = channels // ranks
    span = positions * seq_ranks
    long = span + 2 * HALO
    reach = taps - taps % 2
    wide = -(-(span + reach) // 8) * 8
    strands = 2 * dp_ranks
    width = channels + 2 * LANES
    slim = channels + 2 * part
    rank = lax.axis_index(RANK).reshape(1)
    values, cot = activations[0], cotangent[0]
    along = ("seq_block", "seq_rank")
    ends = [(b * seq_ranks - 1, b * seq_ranks) for b in range(1, seq_blocks)]
    both = jnp.concatenate([values, cot], -1)
    edge = jnp.where(lax.axis_index("seq_rank") == 0, both[:HALO], both[-HALO:])
    edge = lax.ppermute(edge, along, ends + [(target, source) for source, target in ends])
    piece_of = [
        sr * dp_ranks + dr
        for _ in range(seq_blocks)
        for sr in range(seq_ranks)
        for _ in range(dp_blocks)
        for dr in range(dp_ranks)
    ]
    square = -(-rows // LANES) * LANES
    slices = called(
        lambda *refs: spread(piece_of, *refs),
        pltpu.HBM((owners, part, rows), bf16),
        (weights,),
        16,
        scratch=[
            pltpu.VMEM((square, channels), f32),
            pltpu.VMEM((owners, part, rows), bf16),
            pltpu.SemaphoreType.DMA((1,)),
        ],
        out_specs=HBM,
    )
    slices, packed = lax.optimization_barrier((slices, values))
    pieces = lax.all_to_all(slices, EVERY, 0, 0, tiled=True)
    gain = norm_gain.reshape(1, channels)
    core = dp_ranks
    masks = chip_masks(ranks, core)
    block = positions + HALO
    home, cross, *leaving = called(
        lambda *refs: pack_messages(part, core, *refs),
        (pltpu.HBM((block, slim), bf16), shape_of((block, slim), bf16))
        + tuple(shape_of((block, slim + 2 * part), bf16) for _ in masks[1:]),
        (rank, packed, cot, edge, pairing),
        16,
        specs=[SMEM] + [VMEM] * 4,
    )
    arrived = [
        lax.ppermute(message, RANK, flipped_pairs(ranks, mask))
        for message, mask in zip(leaving, masks[1:])
    ]
    both_cores = []
    for group in ((cross, *arrived),):
        crossing = called(stack_crossing, shape_of((len(group), block, slim), bf16), group, 8)
        both_cores.append(lax.ppermute(crossing, RANK, flipped_pairs(ranks, core)))
    home = pltpu.with_memory_space_constraint(home, pltpu.HBM)
    held = (pieces, home, *arrived, *both_cores)
    halves = (len(masks), positions, width)
    shapes = ((owners, part, rows + EXTRA), halves, halves)
    groups = len(both_cores)
    outgoing, cross, own = called(
        lambda *refs: main_body(core, len(masks), groups, *refs),
        tuple(pltpu.HBM(shape, bf16) for shape in shapes),
        (rank, *held, gain, pairing),
        44,
        scratch=[
            pltpu.VMEM(pieces.shape, bf16),
            pltpu.VMEM(home.shape, bf16),
            pltpu.VMEM((len(masks), block, slim), bf16),
            pltpu.VMEM((len(arrived), *arrived[0].shape), bf16),
            pltpu.VMEM((strands, span, channels), bf16),
            pltpu.VMEM((strands, span, LANES), f32),
            pltpu.VMEM((3, strands, HALO, channels), bf16),
            pltpu.VMEM((3, strands, HALO, LANES), f32),
            pltpu.VMEM((2, taps * LANES, channels), bf16),
            pltpu.VMEM((long, taps * LANES), f32),
            pltpu.VMEM((long, LANES), f32),
            pltpu.VMEM((wide, LANES), f32),
            pltpu.VMEM((wide, LANES), f32),
            pltpu.VMEM((taps * part, channels), f32),
            pltpu.VMEM((strands, span, taps * part), bf16),
            pltpu.VMEM((taps * part, channels), bf16),
            pltpu.VMEM((strands, span, LANES), bf16),
            pltpu.VMEM((dp_ranks, span, channels), bf16),
        ]
        + [pltpu.VMEM(shape, bf16) for shape in shapes]
        + [pltpu.SemaphoreType.DMA((2 * ranks + 4,))],
        specs=[SMEM, ANY, HBM] + [ANY] * (len(held) - 2) + [VMEM] * 2,
        out_specs=(HBM,) * 3,
    )
    terms = lax.all_to_all(outgoing, EVERY, 0, 0, tiled=True)
    crossed = lax.ppermute(cross, RANK, flipped_pairs(ranks, core))
    own = pltpu.with_memory_space_constraint(own, pltpu.HBM)
    leaving = called(
        lambda *refs: chip_sum(part, *refs),
        tuple(shape_of((positions, channels + 4 * part), bf16) for _ in masks),
        (own, crossed),
        16,
        scratch=[pltpu.VMEM(halves, bf16)] * 2 + [pltpu.SemaphoreType.DMA((2 * len(masks),))],
        specs=[HBM, ANY],
    )
    arrived = leaving[:1] + tuple(
        lax.ppermute(message, RANK, flipped_pairs(ranks, mask))
        for message, mask in zip(leaving[1:], masks[1:])
    )
    order = [
        [
            ((sb * seq_ranks + sr) * dp_blocks + db) * dp_ranks + dr
            for sb in range(seq_blocks)
            for db in range(dp_blocks)
        ]
        for sr in range(seq_ranks)
        for dr in range(dp_ranks)
    ]
    grad_kernel, grad_gain = called(
        lambda *refs: collect(order, *refs),
        (shape_of((rows, channels), f32), shape_of((1, channels // owners), f32)),
        (terms,),
        16,
        scratch=[pltpu.VMEM((channels + LANES, -(-rows // LANES) * LANES), f32)],
    )
    grad_kernel, home, *arrived = lax.optimization_barrier((grad_kernel, *arrived))
    combined, grad_input = called(
        lambda *refs: finish(part, core, *refs),
        (shape_of((positions, channels), bf16), shape_of((positions, channels), bf16)),
        (rank, values, cot, pairing, home, *arrived),
        16,
        scratch=[pltpu.VMEM((2, ranks, positions, part), bf16)],
        specs=[SMEM] + [VMEM] * (4 + len(arrived)),
    )
    return combined[None], grad_input[None], grad_kernel, grad_gain[0]


def solution(mesh):
    seq, dp = mesh.shape["seq"], mesh.shape["dp"]
    seq_ranks, dp_ranks = 4, 2
    grouped = Mesh(mesh.devices.reshape(seq // seq_ranks, seq_ranks, dp // dp_ranks, dp_ranks), EVERY)
    along = P(("dp_block", "dp_rank"), ("seq_block", "seq_rank"), None)
    return jax.shard_map(
        per_device,
        mesh=grouped,
        in_specs=(along, along, P(EVERY, None), P(), P()),
        out_specs=(along, along, P(EVERY, None), P(EVERY)),
        check_vma=False,
    )
```

```python
import jax
import jax.numpy as jnp
from jax import lax
from jax.experimental import pallas as pl
from jax.experimental.pallas import tpu as pltpu
from jax.sharding import Mesh, PartitionSpec as P

epsilon = 1e-06
RANK = ("seq_rank", "dp_rank")
EVERY = ("seq_block", "seq_rank", "dp_block", "dp_rank")
LANES = 128
HALO = 16
EDGE = 8
EXTRA = 2
VMEM = pl.BlockSpec(memory_space=pltpu.VMEM)
SMEM = pl.BlockSpec(memory_space=pltpu.SMEM)
HBM = pl.BlockSpec(memory_space=pltpu.HBM)
ANY = pl.BlockSpec(memory_space=pl.ANY)
bf16 = jnp.bfloat16
f32 = jnp.float32


def called(body, outs, args, vmem, scratch=(), specs=None, out_specs=None):
    return pl.pallas_call(
        body,
        out_shape=outs,
        in_specs=specs or [VMEM] * len(args),
        out_specs=out_specs or jax.tree.map(lambda _: VMEM, outs),
        scratch_shapes=list(scratch),
        compiler_params=pltpu.CompilerParams(vmem_limit_bytes=vmem * 2**20),
        cost_estimate=pl.CostEstimate(flops=0, bytes_accessed=0, transcendentals=0),
    )(*args)


def shape_of(shape, dtype):
    return jax.ShapeDtypeStruct(shape, dtype)


def dot(a, b, contract):
    return lax.dot_general(a, b, (contract, ((), ())), preferred_element_type=f32)


def gelu_and_slope(x):
    inner = 0.7978845608028654 * (x + 0.044715 * (x * x * x))
    bend = jnp.tanh(inner)
    half_sum = 0.5 * (1.0 + bend)
    slope = half_sum + (0.5 * x) * (1.0 - bend * bend) * (
        0.7978845608028654 * (1.0 + 0.134145 * (x * x))
    )
    return x * half_sum, slope


def swap_map(pairing):
    channels = pairing.shape[1]
    row = lax.broadcasted_iota(jnp.int32, (channels, channels), 0)
    return jnp.where(row == pairing, 1.0, 0.0).astype(bf16)


def chip_masks(ranks, core):
    masks = [mask for mask in range(ranks) if not mask & core]
    return masks[:1] + sorted(masks[1:], key=lambda mask: -mask.bit_count())


class Moves:
    def __init__(self, sems):
        self.sems, self.copies = sems, []

    def start(self, source, target):
        copy = pltpu.make_async_copy(source, target, self.sems.at[len(self.copies)])
        copy.start()
        self.copies.append(copy)
        return copy

    def wait(self):
        for copy in self.copies:
            copy.wait()


def spread(piece_of, weights_ref, out_ref, square, sent, sems):
    rows, channels = weights_ref.shape
    part = out_ref.shape[1]
    square[...] = jnp.zeros_like(square)
    square[:rows] = weights_ref[...].astype(f32)
    turned = square[...].T.astype(bf16)
    for owner, piece in enumerate(piece_of):
        sent[owner] = turned[piece * part : (piece + 1) * part, :rows]
    moves = Moves(sems)
    moves.start(sent, out_ref)
    moves.wait()


def pack_messages(part, core, rank_ref, values_ref, cot_ref, edge_ref, pairing_ref, *outs):
    positions, channels = values_ref.shape
    home_ref, cross_ref, leaving = outs[0], outs[1], outs[2:]
    masks = chip_masks(2 * (len(leaving) + 1), core)
    flips = [mask | c for mask in masks[1:] for c in (core, 0)] + [0, core]
    shape = (part, channels)
    row = lax.broadcasted_iota(jnp.int32, shape, 0)
    column = lax.broadcasted_iota(jnp.int32, shape, 1)
    offsets = [column - row, pairing_ref[...].reshape(1, -1) - row]
    maps = [
        jnp.where(offset == lax.bitwise_xor(rank_ref[0], flip) * part, 1.0, 0.0).astype(bf16)
        for flip in flips
        for offset in offsets
    ]
    maps = jnp.concatenate(maps, 0)
    cot = jnp.concatenate([cot_ref[...], edge_ref[:, channels:]], 0)
    slices = dot(cot, maps, ((1,), (1,))).astype(bf16)
    lane = 0
    for out in (*leaving, home_ref, cross_ref):
        count = out.shape[1] - channels
        out[:positions, :channels] = values_ref[...]
        out[positions:, :channels] = edge_ref[:, :channels]
        out[:, channels:] = slices[:, lane : lane + count]
        lane += count


def stack_crossing(*refs):
    out_ref = refs[-1]
    width = out_ref.shape[2]
    for m, ref in enumerate(refs[:-1]):
        out_ref[m] = ref[:, :width]


def normalize(x, gains):
    x = x.astype(f32)
    x = x * lax.rsqrt(jnp.mean(x * x, -1, keepdims=True) + epsilon)
    return [(x * gain).astype(bf16) for gain in gains]


def swapped_row(row, swap):
    first = row.astype(bf16).astype(f32)
    second = (row - first).astype(bf16).astype(f32)
    third = row - first - second
    index = lax.broadcasted_iota(jnp.int32, (HALO, row.shape[1]), 0)
    parts = jnp.where(index == 0, first, jnp.where(index == 1, second, jnp.where(index == 2, third, 0.0)))
    result = dot(parts.astype(bf16), swap, ((1,), (0,)))
    return result[0:1] + result[1:2] + result[2:3]


def main_body(core, chips, groups, rank_ref, pieces_in, home_in, *refs):
    arrived_in, refs = refs[: chips - 1], refs[chips - 1 :]
    crossed_in, refs = refs[:groups], refs[groups:]
    gain_ref, pairing_ref, leaving_out, cross_out, own_out = refs[:5]
    pieces, home, crossed, arrived, normed_ref, grads_ref, edge_normed_ref, edge_grads_ref = refs[5:13]
    padded, terms, halves, bent, slopes, total, shifted_ref, kernel_ref, gelu_ref = refs[13:22]
    scaled, leaving, cross, own, sems = refs[22:]
    owners, part, rows = pieces.shape
    strands = normed_ref.shape[0]
    dp_ranks = strands // 2
    moves = Moves(sems)
    got_blocks = [moves.start(home_in, home)]
    got_blocks += [moves.start(block, arrived.at[m]) for m, block in enumerate(arrived_in)]
    per = chips // groups
    got_blocks += [moves.start(crossed_in[m // per].at[m % per], crossed.at[m]) for m in range(chips)]
    got_pieces = None
    masks = chip_masks(2 * chips, core)
    seq_ranks = 2 * chips // dp_ranks
    positions = home.shape[0] - EDGE
    channels, width = gain_ref.shape[1], home.shape[1]
    swap = swap_map(pairing_ref[...].reshape(1, -1))
    gains = [gain_ref[...], swapped_row(gain_ref[...], swap)]
    blocks = [(0, home, channels)]
    blocks += [(mask, arrived.at[m], width) for m, mask in enumerate(masks[1:])]
    blocks += [(mask | core, crossed.at[m], channels) for m, mask in enumerate(masks)]
    for got, (flip, ref, lane) in zip(got_blocks, blocks):
        got.wait()
        if got is got_blocks[1]:
            got_pieces = moves.start(pieces_in, pieces)
        source = lax.bitwise_xor(rank_ref[0], flip)
        b, i = lax.rem(source, dp_ranks), lax.div(source, dp_ranks)
        start = pl.multiple_of(i * positions, positions)
        side = jnp.where(i == 0, 0, jnp.where(i == seq_ranks - 1, 1, 2))
        both = normalize(ref[:, :channels], gains)
        for n, normed in enumerate(both):
            first = lane + n * part
            grads = 0.5 * ref[:, first : first + part].astype(f32)
            index = n * dp_ranks + b
            normed_ref[index, pl.ds(start, positions), :] = normed[:positions]
            grads_ref[index, pl.ds(start, positions), :part] = grads[:positions]
            edge_normed_ref[side, index] = normed[positions:].astype(f32)
            edge_grads_ref[side, index, :, :part] = grads[positions:]
    span = normed_ref.shape[1]
    taps = kernel_ref.shape[0] // part
    half = taps // 2
    reach = 2 * half
    wide = bent.shape[0]

    def runs(owner):
        first, last = owner * rows, (owner + 1) * rows
        while first < last:
            tap, channel = divmod(first, channels)
            count = min(last - first, channels - channel)
            yield tap, channel, count, first - owner * rows
            first += count

    got_pieces.wait()
    arrivals = len(moves.copies)
    for owner in range(owners):
        for tap, channel, count, offset in runs(owner):
            kernel_ref[tap * part : (tap + 1) * part, channel : channel + count] = pieces[
                owner, :, offset : offset + count
            ]
    kernel = kernel_ref[...]
    kernels = [kernel, dot(kernel, swap, ((1,), (0,))).astype(bf16)]
    padded[...] = jnp.zeros_like(padded)
    for n in range(2):
        for k in range(taps):
            padded[n, k * LANES : k * LANES + part, :] = kernels[n][k * part : (k + 1) * part, :]
    edge_terms = []
    for n in range(2):
        edges = [
            edge_normed_ref[side, n * dp_ranks + b] for side in range(2) for b in range(dp_ranks)
        ]
        edge_terms.append(dot(jnp.concatenate(edges, 0).astype(bf16), padded[n], ((1,), (1,))))
    for strand in range(strands):
        forward = strand < dp_ranks
        n, b = divmod(strand, dp_ranks)
        terms[HALO : HALO + span, :] = dot(normed_ref[strand], padded[n], ((1,), (1,)))
        halves[HALO : HALO + span, :] = grads_ref[strand]
        for side, start in enumerate((HALO - EDGE, HALO + span)):
            first = (side * dp_ranks + b) * EDGE
            terms[start : start + EDGE, :] = edge_terms[n][first : first + EDGE]
            halves[start : start + EDGE, :] = edge_grads_ref[side, strand]
        preact = jnp.zeros((wide, LANES), f32)
        for k in range(taps):
            start = HALO - reach + k if forward else HALO - k
            preact += terms[start : start + wide, k * LANES : (k + 1) * LANES]
        result, slope = gelu_and_slope(preact)
        bent[...] = result
        gelu_ref[strand] = bent[half : half + span, :].astype(bf16)
        slopes[...] = halves[HALO - half : HALO - half + wide, :] * slope
        for k in range(taps):
            start = reach - k if forward else k
            shifted_ref[strand, :, k * part : (k + 1) * part] = slopes[start : start + span, :part].astype(bf16)
    plain, other = [
        dot(
            shifted_ref[n * dp_ranks : (n + 1) * dp_ranks].reshape(dp_ranks * span, taps * part),
            normed_ref[n * dp_ranks : (n + 1) * dp_ranks].reshape(dp_ranks * span, channels),
            ((0,), (0,)),
        )
        for n in range(2)
    ]
    total[...] = plain + dot(other.astype(bf16), swap, ((1,), (0,)))
    gain = jnp.sum(total[...] * kernel.astype(f32), 0, keepdims=True) / gain_ref[...]
    gain_high = gain.astype(bf16).astype(f32)
    row = lax.broadcasted_iota(jnp.int32, (HALO, channels), 0)
    extra = jnp.where(row == 0, gain_high, jnp.where(row == 1, gain - gain_high, 0.0)).T
    own_gain = channels // owners
    for owner in range(owners):
        for tap, channel, count, offset in runs(owner):
            leaving[owner, :, offset : offset + count] = total[
                tap * part : (tap + 1) * part, channel : channel + count
            ].astype(bf16)
        leaving[owner, :, rows:] = jnp.zeros((part, EXTRA), bf16)
        leaving[owner, :own_gain, rows:] = extra[
            owner * own_gain : (owner + 1) * own_gain, :EXTRA
        ].astype(bf16)
    moves.start(leaving, leaving_out)
    for b in range(dp_ranks):
        scaled[b] = (
            dot(shifted_ref[b], kernels[0], ((1,), (0,))) * gains[0]
            + dot(shifted_ref[dp_ranks + b], kernels[1], ((1,), (0,))) * gains[1]
        ).astype(bf16)
    order = [*range(1, chips), 0]
    for out, target_out, flip in ((cross, cross_out, core), (own, own_out, 0)):
        for m, mask in [(m, masks[m]) for m in order]:
            target = lax.bitwise_xor(rank_ref[0], mask | flip)
            b = lax.rem(target, dp_ranks)
            start = pl.multiple_of(lax.div(target, dp_ranks) * positions, positions)
            out[m, :, :channels] = scaled[b, pl.ds(start, positions), :]
            for n in range(2):
                lane = channels + n * LANES
                out[m, :, lane : lane + LANES] = gelu_ref[n * dp_ranks + b, pl.ds(start, positions), :]
            moves.start(out.at[m], target_out.at[m])
    for copy in moves.copies[arrivals:]:
        copy.wait()


def chip_sum(part, own_ref, crossed_ref, *outs):
    channels = own_ref.shape[2] - 2 * LANES
    for m, out in enumerate(outs):
        out[:, :channels] = (
            own_ref[m, :, :channels].astype(f32) + crossed_ref[m, :, :channels].astype(f32)
        ).astype(bf16)
        for c, ref in enumerate((own_ref, crossed_ref)):
            for n in range(2):
                lane = channels + n * LANES
                start = channels + (2 * c + n) * part
                out[:, start : start + part] = ref[m, :, lane : lane + part]


def finish(part, core, rank_ref, values_ref, cot_ref, pairing_ref, *refs):
    arrived, (combined_ref, grad_ref, gelus) = refs[:-3], refs[-3:]
    channels = values_ref.shape[1]
    ranks = gelus.shape[1]
    scaled = jnp.zeros(values_ref.shape, f32)
    for mask, block in zip(chip_masks(ranks, core), arrived):
        scaled += block[:, :channels].astype(f32)
        for c in range(2):
            source = lax.bitwise_xor(rank_ref[0], mask | c * core)
            for n in range(2):
                start = channels + (2 * c + n) * part
                gelus[n, source] = block[:, start : start + part]
    plain, other = [jnp.concatenate([gelus[n, j] for j in range(ranks)], -1) for n in range(2)]
    plain = plain.astype(f32)
    other = dot(other, swap_map(pairing_ref[...].reshape(1, -1)), ((1,), (0,)))
    values = values_ref[...].astype(f32)
    rms = lax.rsqrt(jnp.mean(values * values, -1, keepdims=True) + epsilon)
    reverse_out = (values + other).astype(bf16).astype(f32)
    combined_ref[...] = (0.5 * (values + plain + reverse_out)).astype(bf16)
    along = jnp.mean(scaled * values, -1, keepdims=True)
    grad_ref[...] = (cot_ref[...].astype(f32) + rms * scaled - values * (rms * rms * rms * along)).astype(bf16)


def collect(owner_of, terms_ref, kernel_ref, gain_ref, joined):
    part = terms_ref.shape[1]
    rows = kernel_ref.shape[0]
    own_gain = gain_ref.shape[1]
    joined[...] = jnp.zeros_like(joined)
    gain = jnp.zeros((own_gain, EXTRA), f32)
    for rank, owners in enumerate(owner_of):
        total = terms_ref[owners[0]].astype(f32)
        for owner in owners[1:]:
            total += terms_ref[owner].astype(f32)
        joined[rank * part : (rank + 1) * part, :rows] = total[:, :rows]
        gain += total[:own_gain, rows:]
    channels = kernel_ref.shape[1]
    joined[channels : channels + own_gain, :EXTRA] = gain
    turned = joined[...].T
    kernel_ref[...] = turned[:rows, :channels]
    gain_ref[...] = sum(turned[n : n + 1, channels : channels + own_gain] for n in range(EXTRA))


def flipped_pairs(count, mask):
    return [(i, i ^ mask) for i in range(count)]


def per_device(activations, cotangent, weights, norm_gain, pairing):
    seq_ranks = lax.axis_size("seq_rank")
    dp_ranks = lax.axis_size("dp_rank")
    seq_blocks = lax.axis_size("seq_block")
    dp_blocks = lax.axis_size("dp_block")
    ranks = seq_ranks * dp_ranks
    owners = ranks * seq_blocks * dp_blocks
    positions, channels = activations.shape[1:]
    rows = weights.shape[0]
    taps = rows * owners // channels
    part = channels // ranks
    span = positions * seq_ranks
    long = span + 2 * HALO
    reach = taps - taps % 2
    wide = -(-(span + reach) // 8) * 8
    strands = 2 * dp_ranks
    width = channels + 2 * LANES
    slim = channels + 2 * part
    rank = lax.axis_index(RANK).reshape(1)
    values, cot = activations[0], cotangent[0]
    along = ("seq_block", "seq_rank")
    ends = [(b * seq_ranks - 1, b * seq_ranks) for b in range(1, seq_blocks)]
    both = jnp.concatenate([values, cot], -1)
    edge = jnp.where(lax.axis_index("seq_rank") == 0, both[:EDGE], both[-EDGE:])
    edge = lax.ppermute(edge, along, ends + [(target, source) for source, target in ends])
    piece_of = [
        sr * dp_ranks + dr
        for _ in range(seq_blocks)
        for sr in range(seq_ranks)
        for _ in range(dp_blocks)
        for dr in range(dp_ranks)
    ]
    square = -(-rows // LANES) * LANES
    slices = called(
        lambda *refs: spread(piece_of, *refs),
        pltpu.HBM((owners, part, rows), bf16),
        (weights,),
        16,
        scratch=[
            pltpu.VMEM((square, channels), f32),
            pltpu.VMEM((owners, part, rows), bf16),
            pltpu.SemaphoreType.DMA((1,)),
        ],
        out_specs=HBM,
    )
    slices, packed = lax.optimization_barrier((slices, values))
    pieces = lax.all_to_all(slices, EVERY, 0, 0, tiled=True)
    gain = norm_gain.reshape(1, channels)
    core = dp_ranks
    masks = chip_masks(ranks, core)
    block = positions + EDGE
    home, cross, *leaving = called(
        lambda *refs: pack_messages(part, core, *refs),
        (pltpu.HBM((block, slim), bf16), shape_of((block, slim), bf16))
        + tuple(shape_of((block, slim + 2 * part), bf16) for _ in masks[1:]),
        (rank, packed, cot, edge, pairing),
        16,
        specs=[SMEM] + [VMEM] * 4,
    )
    arrived = [
        lax.ppermute(message, RANK, flipped_pairs(ranks, mask))
        for message, mask in zip(leaving, masks[1:])
    ]
    both_cores = []
    for group in ((cross, *arrived),):
        crossing = called(stack_crossing, shape_of((len(group), block, slim), bf16), group, 8)
        both_cores.append(lax.ppermute(crossing, RANK, flipped_pairs(ranks, core)))
    home = pltpu.with_memory_space_constraint(home, pltpu.HBM)
    held = (pieces, home, *arrived, *both_cores)
    halves = (len(masks), positions, width)
    shapes = ((owners, part, rows + EXTRA), halves, halves)
    groups = len(both_cores)
    outgoing, cross, own = called(
        lambda *refs: main_body(core, len(masks), groups, *refs),
        tuple(pltpu.HBM(shape, bf16) for shape in shapes),
        (rank, *held, gain, pairing),
        44,
        scratch=[
            pltpu.VMEM(pieces.shape, bf16),
            pltpu.VMEM(home.shape, bf16),
            pltpu.VMEM((len(masks), block, slim), bf16),
            pltpu.VMEM((len(arrived), *arrived[0].shape), bf16),
            pltpu.VMEM((strands, span, channels), bf16),
            pltpu.VMEM((strands, span, LANES), f32),
            pltpu.VMEM((3, strands, EDGE, channels), f32),
            pltpu.VMEM((3, strands, EDGE, LANES), f32),
            pltpu.VMEM((2, taps * LANES, channels), bf16),
            pltpu.VMEM((long, taps * LANES), f32),
            pltpu.VMEM((long, LANES), f32),
            pltpu.VMEM((wide, LANES), f32),
            pltpu.VMEM((wide, LANES), f32),
            pltpu.VMEM((taps * part, channels), f32),
            pltpu.VMEM((strands, span, taps * part), bf16),
            pltpu.VMEM((taps * part, channels), bf16),
            pltpu.VMEM((strands, span, LANES), bf16),
            pltpu.VMEM((dp_ranks, span, channels), bf16),
        ]
        + [pltpu.VMEM(shape, bf16) for shape in shapes]
        + [pltpu.SemaphoreType.DMA((2 * ranks + 4,))],
        specs=[SMEM, ANY, HBM] + [ANY] * (len(held) - 2) + [VMEM] * 2,
        out_specs=(HBM,) * 3,
    )
    terms = lax.all_to_all(outgoing, EVERY, 0, 0, tiled=True)
    crossed = lax.ppermute(cross, RANK, flipped_pairs(ranks, core))
    leaving = called(
        lambda *refs: chip_sum(part, *refs),
        tuple(shape_of((positions, channels + 4 * part), bf16) for _ in masks),
        (own, crossed),
        8,
    )
    arrived = leaving[:1] + tuple(
        lax.ppermute(message, RANK, flipped_pairs(ranks, mask))
        for message, mask in zip(leaving[1:], masks[1:])
    )
    order = [
        [
            ((sb * seq_ranks + sr) * dp_blocks + db) * dp_ranks + dr
            for sb in range(seq_blocks)
            for db in range(dp_blocks)
        ]
        for sr in range(seq_ranks)
        for dr in range(dp_ranks)
    ]
    grad_kernel, grad_gain = called(
        lambda *refs: collect(order, *refs),
        (shape_of((rows, channels), f32), shape_of((1, channels // owners), f32)),
        (terms,),
        16,
        scratch=[pltpu.VMEM((channels + LANES, -(-rows // LANES) * LANES), f32)],
    )
    grad_kernel, home, *arrived = lax.optimization_barrier((grad_kernel, *arrived))
    combined, grad_input = called(
        lambda *refs: finish(part, core, *refs),
        (shape_of((positions, channels), bf16), shape_of((positions, channels), bf16)),
        (rank, values, cot, pairing, home, *arrived),
        16,
        scratch=[pltpu.VMEM((2, ranks, positions, part), bf16)],
        specs=[SMEM] + [VMEM] * (4 + len(arrived)),
    )
    return combined[None], grad_input[None], grad_kernel, grad_gain[0]


def solution(mesh):
    seq, dp = mesh.shape["seq"], mesh.shape["dp"]
    seq_ranks, dp_ranks = 4, 2
    grouped = Mesh(mesh.devices.reshape(seq // seq_ranks, seq_ranks, dp // dp_ranks, dp_ranks), EVERY)
    along = P(("dp_block", "dp_rank"), ("seq_block", "seq_rank"), None)
    return jax.shard_map(
        per_device,
        mesh=grouped,
        in_specs=(along, along, P(EVERY, None), P(), P()),
        out_specs=(along, along, P(EVERY, None), P(EVERY)),
        check_vma=False,
    )
```

```python
import jax
import jax.numpy as jnp
from jax import lax
from jax.experimental import pallas as pl
from jax.experimental.pallas import tpu as pltpu
from jax.sharding import Mesh, PartitionSpec as P

epsilon = 1e-06
RANK = ("seq_rank", "dp_rank")
EVERY = ("seq_block", "seq_rank", "dp_block", "dp_rank")
LANES = 128
HALO = 16
EDGE = 8
EXTRA = 2
VMEM = pl.BlockSpec(memory_space=pltpu.VMEM)
SMEM = pl.BlockSpec(memory_space=pltpu.SMEM)
HBM = pl.BlockSpec(memory_space=pltpu.HBM)
ANY = pl.BlockSpec(memory_space=pl.ANY)
bf16 = jnp.bfloat16
f32 = jnp.float32


def called(body, outs, args, vmem, scratch=(), specs=None, out_specs=None):
    return pl.pallas_call(
        body,
        out_shape=outs,
        in_specs=specs or [VMEM] * len(args),
        out_specs=out_specs or jax.tree.map(lambda _: VMEM, outs),
        scratch_shapes=list(scratch),
        compiler_params=pltpu.CompilerParams(vmem_limit_bytes=vmem * 2**20),
        cost_estimate=pl.CostEstimate(flops=0, bytes_accessed=0, transcendentals=0),
    )(*args)


def shape_of(shape, dtype):
    return jax.ShapeDtypeStruct(shape, dtype)


def dot(a, b, contract):
    return lax.dot_general(a, b, (contract, ((), ())), preferred_element_type=f32)


def gelu_and_slope(x):
    inner = 0.7978845608028654 * (x + 0.044715 * (x * x * x))
    bend = jnp.tanh(inner)
    half_sum = 0.5 * (1.0 + bend)
    slope = half_sum + (0.5 * x) * (1.0 - bend * bend) * (
        0.7978845608028654 * (1.0 + 0.134145 * (x * x))
    )
    return x * half_sum, slope


def swap_map(pairing):
    channels = pairing.shape[1]
    row = lax.broadcasted_iota(jnp.int32, (channels, channels), 0)
    return jnp.where(row == pairing, 1.0, 0.0).astype(bf16)


def chip_masks(ranks, core):
    masks = [mask for mask in range(ranks) if not mask & core]
    return masks[:1] + sorted(masks[1:], key=lambda mask: -mask.bit_count())


class Moves:
    def __init__(self, sems):
        self.sems, self.copies = sems, []

    def start(self, source, target):
        copy = pltpu.make_async_copy(source, target, self.sems.at[len(self.copies)])
        copy.start()
        self.copies.append(copy)
        return copy

    def wait(self):
        for copy in self.copies:
            copy.wait()


def spread(piece_of, weights_ref, out_ref, square, sent, sems):
    rows, channels = weights_ref.shape
    part = out_ref.shape[1]
    square[...] = jnp.zeros_like(square)
    square[:rows] = weights_ref[...].astype(f32)
    turned = square[...].T.astype(bf16)
    for owner, piece in enumerate(piece_of):
        sent[owner] = turned[piece * part : (piece + 1) * part, :rows]
    moves = Moves(sems)
    moves.start(sent, out_ref)
    moves.wait()


def pack_messages(part, core, rank_ref, values_ref, cot_ref, edge_ref, pairing_ref, *outs):
    positions, channels = values_ref.shape
    home_ref, cross_ref, leaving = outs[0], outs[1], outs[2:]
    masks = chip_masks(2 * (len(leaving) + 1), core)
    flips = [mask | c for mask in masks[1:] for c in (core, 0)] + [0, core]
    shape = (part, channels)
    row = lax.broadcasted_iota(jnp.int32, shape, 0)
    column = lax.broadcasted_iota(jnp.int32, shape, 1)
    offsets = [column - row, pairing_ref[...].reshape(1, -1) - row]
    maps = [
        jnp.where(offset == lax.bitwise_xor(rank_ref[0], flip) * part, 1.0, 0.0).astype(bf16)
        for flip in flips
        for offset in offsets
    ]
    maps = jnp.concatenate(maps, 0)
    cot = jnp.concatenate([cot_ref[...], edge_ref[:, channels:]], 0)
    slices = dot(cot, maps, ((1,), (1,))).astype(bf16)
    lane = 0
    for out in (*leaving, home_ref, cross_ref):
        count = out.shape[1] - channels
        out[:positions, :channels] = values_ref[...]
        out[positions:, :channels] = edge_ref[:, :channels]
        out[:, channels:] = slices[:, lane : lane + count]
        lane += count


def stack_crossing(*refs):
    out_ref = refs[-1]
    for m, ref in enumerate(refs[:-1]):
        out_ref[m, :, : ref.shape[1]] = ref[...]


def normalize(x, gains):
    x = x.astype(f32)
    x = x * lax.rsqrt(jnp.mean(x * x, -1, keepdims=True) + epsilon)
    return [(x * gain).astype(bf16) for gain in gains]


def swapped_row(row, swap):
    first = row.astype(bf16).astype(f32)
    second = (row - first).astype(bf16).astype(f32)
    third = row - first - second
    index = lax.broadcasted_iota(jnp.int32, (HALO, row.shape[1]), 0)
    parts = jnp.where(index == 0, first, jnp.where(index == 1, second, jnp.where(index == 2, third, 0.0)))
    result = dot(parts.astype(bf16), swap, ((1,), (0,)))
    return result[0:1] + result[1:2] + result[2:3]


def main_body(core, chips, groups, rank_ref, pieces_in, home_in, *refs):
    arrived_in, refs = refs[: chips - 1], refs[chips - 1 :]
    crossed_in, refs = refs[:groups], refs[groups:]
    gain_ref, pairing_ref, leaving_out, cross_out, own_out = refs[:5]
    pieces, home, crossed, arrived, normed_ref, grads_ref, edge_normed_ref, edge_grads_ref = refs[5:13]
    padded, terms, halves, bent, slopes, total, shifted_ref, kernel_ref, gelu_ref = refs[13:22]
    scaled, leaving, cross, own, sems = refs[22:]
    owners, part, rows = pieces.shape
    strands = normed_ref.shape[0]
    dp_ranks = strands // 2
    moves = Moves(sems)
    got_blocks = [moves.start(home_in, home)]
    got_blocks += [moves.start(block, arrived.at[m]) for m, block in enumerate(arrived_in)]
    per = chips // groups
    got_blocks += [moves.start(crossed_in[m // per].at[m % per], crossed.at[m]) for m in range(chips)]
    got_pieces = None
    masks = chip_masks(2 * chips, core)
    seq_ranks = 2 * chips // dp_ranks
    positions = home.shape[0] - EDGE
    channels, width = gain_ref.shape[1], home.shape[1]
    swap = swap_map(pairing_ref[...].reshape(1, -1))
    gains = [gain_ref[...], swapped_row(gain_ref[...], swap)]
    blocks = [(0, home, channels)]
    blocks += [(mask, arrived.at[m], width) for m, mask in enumerate(masks[1:])]
    blocks += [(mask | core, crossed.at[m], channels) for m, mask in enumerate(masks)]
    for got, (flip, ref, lane) in zip(got_blocks, blocks):
        got.wait()
        if got is got_blocks[1]:
            got_pieces = moves.start(pieces_in, pieces)
        source = lax.bitwise_xor(rank_ref[0], flip)
        b, i = lax.rem(source, dp_ranks), lax.div(source, dp_ranks)
        start = pl.multiple_of(i * positions, positions)
        side = jnp.where(i == 0, 0, jnp.where(i == seq_ranks - 1, 1, 2))
        both = normalize(ref[:, :channels], gains)
        for n, normed in enumerate(both):
            first = lane + n * part
            grads = 0.5 * ref[:, first : first + part].astype(f32)
            index = n * dp_ranks + b
            normed_ref[index, pl.ds(start, positions), :] = normed[:positions]
            grads_ref[index, pl.ds(start, positions), :part] = grads[:positions]
            edge_normed_ref[side, index] = normed[positions:].astype(f32)
            edge_grads_ref[side, index, :, :part] = grads[positions:]
    span = normed_ref.shape[1]
    taps = kernel_ref.shape[0] // part
    half = taps // 2
    reach = 2 * half
    wide = bent.shape[0]

    def runs(owner):
        first, last = owner * rows, (owner + 1) * rows
        while first < last:
            tap, channel = divmod(first, channels)
            count = min(last - first, channels - channel)
            yield tap, channel, count, first - owner * rows
            first += count

    got_pieces.wait()
    arrivals = len(moves.copies)
    for owner in range(owners):
        for tap, channel, count, offset in runs(owner):
            kernel_ref[tap * part : (tap + 1) * part, channel : channel + count] = pieces[
                owner, :, offset : offset + count
            ]
    kernel = kernel_ref[...]
    kernels = [kernel, dot(kernel, swap, ((1,), (0,))).astype(bf16)]
    padded[...] = jnp.zeros_like(padded)
    for n in range(2):
        for k in range(taps):
            padded[n, k * LANES : k * LANES + part, :] = kernels[n][k * part : (k + 1) * part, :]
    edge_terms = []
    for n in range(2):
        edges = [
            edge_normed_ref[side, n * dp_ranks + b] for side in range(2) for b in range(dp_ranks)
        ]
        edge_terms.append(dot(jnp.concatenate(edges, 0).astype(bf16), padded[n], ((1,), (1,))))
    for strand in range(strands):
        forward = strand < dp_ranks
        n, b = divmod(strand, dp_ranks)
        terms[HALO : HALO + span, :] = dot(normed_ref[strand], padded[n], ((1,), (1,)))
        halves[HALO : HALO + span, :] = grads_ref[strand]
        for side, start in enumerate((HALO - EDGE, HALO + span)):
            first = (side * dp_ranks + b) * EDGE
            terms[start : start + EDGE, :] = edge_terms[n][first : first + EDGE]
            halves[start : start + EDGE, :] = edge_grads_ref[side, strand]
        preact = jnp.zeros((wide, LANES), f32)
        for k in range(taps):
            start = HALO - reach + k if forward else HALO - k
            preact += terms[start : start + wide, k * LANES : (k + 1) * LANES]
        result, slope = gelu_and_slope(preact)
        bent[...] = result
        gelu_ref[strand] = bent[half : half + span, :].astype(bf16)
        slopes[...] = halves[HALO - half : HALO - half + wide, :] * slope
        for k in range(taps):
            start = reach - k if forward else k
            shifted_ref[strand, :, k * part : (k + 1) * part] = slopes[start : start + span, :part].astype(bf16)
    plain, other = [
        dot(
            shifted_ref[n * dp_ranks : (n + 1) * dp_ranks].reshape(dp_ranks * span, taps * part),
            normed_ref[n * dp_ranks : (n + 1) * dp_ranks].reshape(dp_ranks * span, channels),
            ((0,), (0,)),
        )
        for n in range(2)
    ]
    total[...] = plain + dot(other.astype(bf16), swap, ((1,), (0,)))
    gain = jnp.sum(total[...] * kernel.astype(f32), 0, keepdims=True) / gain_ref[...]
    gain_high = gain.astype(bf16).astype(f32)
    row = lax.broadcasted_iota(jnp.int32, (HALO, channels), 0)
    extra = jnp.where(row == 0, gain_high, jnp.where(row == 1, gain - gain_high, 0.0)).T
    own_gain = channels // owners
    for owner in range(owners):
        for tap, channel, count, offset in runs(owner):
            leaving[owner, :, offset : offset + count] = total[
                tap * part : (tap + 1) * part, channel : channel + count
            ].astype(bf16)
        leaving[owner, :, rows:] = jnp.zeros((part, EXTRA), bf16)
        leaving[owner, :own_gain, rows:] = extra[
            owner * own_gain : (owner + 1) * own_gain, :EXTRA
        ].astype(bf16)
    moves.start(leaving, leaving_out)
    for b in range(dp_ranks):
        scaled[b] = (
            dot(shifted_ref[b], kernels[0], ((1,), (0,))) * gains[0]
            + dot(shifted_ref[dp_ranks + b], kernels[1], ((1,), (0,))) * gains[1]
        ).astype(bf16)
    order = [*range(1, chips), 0]
    for out, target_out, flip in ((cross, cross_out, core), (own, own_out, 0)):
        for m, mask in [(m, masks[m]) for m in order]:
            target = lax.bitwise_xor(rank_ref[0], mask | flip)
            b = lax.rem(target, dp_ranks)
            start = pl.multiple_of(lax.div(target, dp_ranks) * positions, positions)
            out[m, :, :channels] = scaled[b, pl.ds(start, positions), :]
            for n in range(2):
                lane = channels + n * LANES
                out[m, :, lane : lane + LANES] = gelu_ref[n * dp_ranks + b, pl.ds(start, positions), :]
            moves.start(out.at[m], target_out.at[m])
    for copy in moves.copies[arrivals:]:
        copy.wait()


def chip_sum(part, own_ref, crossed_ref, *outs):
    channels = own_ref.shape[2] - 2 * LANES
    for m, out in enumerate(outs):
        out[:, :channels] = (
            own_ref[m, :, :channels].astype(f32) + crossed_ref[m, :, :channels].astype(f32)
        ).astype(bf16)
        for c, ref in enumerate((own_ref, crossed_ref)):
            for n in range(2):
                lane = channels + n * LANES
                start = channels + (2 * c + n) * part
                out[:, start : start + part] = ref[m, :, lane : lane + part]


def finish(part, core, rank_ref, values_ref, cot_ref, pairing_ref, *refs):
    arrived, (combined_ref, grad_ref, gelus) = refs[:-3], refs[-3:]
    channels = values_ref.shape[1]
    ranks = gelus.shape[1]
    scaled = jnp.zeros(values_ref.shape, f32)
    for mask, block in zip(chip_masks(ranks, core), arrived):
        scaled += block[:, :channels].astype(f32)
        for c in range(2):
            source = lax.bitwise_xor(rank_ref[0], mask | c * core)
            for n in range(2):
                start = channels + (2 * c + n) * part
                gelus[n, source] = block[:, start : start + part]
    plain, other = [jnp.concatenate([gelus[n, j] for j in range(ranks)], -1) for n in range(2)]
    plain = plain.astype(f32)
    other = dot(other, swap_map(pairing_ref[...].reshape(1, -1)), ((1,), (0,)))
    values = values_ref[...].astype(f32)
    rms = lax.rsqrt(jnp.mean(values * values, -1, keepdims=True) + epsilon)
    reverse_out = (values + other).astype(bf16).astype(f32)
    combined_ref[...] = (0.5 * (values + plain + reverse_out)).astype(bf16)
    along = jnp.mean(scaled * values, -1, keepdims=True)
    grad_ref[...] = (cot_ref[...].astype(f32) + rms * scaled - values * (rms * rms * rms * along)).astype(bf16)


def collect(owner_of, terms_ref, kernel_ref, gain_ref, joined):
    part = terms_ref.shape[1]
    rows = kernel_ref.shape[0]
    own_gain = gain_ref.shape[1]
    joined[...] = jnp.zeros_like(joined)
    gain = jnp.zeros((own_gain, EXTRA), f32)
    for rank, owners in enumerate(owner_of):
        total = terms_ref[owners[0]].astype(f32)
        for owner in owners[1:]:
            total += terms_ref[owner].astype(f32)
        joined[rank * part : (rank + 1) * part, :rows] = total[:, :rows]
        gain += total[:own_gain, rows:]
    channels = kernel_ref.shape[1]
    joined[channels : channels + own_gain, :EXTRA] = gain
    turned = joined[...].T
    kernel_ref[...] = turned[:rows, :channels]
    gain_ref[...] = sum(turned[n : n + 1, channels : channels + own_gain] for n in range(EXTRA))


def flipped_pairs(count, mask):
    return [(i, i ^ mask) for i in range(count)]


def per_device(activations, cotangent, weights, norm_gain, pairing):
    seq_ranks = lax.axis_size("seq_rank")
    dp_ranks = lax.axis_size("dp_rank")
    seq_blocks = lax.axis_size("seq_block")
    dp_blocks = lax.axis_size("dp_block")
    ranks = seq_ranks * dp_ranks
    owners = ranks * seq_blocks * dp_blocks
    positions, channels = activations.shape[1:]
    rows = weights.shape[0]
    taps = rows * owners // channels
    part = channels // ranks
    span = positions * seq_ranks
    long = span + 2 * HALO
    reach = taps - taps % 2
    wide = -(-(span + reach) // 8) * 8
    strands = 2 * dp_ranks
    width = channels + 2 * LANES
    slim = channels + 2 * part
    rank = lax.axis_index(RANK).reshape(1)
    values, cot = activations[0], cotangent[0]
    along = ("seq_block", "seq_rank")
    ends = [(b * seq_ranks - 1, b * seq_ranks) for b in range(1, seq_blocks)]
    both = jnp.concatenate([values, cot], -1)
    edge = jnp.where(lax.axis_index("seq_rank") == 0, both[:EDGE], both[-EDGE:])
    edge = lax.ppermute(edge, along, ends + [(target, source) for source, target in ends])
    piece_of = [
        sr * dp_ranks + dr
        for _ in range(seq_blocks)
        for sr in range(seq_ranks)
        for _ in range(dp_blocks)
        for dr in range(dp_ranks)
    ]
    square = -(-rows // LANES) * LANES
    slices = called(
        lambda *refs: spread(piece_of, *refs),
        pltpu.HBM((owners, part, rows), bf16),
        (weights,),
        16,
        scratch=[
            pltpu.VMEM((square, channels), f32),
            pltpu.VMEM((owners, part, rows), bf16),
            pltpu.SemaphoreType.DMA((1,)),
        ],
        out_specs=HBM,
    )
    slices, packed = lax.optimization_barrier((slices, values))
    pieces = lax.all_to_all(slices, EVERY, 0, 0, tiled=True)
    gain = norm_gain.reshape(1, channels)
    core = dp_ranks
    masks = chip_masks(ranks, core)
    block = positions + EDGE
    home, cross, *leaving = called(
        lambda *refs: pack_messages(part, core, *refs),
        (pltpu.HBM((block, slim), bf16), shape_of((block, slim), bf16))
        + tuple(shape_of((block, slim + 2 * part), bf16) for _ in masks[1:]),
        (rank, packed, cot, edge, pairing),
        16,
        specs=[SMEM] + [VMEM] * 4,
    )
    arrived = [
        lax.ppermute(message, RANK, flipped_pairs(ranks, mask))
        for message, mask in zip(leaving, masks[1:])
    ]
    both_cores = []
    for group in ((cross, *arrived),):
        crossing = called(stack_crossing, shape_of((len(group), block, slim + 2 * part), bf16), group, 8)
        both_cores.append(lax.ppermute(crossing, RANK, flipped_pairs(ranks, core)))
    home = pltpu.with_memory_space_constraint(home, pltpu.HBM)
    held = (pieces, home, *arrived, *both_cores)
    halves = (len(masks), positions, width)
    shapes = ((owners, part, rows + EXTRA), halves, halves)
    groups = len(both_cores)
    outgoing, cross, own = called(
        lambda *refs: main_body(core, len(masks), groups, *refs),
        tuple(pltpu.HBM(shape, bf16) for shape in shapes),
        (rank, *held, gain, pairing),
        44,
        scratch=[
            pltpu.VMEM(pieces.shape, bf16),
            pltpu.VMEM(home.shape, bf16),
            pltpu.VMEM((len(masks), block, slim + 2 * part), bf16),
            pltpu.VMEM((len(arrived), *arrived[0].shape), bf16),
            pltpu.VMEM((strands, span, channels), bf16),
            pltpu.VMEM((strands, span, LANES), f32),
            pltpu.VMEM((3, strands, EDGE, channels), f32),
            pltpu.VMEM((3, strands, EDGE, LANES), f32),
            pltpu.VMEM((2, taps * LANES, channels), bf16),
            pltpu.VMEM((long, taps * LANES), f32),
            pltpu.VMEM((long, LANES), f32),
            pltpu.VMEM((wide, LANES), f32),
            pltpu.VMEM((wide, LANES), f32),
            pltpu.VMEM((taps * part, channels), f32),
            pltpu.VMEM((strands, span, taps * part), bf16),
            pltpu.VMEM((taps * part, channels), bf16),
            pltpu.VMEM((strands, span, LANES), bf16),
            pltpu.VMEM((dp_ranks, span, channels), bf16),
        ]
        + [pltpu.VMEM(shape, bf16) for shape in shapes]
        + [pltpu.SemaphoreType.DMA((2 * ranks + 4,))],
        specs=[SMEM, ANY, HBM] + [ANY] * (len(held) - 2) + [VMEM] * 2,
        out_specs=(HBM,) * 3,
    )
    terms = lax.all_to_all(outgoing, EVERY, 0, 0, tiled=True)
    crossed = lax.ppermute(cross, RANK, flipped_pairs(ranks, core))
    leaving = called(
        lambda *refs: chip_sum(part, *refs),
        tuple(shape_of((positions, channels + 4 * part), bf16) for _ in masks),
        (own, crossed),
        8,
    )
    arrived = leaving[:1] + tuple(
        lax.ppermute(message, RANK, flipped_pairs(ranks, mask))
        for message, mask in zip(leaving[1:], masks[1:])
    )
    order = [
        [
            ((sb * seq_ranks + sr) * dp_blocks + db) * dp_ranks + dr
            for sb in range(seq_blocks)
            for db in range(dp_blocks)
        ]
        for sr in range(seq_ranks)
        for dr in range(dp_ranks)
    ]
    grad_kernel, grad_gain = called(
        lambda *refs: collect(order, *refs),
        (shape_of((rows, channels), f32), shape_of((1, channels // owners), f32)),
        (terms,),
        16,
        scratch=[pltpu.VMEM((channels + LANES, -(-rows // LANES) * LANES), f32)],
    )
    grad_kernel, home, *arrived = lax.optimization_barrier((grad_kernel, *arrived))
    combined, grad_input = called(
        lambda *refs: finish(part, core, *refs),
        (shape_of((positions, channels), bf16), shape_of((positions, channels), bf16)),
        (rank, values, cot, pairing, home, *arrived),
        16,
        scratch=[pltpu.VMEM((2, ranks, positions, part), bf16)],
        specs=[SMEM] + [VMEM] * (4 + len(arrived)),
    )
    return combined[None], grad_input[None], grad_kernel, grad_gain[0]


def solution(mesh):
    seq, dp = mesh.shape["seq"], mesh.shape["dp"]
    seq_ranks, dp_ranks = 4, 2
    grouped = Mesh(mesh.devices.reshape(seq // seq_ranks, seq_ranks, dp // dp_ranks, dp_ranks), EVERY)
    along = P(("dp_block", "dp_rank"), ("seq_block", "seq_rank"), None)
    return jax.shard_map(
        per_device,
        mesh=grouped,
        in_specs=(along, along, P(EVERY, None), P(), P()),
        out_specs=(along, along, P(EVERY, None), P(EVERY)),
        check_vma=False,
    )
```

```python
import jax
import jax.numpy as jnp
from jax import lax
from jax.experimental import pallas as pl
from jax.experimental.pallas import tpu as pltpu
from jax.sharding import Mesh, PartitionSpec as P

epsilon = 1e-06
RANK = ("seq_rank", "dp_rank")
EVERY = ("seq_block", "seq_rank", "dp_block", "dp_rank")
LANES = 128
HALO = 16
EXTRA = 2
VMEM = pl.BlockSpec(memory_space=pltpu.VMEM)
SMEM = pl.BlockSpec(memory_space=pltpu.SMEM)
HBM = pl.BlockSpec(memory_space=pltpu.HBM)
ANY = pl.BlockSpec(memory_space=pl.ANY)
bf16 = jnp.bfloat16
f32 = jnp.float32


def called(body, outs, args, vmem, scratch=(), specs=None, out_specs=None):
    return pl.pallas_call(
        body,
        out_shape=outs,
        in_specs=specs or [VMEM] * len(args),
        out_specs=out_specs or jax.tree.map(lambda _: VMEM, outs),
        scratch_shapes=list(scratch),
        compiler_params=pltpu.CompilerParams(vmem_limit_bytes=vmem * 2**20),
        cost_estimate=pl.CostEstimate(flops=0, bytes_accessed=0, transcendentals=0),
    )(*args)


def shape_of(shape, dtype):
    return jax.ShapeDtypeStruct(shape, dtype)


def dot(a, b, contract):
    return lax.dot_general(a, b, (contract, ((), ())), preferred_element_type=f32)


def gelu_and_slope(x):
    inner = 0.7978845608028654 * (x + 0.044715 * (x * x * x))
    bend = jnp.tanh(inner)
    half_sum = 0.5 * (1.0 + bend)
    slope = half_sum + (0.5 * x) * (1.0 - bend * bend) * (
        0.7978845608028654 * (1.0 + 0.134145 * (x * x))
    )
    return x * half_sum, slope


def swap_map(pairing):
    channels = pairing.shape[1]
    row = lax.broadcasted_iota(jnp.int32, (channels, channels), 0)
    return jnp.where(row == pairing, 1.0, 0.0).astype(bf16)


def chip_masks(ranks, core):
    masks = [mask for mask in range(ranks) if not mask & core]
    return masks[:1] + sorted(masks[1:], key=lambda mask: -mask.bit_count())


class Moves:
    def __init__(self, sems):
        self.sems, self.copies = sems, []

    def start(self, source, target):
        copy = pltpu.make_async_copy(source, target, self.sems.at[len(self.copies)])
        copy.start()
        self.copies.append(copy)
        return copy

    def wait(self):
        for copy in self.copies:
            copy.wait()


def spread(piece_of, weights_ref, out_ref, square, sent, sems):
    rows, channels = weights_ref.shape
    part = out_ref.shape[1]
    square[...] = jnp.zeros_like(square)
    square[:rows] = weights_ref[...].astype(f32)
    turned = square[...].T.astype(bf16)
    for owner, piece in enumerate(piece_of):
        sent[owner] = turned[piece * part : (piece + 1) * part, :rows]
    moves = Moves(sems)
    moves.start(sent, out_ref)
    moves.wait()


def pack_messages(part, core, rank_ref, values_ref, cot_ref, edge_ref, pairing_ref, *outs):
    positions, channels = values_ref.shape
    home_ref, cross_ref, leaving = outs[0], outs[1], outs[2:]
    masks = chip_masks(2 * (len(leaving) + 1), core)
    flips = [mask | c for mask in masks[1:] for c in (core, 0)] + [0, core]
    shape = (part, channels)
    row = lax.broadcasted_iota(jnp.int32, shape, 0)
    column = lax.broadcasted_iota(jnp.int32, shape, 1)
    offsets = [column - row, pairing_ref[...].reshape(1, -1) - row]
    maps = [
        jnp.where(offset == lax.bitwise_xor(rank_ref[0], flip) * part, 1.0, 0.0).astype(bf16)
        for flip in flips
        for offset in offsets
    ]
    maps = jnp.concatenate(maps, 0)
    cot = jnp.concatenate([cot_ref[...], edge_ref[:, channels:]], 0)
    slices = dot(cot, maps, ((1,), (1,))).astype(bf16)
    lane = 0
    for out in (*leaving, home_ref, cross_ref):
        count = out.shape[1] - channels
        out[:positions, :channels] = values_ref[...]
        out[positions:, :channels] = edge_ref[:, :channels]
        out[:, channels:] = slices[:, lane : lane + count]
        lane += count


def stack_crossing(*refs):
    out_ref = refs[-1]
    width = out_ref.shape[2]
    for m, ref in enumerate(refs[:-1]):
        out_ref[m] = ref[:, :width]


def normalize(x, gains):
    x = x.astype(f32)
    x = x * lax.rsqrt(jnp.mean(x * x, -1, keepdims=True) + epsilon)
    return [(x * gain).astype(bf16) for gain in gains]


def swapped_row(row, swap):
    first = row.astype(bf16).astype(f32)
    second = (row - first).astype(bf16).astype(f32)
    third = row - first - second
    index = lax.broadcasted_iota(jnp.int32, (HALO, row.shape[1]), 0)
    parts = jnp.where(index == 0, first, jnp.where(index == 1, second, jnp.where(index == 2, third, 0.0)))
    result = dot(parts.astype(bf16), swap, ((1,), (0,)))
    return result[0:1] + result[1:2] + result[2:3]


def main_body(core, chips, groups, rank_ref, pieces_in, home_in, *refs):
    arrived_in, refs = refs[: chips - 1], refs[chips - 1 :]
    crossed_in, refs = refs[:groups], refs[groups:]
    gain_ref, pairing_ref, leaving_out, cross_out, own_out = refs[:5]
    pieces, home, crossed, arrived, normed_ref, grads_ref, edge_normed_ref, edge_grads_ref = refs[5:13]
    padded, terms, halves, bent, slopes, total, shifted_ref, kernel_ref, gelu_ref = refs[13:22]
    scaled, leaving, cross, own, sems = refs[22:]
    owners, part, rows = pieces.shape
    strands = normed_ref.shape[0]
    dp_ranks = strands // 2
    moves = Moves(sems)
    got_blocks = [moves.start(home_in, home)]
    got_blocks += [moves.start(block, arrived.at[m]) for m, block in enumerate(arrived_in)]
    per = chips // groups
    got_blocks += [moves.start(crossed_in[m // per].at[m % per], crossed.at[m]) for m in range(chips)]
    got_pieces = None
    masks = chip_masks(2 * chips, core)
    seq_ranks = 2 * chips // dp_ranks
    positions = home.shape[0] - HALO
    channels, width = gain_ref.shape[1], home.shape[1]
    swap = swap_map(pairing_ref[...].reshape(1, -1))
    gains = [gain_ref[...], swapped_row(gain_ref[...], swap)]
    blocks = [(0, home, channels)]
    blocks += [(mask, arrived.at[m], width) for m, mask in enumerate(masks[1:])]
    blocks += [(mask | core, crossed.at[m], channels) for m, mask in enumerate(masks)]
    for got, (flip, ref, lane) in zip(got_blocks, blocks):
        got.wait()
        if got is got_blocks[1]:
            got_pieces = moves.start(pieces_in, pieces)
        source = lax.bitwise_xor(rank_ref[0], flip)
        b, i = lax.rem(source, dp_ranks), lax.div(source, dp_ranks)
        start = pl.multiple_of(i * positions, positions)
        side = jnp.where(i == 0, 0, jnp.where(i == seq_ranks - 1, 1, 2))
        both = normalize(ref[:, :channels], gains)
        for n, normed in enumerate(both):
            first = lane + n * part
            grads = 0.5 * ref[:, first : first + part].astype(f32)
            index = n * dp_ranks + b
            normed_ref[index, pl.ds(start, positions), :] = normed[:positions]
            grads_ref[index, pl.ds(start, positions), :part] = grads[:positions]
            edge_normed_ref[side, index] = normed[positions:]
            edge_grads_ref[side, index, :, :part] = grads[positions:]
    span = normed_ref.shape[1]
    taps = kernel_ref.shape[0] // part
    half = taps // 2
    reach = 2 * half
    wide = bent.shape[0]

    def runs(owner):
        first, last = owner * rows, (owner + 1) * rows
        while first < last:
            tap, channel = divmod(first, channels)
            count = min(last - first, channels - channel)
            yield tap, channel, count, first - owner * rows
            first += count

    got_pieces.wait()
    arrivals = len(moves.copies)
    for owner in range(owners):
        for tap, channel, count, offset in runs(owner):
            kernel_ref[tap * part : (tap + 1) * part, channel : channel + count] = pieces[
                owner, :, offset : offset + count
            ]
    kernel = kernel_ref[...]
    kernels = [kernel, dot(kernel, swap, ((1,), (0,))).astype(bf16)]
    padded[...] = jnp.zeros_like(padded)
    for n in range(2):
        for k in range(taps):
            padded[n, k * LANES : k * LANES + part, :] = kernels[n][k * part : (k + 1) * part, :]
    edge_terms = []
    for n in range(2):
        edges = [
            edge_normed_ref[side, n * dp_ranks + b] for side in range(2) for b in range(dp_ranks)
        ]
        edge_terms.append(dot(jnp.concatenate(edges, 0), padded[n], ((1,), (1,))))
    for strand in range(strands):
        forward = strand < dp_ranks
        n, b = divmod(strand, dp_ranks)
        terms[HALO : HALO + span, :] = dot(normed_ref[strand], padded[n], ((1,), (1,)))
        halves[HALO : HALO + span, :] = grads_ref[strand]
        for side, start in enumerate((0, HALO + span)):
            first = (side * dp_ranks + b) * HALO
            terms[start : start + HALO, :] = edge_terms[n][first : first + HALO]
            halves[start : start + HALO, :] = edge_grads_ref[side, strand]
        preact = jnp.zeros((wide, LANES), f32)
        for k in range(taps):
            start = HALO - reach + k if forward else HALO - k
            preact += terms[start : start + wide, k * LANES : (k + 1) * LANES]
        result, slope = gelu_and_slope(preact)
        bent[...] = result
        gelu_ref[strand] = bent[half : half + span, :].astype(bf16)
        slopes[...] = halves[HALO - half : HALO - half + wide, :] * slope
        for k in range(taps):
            start = reach - k if forward else k
            shifted_ref[strand, :, k * part : (k + 1) * part] = slopes[start : start + span, :part].astype(bf16)
    plain, other = [
        dot(
            shifted_ref[n * dp_ranks : (n + 1) * dp_ranks].reshape(dp_ranks * span, taps * part),
            normed_ref[n * dp_ranks : (n + 1) * dp_ranks].reshape(dp_ranks * span, channels),
            ((0,), (0,)),
        )
        for n in range(2)
    ]
    total[...] = plain + dot(other.astype(bf16), swap, ((1,), (0,)))
    gain = jnp.sum(total[...] * kernel.astype(f32), 0, keepdims=True) / gain_ref[...]
    gain_high = gain.astype(bf16).astype(f32)
    row = lax.broadcasted_iota(jnp.int32, (HALO, channels), 0)
    extra = jnp.where(row == 0, gain_high, jnp.where(row == 1, gain - gain_high, 0.0)).T
    own_gain = channels // owners
    for owner in range(owners):
        for tap, channel, count, offset in runs(owner):
            leaving[owner, :, offset : offset + count] = total[
                tap * part : (tap + 1) * part, channel : channel + count
            ].astype(bf16)
        leaving[owner, :, rows:] = jnp.zeros((part, EXTRA), bf16)
        leaving[owner, :own_gain, rows:] = extra[
            owner * own_gain : (owner + 1) * own_gain, :EXTRA
        ].astype(bf16)
    moves.start(leaving, leaving_out)
    for b in range(dp_ranks):
        scaled[b] = (
            dot(shifted_ref[b], kernels[0], ((1,), (0,))) * gains[0]
            + dot(shifted_ref[dp_ranks + b], kernels[1], ((1,), (0,))) * gains[1]
        ).astype(bf16)
    order = [*range(1, chips), 0]
    for out, target_out, flip in ((cross, cross_out, core), (own, own_out, 0)):
        for m, mask in [(m, masks[m]) for m in order]:
            target = lax.bitwise_xor(rank_ref[0], mask | flip)
            b = lax.rem(target, dp_ranks)
            start = pl.multiple_of(lax.div(target, dp_ranks) * positions, positions)
            out[m, :, :channels] = scaled[b, pl.ds(start, positions), :]
            for n in range(2):
                lane = channels + n * LANES
                out[m, :, lane : lane + LANES] = gelu_ref[n * dp_ranks + b, pl.ds(start, positions), :]
            moves.start(out.at[m], target_out.at[m])
    for copy in moves.copies[arrivals:]:
        copy.wait()


def chip_sum(part, own_ref, crossed_ref, *outs):
    channels = own_ref.shape[2] - 2 * LANES
    for m, out in enumerate(outs):
        out[:, :channels] = (
            own_ref[m, :, :channels].astype(f32) + crossed_ref[m, :, :channels].astype(f32)
        ).astype(bf16)
        for c, ref in enumerate((own_ref, crossed_ref)):
            for n in range(2):
                lane = channels + n * LANES
                start = channels + (2 * c + n) * part
                out[:, start : start + part] = ref[m, :, lane : lane + part]


def finish(part, core, rank_ref, values_ref, cot_ref, pairing_ref, *refs):
    arrived, (combined_ref, grad_ref, gelus) = refs[:-3], refs[-3:]
    channels = values_ref.shape[1]
    ranks = gelus.shape[1]
    scaled = jnp.zeros(values_ref.shape, f32)
    for mask, block in zip(chip_masks(ranks, core), arrived):
        scaled += block[:, :channels].astype(f32)
        for c in range(2):
            source = lax.bitwise_xor(rank_ref[0], mask | c * core)
            for n in range(2):
                start = channels + (2 * c + n) * part
                gelus[n, source] = block[:, start : start + part]
    plain, other = [jnp.concatenate([gelus[n, j] for j in range(ranks)], -1) for n in range(2)]
    plain = plain.astype(f32)
    other = dot(other, swap_map(pairing_ref[...].reshape(1, -1)), ((1,), (0,)))
    values = values_ref[...].astype(f32)
    rms = lax.rsqrt(jnp.mean(values * values, -1, keepdims=True) + epsilon)
    reverse_out = (values + other).astype(bf16).astype(f32)
    combined_ref[...] = (0.5 * (values + plain + reverse_out)).astype(bf16)
    along = jnp.mean(scaled * values, -1, keepdims=True)
    grad_ref[...] = (cot_ref[...].astype(f32) + rms * scaled - values * (rms * rms * rms * along)).astype(bf16)


def collect(owner_of, terms_ref, kernel_ref, gain_ref, joined):
    part = terms_ref.shape[1]
    rows = kernel_ref.shape[0]
    own_gain = gain_ref.shape[1]
    joined[...] = jnp.zeros_like(joined)
    gain = jnp.zeros((own_gain, EXTRA), f32)
    for rank, owners in enumerate(owner_of):
        total = terms_ref[owners[0]].astype(f32)
        for owner in owners[1:]:
            total += terms_ref[owner].astype(f32)
        joined[rank * part : (rank + 1) * part, :rows] = total[:, :rows]
        gain += total[:own_gain, rows:]
    channels = kernel_ref.shape[1]
    joined[channels : channels + own_gain, :EXTRA] = gain
    turned = joined[...].T
    kernel_ref[...] = turned[:rows, :channels]
    gain_ref[...] = sum(turned[n : n + 1, channels : channels + own_gain] for n in range(EXTRA))


def flipped_pairs(count, mask):
    return [(i, i ^ mask) for i in range(count)]


def per_device(activations, cotangent, weights, norm_gain, pairing):
    seq_ranks = lax.axis_size("seq_rank")
    dp_ranks = lax.axis_size("dp_rank")
    seq_blocks = lax.axis_size("seq_block")
    dp_blocks = lax.axis_size("dp_block")
    ranks = seq_ranks * dp_ranks
    owners = ranks * seq_blocks * dp_blocks
    positions, channels = activations.shape[1:]
    rows = weights.shape[0]
    taps = rows * owners // channels
    part = channels // ranks
    span = positions * seq_ranks
    long = span + 2 * HALO
    reach = taps - taps % 2
    wide = -(-(span + reach) // 8) * 8
    strands = 2 * dp_ranks
    width = channels + 2 * LANES
    slim = channels + 2 * part
    rank = lax.axis_index(RANK).reshape(1)
    values, cot = activations[0], cotangent[0]
    along = ("seq_block", "seq_rank")
    ends = [(b * seq_ranks - 1, b * seq_ranks) for b in range(1, seq_blocks)]
    both = jnp.concatenate([values, cot], -1)
    edge = jnp.where(lax.axis_index("seq_rank") == 0, both[:HALO], both[-HALO:])
    edge = lax.ppermute(edge, along, ends + [(target, source) for source, target in ends])
    piece_of = [
        sr * dp_ranks + dr
        for _ in range(seq_blocks)
        for sr in range(seq_ranks)
        for _ in range(dp_blocks)
        for dr in range(dp_ranks)
    ]
    square = -(-rows // LANES) * LANES
    slices = called(
        lambda *refs: spread(piece_of, *refs),
        pltpu.HBM((owners, part, rows), bf16),
        (weights,),
        16,
        scratch=[
            pltpu.VMEM((square, channels), f32),
            pltpu.VMEM((owners, part, rows), bf16),
            pltpu.SemaphoreType.DMA((1,)),
        ],
        out_specs=HBM,
    )
    slices, packed = lax.optimization_barrier((slices, values))
    pieces = lax.all_to_all(slices, EVERY, 0, 0, tiled=True)
    gain = norm_gain.reshape(1, channels)
    core = dp_ranks
    masks = chip_masks(ranks, core)
    block = positions + HALO
    home, cross, *leaving = called(
        lambda *refs: pack_messages(part, core, *refs),
        (pltpu.HBM((block, slim), bf16), shape_of((block, slim), bf16))
        + tuple(shape_of((block, slim + 2 * part), bf16) for _ in masks[1:]),
        (rank, packed, cot, edge, pairing),
        16,
        specs=[SMEM] + [VMEM] * 4,
    )
    arrived = [
        lax.ppermute(message, RANK, flipped_pairs(ranks, mask))
        for message, mask in zip(leaving, masks[1:])
    ]
    both_cores = []
    for group in ((cross, *arrived),):
        crossing = called(stack_crossing, shape_of((len(group), block, slim), bf16), group, 8)
        both_cores.append(lax.ppermute(crossing, RANK, flipped_pairs(ranks, core)))
    home = pltpu.with_memory_space_constraint(home, pltpu.HBM)
    held = (pieces, home, *arrived, *both_cores)
    halves = (len(masks), positions, width)
    shapes = ((owners, part, rows + EXTRA), halves, halves)
    groups = len(both_cores)
    outgoing, cross, own = called(
        lambda *refs: main_body(core, len(masks), groups, *refs),
        tuple(pltpu.HBM(shape, bf16) for shape in shapes),
        (rank, *held, gain, pairing),
        44,
        scratch=[
            pltpu.VMEM(pieces.shape, bf16),
            pltpu.VMEM(home.shape, bf16),
            pltpu.VMEM((len(masks), block, slim), bf16),
            pltpu.VMEM((len(arrived), *arrived[0].shape), bf16),
            pltpu.VMEM((strands, span, channels), bf16),
            pltpu.VMEM((strands, span, LANES), f32),
            pltpu.VMEM((3, strands, HALO, channels), bf16),
            pltpu.VMEM((3, strands, HALO, LANES), f32),
            pltpu.VMEM((2, taps * LANES, channels), bf16),
            pltpu.VMEM((long, taps * LANES), f32),
            pltpu.VMEM((long, LANES), f32),
            pltpu.VMEM((wide, LANES), f32),
            pltpu.VMEM((wide, LANES), f32),
            pltpu.VMEM((taps * part, channels), f32),
            pltpu.VMEM((strands, span, taps * part), bf16),
            pltpu.VMEM((taps * part, channels), bf16),
            pltpu.VMEM((strands, span, LANES), bf16),
            pltpu.VMEM((dp_ranks, span, channels), bf16),
        ]
        + [pltpu.VMEM(shape, bf16) for shape in shapes]
        + [pltpu.SemaphoreType.DMA((2 * ranks + 4,))],
        specs=[SMEM, ANY, HBM] + [ANY] * (len(held) - 2) + [VMEM] * 2,
        out_specs=(HBM,) * 3,
    )
    terms = lax.all_to_all(outgoing, EVERY, 0, 0, tiled=True)
    crossed = lax.ppermute(cross, RANK, flipped_pairs(ranks, core))
    leaving = called(
        lambda *refs: chip_sum(part, *refs),
        tuple(shape_of((positions, channels + 4 * part), bf16) for _ in masks),
        (own, crossed),
        8,
    )
    arrived = leaving[:1] + tuple(
        lax.ppermute(message, RANK, flipped_pairs(ranks, mask))
        for message, mask in zip(leaving[1:], masks[1:])
    )
    order = [
        [
            ((sb * seq_ranks + sr) * dp_blocks + db) * dp_ranks + dr
            for sb in range(seq_blocks)
            for db in range(dp_blocks)
        ]
        for sr in range(seq_ranks)
        for dr in range(dp_ranks)
    ]
    grad_kernel, grad_gain = called(
        lambda *refs: collect(order, *refs),
        (shape_of((rows, channels), f32), shape_of((1, channels // owners), f32)),
        (terms,),
        16,
        scratch=[pltpu.VMEM((channels + LANES, -(-rows // LANES) * LANES), f32)],
    )
    grad_kernel, home, *arrived = lax.optimization_barrier((grad_kernel, *arrived))
    combined, grad_input = called(
        lambda *refs: finish(part, core, *refs),
        (shape_of((positions, channels), bf16), shape_of((positions, channels), bf16)),
        (rank, values, cot, pairing, home, *arrived),
        16,
        scratch=[pltpu.VMEM((2, ranks, positions, part), bf16)],
        specs=[SMEM] + [VMEM] * (4 + len(arrived)),
    )
    return combined[None], grad_input[None], grad_kernel, grad_gain[0]


def solution(mesh):
    seq, dp = mesh.shape["seq"], mesh.shape["dp"]
    seq_ranks, dp_ranks = 4, 2
    grouped = Mesh(mesh.devices.reshape(seq // seq_ranks, seq_ranks, dp // dp_ranks, dp_ranks), EVERY)
    along = P(("dp_block", "dp_rank"), ("seq_block", "seq_rank"), None)
    return jax.shard_map(
        per_device,
        mesh=grouped,
        in_specs=(along, along, P(EVERY, None), P(), P()),
        out_specs=(along, along, P(EVERY, None), P(EVERY)),
        check_vma=False,
    )
```
